32 devices in a mesh: grp: 4 (over y, core), box: 8 (over z, x).
Axes of the slice: x: 2, y: 2, z: 4, core: 2. Of those that a mesh axis runs over, the one named last changes fastest.
Arguments:
- load: float32 [64, 4, 8, 512], P(None, 'grp', 'box'), may hold values from -6 to 6
- leaf_load_map: float32 [4, 8, 128, 512], P('grp', 'box'), may hold values from -0.25 to 0.25
- leaf_out_map: float32 [4, 8, 128, 128], P('grp', 'box'), may hold values from -0.5 to 0.5
- leaf_field_map: float32 [4, 8, 512, 640], P('grp', 'box'), may hold values from -0.25 to 0.25
- x_solve: float32 [3, 4, 8, 64, 64], P(None, 'grp', 'box'), as said below
- x_out: float32 [3, 4, 8, 128, 64], P(None, 'grp', 'box'), may hold values from -0.375 to 0.375
- x_in: float32 [3, 4, 8, 64, 128], P(None, 'grp', 'box'), may hold values from -0.25 to 0.25
- y_solve: float32 [2, 4, 8, 64, 512], P(None, 'grp', 'box'), as said below
- y_out: float32 [2, 4, 8, 128, 512], P(None, 'grp', 'box'), may hold values from -0.125 to 0.125
- y_in: float32 [2, 4, 8, 512, 128], P(None, 'grp', 'box'), may hold values from -0.21875 to 0.21875
- reflect: float32 [4, 8, 128], P('grp', 'box'), may hold values from -0.9 to 0.9
Outputs:
- field_vals: float32 [64, 4, 8, 512], P(None, 'grp', 'box')
- edge_trace: float32 [64, 4, 8, 128], P(None, 'grp', 'box')
The draws below stay inside these ranges and needn't reach their ends.
Inputs may be any that keep to these rules, and one draw needn't show every extreme that they name: x_solve[j, r, c] is the same matrix for all c with the same c // 2^(j+1). y_solve[j, r, c] is the same matrix for all r with the same r // 2^(j+1).
All inputs are finite; a program needn't handle non-finite values.
Results may differ from the reference program's by a relative error of at most 0.00011.
Values sent between devices are 32-bit elements; how exact they have to be, the bound alone decides.
No kernel may reach another device: no remote copies, remote signals or barrier semaphores. Data moves between devices by JAX's collectives and lax.ppermute only.
A program may use at most 64 MiB of HBM per device.

```python
import math
import jax
import jax.numpy as jnp
from jax import lax

WAVES = 64
EDGE = 32
LB = 128
INNER = 512
NX = 8
NY = 4
IFACE = 512
XB = 3
YB = 2


def draw_x_solve(key, part):
    double_edge = 2 * EDGE
    base_draw = jax.random.normal(key, (XB, NY, NX, double_edge, double_edge), jnp.float32) * (0.7 / math.sqrt(double_edge))
    base_draw = base_draw + 0.5 * jnp.eye(double_edge, dtype=jnp.float32)
    col_ids = jnp.arange(NX)
    copies = []
    for merge_level in range(XB):
        group_span = 2 ** (merge_level + 1)
        first_col = col_ids // group_span * group_span
        copies.append(jnp.take(base_draw[merge_level], first_col, axis=1))
    return jnp.stack(copies, axis=0)


def draw_y_solve(key, part):
    double_edge = 2 * EDGE
    base_draw = jax.random.normal(key, (YB, NY, NX, double_edge, IFACE), jnp.float32) * (0.7 / math.sqrt(IFACE))
    diag_hit = jnp.arange(NX)[:, None, None] * double_edge + jnp.arange(double_edge)[None, :, None] == jnp.arange(IFACE)[None, None, :]
    base_draw = base_draw + 0.5 * diag_hit.astype(jnp.float32)
    row_ids = jnp.arange(NY)
    copies = []
    for merge_level in range(YB):
        group_span = 2 ** (merge_level + 1)
        first_row = row_ids // group_span * group_span
        copies.append(jnp.take(base_draw[merge_level], first_row, axis=0))
    return jnp.stack(copies, axis=0)


def level_of(own_key, shape, pieces, smallest, largest):
    gain, own = 1.0, jax.random.fold_in(own_key, 6)
    for position, parts in pieces:
        draws = jnp.exp(jax.random.uniform(jax.random.fold_in(own, position), (parts,), jnp.float32, smallest / len(pieces), largest / len(pieces)))
        gain = gain * jnp.repeat(draws, shape[position] // parts).reshape([-1 if axis == position else 1 for axis in range(len(shape))])
    return gain


def centred(own_key, shape, spread, most, split=(), kind=jnp.bfloat16):
    result = jax.random.normal(own_key, shape, jnp.float32) * spread
    if len(split) > 0:
        result = level_of(own_key, shape, split, -0.22, 0.18) * result
    return jnp.clip(result, min=-most, max=most).astype(kind)


def setup_inputs(seed: int = 0) -> dict:
    splits = jax.random.split(jax.random.key(seed), 12)
    load = centred(splits[0], (WAVES, NY, NX, INNER), 1.0, 6.0, ((1, 4), (2, 8)), jnp.float32)
    leaf_load_map = centred(splits[1], (NY, NX, LB, INNER), INNER ** -0.5, 0.25, ((0, 4), (1, 8)), jnp.float32)
    leaf_out_map = centred(splits[2], (NY, NX, LB, LB), LB ** -0.5, 0.5, ((0, 4), (1, 8)), jnp.float32)
    leaf_field_map = centred(splits[3], (NY, NX, INNER, LB + INNER), (LB + INNER) ** -0.5, 0.25, ((0, 4), (1, 8)), jnp.float32)
    x_solve = draw_x_solve(jax.random.fold_in(splits[11], 71), 0)
    x_out = centred(splits[5], (XB, NY, NX, LB, 2 * EDGE), (8 * EDGE) ** -0.5, 0.375, ((1, 4), (2, 8)), jnp.float32)
    x_in = centred(splits[6], (XB, NY, NX, 2 * EDGE, LB), (2 * (NX + 1) * EDGE) ** -0.5, 0.25, ((1, 4), (2, 8)), jnp.float32)
    y_solve = draw_y_solve(jax.random.fold_in(splits[11], 71), 0)
    y_out = centred(splits[8], (YB, NY, NX, LB, IFACE), (4 * IFACE) ** -0.5, 0.125, ((1, 4), (2, 8)), jnp.float32)
    y_in = centred(splits[9], (YB, NY, NX, IFACE, LB), (2 * (NX + NY) * EDGE) ** -0.5, 0.21875, ((1, 4), (2, 8)), jnp.float32)
    reflect = jnp.clip(jax.random.uniform(splits[10], (NY, NX, LB), jnp.float32, -0.9, 0.9) * level_of(splits[10], (NY, NX, LB), ((0, 4), (1, 8)), -0.4, 0.0), -0.9, 0.9)
    return dict(load=load, leaf_load_map=leaf_load_map, leaf_out_map=leaf_out_map, leaf_field_map=leaf_field_map, x_solve=x_solve, x_out=x_out, x_in=x_in, y_solve=y_solve, y_out=y_out, y_in=y_in, reflect=reflect)


precise = lax.Precision.HIGHEST


def pick_edge(source, edge_no, edge_len):
    return source[..., edge_no * edge_len:(edge_no + 1) * edge_len]


def with_edge(source, edge_no, edge_len, values):
    return jnp.concatenate([source[..., :edge_no * edge_len], values, source[..., (edge_no + 1) * edge_len:]], axis=-1)


def reference(load, leaf_load_map, leaf_out_map, leaf_field_map, x_solve, x_out, x_in, y_solve, y_out, y_in, reflect):
    edge_len = leaf_out_map.shape[-1] // 4
    wave_count = load.shape[0]
    row_count = load.shape[1]
    col_count = load.shape[2]
    start_out = jnp.einsum('wrck,rcek->wrce', load, leaf_load_map, precision=precise)
    outgoing_now = start_out
    columns = jnp.arange(col_count)
    row_ids = jnp.arange(row_count)
    x_keep = []
    for merge_level in range(XB):
        group_span = 2 ** (merge_level + 1)
        left_cut = columns // group_span * group_span + group_span // 2 - 1
        cut_data = jnp.concatenate([pick_edge(outgoing_now, 1, edge_len)[:, :, left_cut], pick_edge(outgoing_now, 3, edge_len)[:, :, left_cut + 1]], axis=-1)
        solved = jnp.einsum('wrck,rcjk->wrcj', cut_data, x_solve[merge_level], precision=precise)
        x_keep.append(solved)
        outgoing_now = outgoing_now + jnp.einsum('wrcj,rcej->wrce', solved, x_out[merge_level], precision=precise)
    y_keep = []
    for merge_level in range(YB):
        group_span = 2 ** (merge_level + 1)
        low_cut = row_ids // group_span * group_span + group_span // 2 - 1
        cut_data = jnp.concatenate([pick_edge(outgoing_now, 2, edge_len)[:, low_cut], pick_edge(outgoing_now, 0, edge_len)[:, low_cut + 1]], axis=-1)
        flat_data = cut_data.reshape(wave_count, row_count, -1)
        solved = jnp.einsum('wrk,rcjk->wrcj', flat_data, y_solve[merge_level], precision=precise)
        y_keep.append(solved)
        flat_solved = solved.reshape(wave_count, row_count, -1)
        outgoing_now = outgoing_now + jnp.einsum('wrk,rcek->wrce', flat_solved, y_out[merge_level], precision=precise)
    edge_ids = jnp.arange(4 * edge_len) // edge_len
    on_boundary = ((edge_ids[None, None, :] == 0) & (row_ids[:, None, None] == 0)) | ((edge_ids[None, None, :] == 1) & (columns[None, :, None] == col_count - 1)) | ((edge_ids[None, None, :] == 2) & (row_ids[:, None, None] == row_count - 1)) | ((edge_ids[None, None, :] == 3) & (columns[None, :, None] == 0))
    incoming = jnp.where(on_boundary[None], outgoing_now * reflect[None], jnp.zeros_like(outgoing_now))
    for merge_level in reversed(range(YB)):
        group_span = 2 ** (merge_level + 1)
        low_cut = row_ids // group_span * group_span + group_span // 2 - 1
        cut_terms = jnp.einsum('wrce,rcke->wrk', incoming, y_in[merge_level], precision=precise)
        grouped = cut_terms.reshape(wave_count, row_count // group_span, group_span, -1).sum(axis=2)
        summed_in = jnp.repeat(grouped, group_span, axis=1).reshape(wave_count, row_count, col_count, 2 * edge_len)
        cut_in = y_keep[merge_level] + summed_in
        is_low = (row_ids == low_cut)[None, :, None, None]
        is_high = (row_ids == low_cut + 1)[None, :, None, None]
        incoming = with_edge(incoming, 2, edge_len, jnp.where(is_low, cut_in[..., :edge_len], pick_edge(incoming, 2, edge_len)))
        incoming = with_edge(incoming, 0, edge_len, jnp.where(is_high, cut_in[..., edge_len:], pick_edge(incoming, 0, edge_len)))
    for merge_level in reversed(range(XB)):
        group_span = 2 ** (merge_level + 1)
        left_cut = columns // group_span * group_span + group_span // 2 - 1
        cut_terms = jnp.einsum('wrce,rcke->wrck', incoming, x_in[merge_level], precision=precise)
        grouped = cut_terms.reshape(wave_count, row_count, col_count // group_span, group_span, -1).sum(axis=3)
        summed_in = jnp.repeat(grouped, group_span, axis=2)
        cut_in = x_keep[merge_level] + summed_in
        is_left = (columns == left_cut)[None, None, :, None]
        is_right = (columns == left_cut + 1)[None, None, :, None]
        incoming = with_edge(incoming, 1, edge_len, jnp.where(is_left, cut_in[..., :edge_len], pick_edge(incoming, 1, edge_len)))
        incoming = with_edge(incoming, 3, edge_len, jnp.where(is_right, cut_in[..., edge_len:], pick_edge(incoming, 3, edge_len)))
    field_vals = jnp.einsum('wrck,rcik->wrci', jnp.concatenate([incoming, load], axis=-1), leaf_field_map, precision=precise)
    outgoing_end = jnp.einsum('wrck,rcek->wrce', incoming, leaf_out_map, precision=precise) + start_out
    trace_raw = incoming - outgoing_end
    bottom_edge = pick_edge(trace_raw, 0, edge_len)
    right_edge = pick_edge(trace_raw, 1, edge_len)
    top_edge = pick_edge(trace_raw, 2, edge_len)
    left_edge = pick_edge(trace_raw, 3, edge_len)
    east_nb = jnp.concatenate([left_edge[:, :, 1:], jnp.zeros_like(left_edge[:, :, :1])], axis=2)
    west_nb = jnp.concatenate([jnp.zeros_like(right_edge[:, :, :1]), right_edge[:, :, :-1]], axis=2)
    north_nb = jnp.concatenate([bottom_edge[:, 1:], jnp.zeros_like(bottom_edge[:, :1])], axis=1)
    south_nb = jnp.concatenate([jnp.zeros_like(top_edge[:, :1]), top_edge[:, :-1]], axis=1)
    has_east = (columns < col_count - 1)[None, None, :, None]
    has_west = (columns > 0)[None, None, :, None]
    has_north = (row_ids < row_count - 1)[None, :, None, None]
    has_south = (row_ids > 0)[None, :, None, None]
    new_bottom = jnp.where(has_south, 0.5 * (bottom_edge + south_nb), bottom_edge)
    new_right = jnp.where(has_east, 0.5 * (right_edge + east_nb), right_edge)
    new_top = jnp.where(has_north, 0.5 * (top_edge + north_nb), top_edge)
    new_left = jnp.where(has_west, 0.5 * (left_edge + west_nb), left_edge)
    edge_trace = jnp.concatenate([new_bottom, new_right, new_top, new_left], axis=-1)
    return field_vals, edge_trace
```

```python
import functools

import jax
import jax.numpy as jnp
from jax import lax
from jax.experimental import pallas as pl
from jax.experimental.pallas import tpu as pltpu
from jax.sharding import Mesh, PartitionSpec as P

f32 = jnp.float32
LANES = 128


def dot_t(a, b):
    dims = (((1,), (1,)), ((), ()))

    def parts(x):
        high = x.astype(jnp.bfloat16)
        return high, (x - high.astype(f32)).astype(jnp.bfloat16)

    def product(x, y):
        return lax.dot_general(x, y, dims, preferred_element_type=f32)

    a_high, a_low = parts(a)
    b_high, b_low = parts(b)
    return product(a_high, b_high) + (product(a_high, b_low) + product(a_low, b_high))


def fused(body, outs, *args, scratch=()):
    vmem = pl.BlockSpec(memory_space=pltpu.VMEM)
    return pl.pallas_call(
        body,
        out_shape=[jax.ShapeDtypeStruct(s, f32) for s in outs],
        in_specs=[vmem] * len(args),
        out_specs=[vmem] * len(outs),
        scratch_shapes=[pltpu.VMEM(s, f32) for s in scratch],
        compiler_params=pltpu.CompilerParams(vmem_limit_bytes=12 << 20),
    )(*args)


def packed(x, width):
    runs = LANES // width
    rows = x.shape[0] // runs
    return jnp.concatenate([x[i * rows : (i + 1) * rows] for i in range(runs)], axis=1)


def unpacked(x, width):
    return jnp.concatenate(
        [x[:, i * width : (i + 1) * width] for i in range(x.shape[1] // width)], axis=0
    )


def pad_lanes(x, lanes):
    if x.shape[1] == lanes:
        return x
    return jnp.concatenate([x, jnp.zeros((x.shape[0], lanes - x.shape[1]), f32)], axis=1)


def local(
    row_axes,
    load,
    leaf_load_map,
    leaf_out_map,
    leaf_field_map,
    x_solve,
    x_out,
    x_in,
    y_solve,
    y_out,
    y_in,
    reflect,
):
    edge = leaf_out_map.shape[-1] // 4
    cols = lax.axis_size("box")
    rows = 1
    for axis in row_axes:
        rows *= lax.axis_size(axis)
    x_levels = x_solve.shape[0]
    y_levels = y_solve.shape[0]
    waves = load.shape[0]
    leaf = 4 * edge
    pair = 2 * edge
    iface = cols * pair
    load_here = load[:, 0, 0, :]
    inner = load_here.shape[1]

    def my_column():
        return lax.axis_index("box")

    def my_row():
        return lax.axis_index(row_axes)

    def bit(value, level):
        return (value >> level) & 1

    def edge_of(x, number):
        return x[:, number * edge : (number + 1) * edge]

    def exchange_shape(level):
        kept = x_levels - 1 - level
        lanes = max(pair + kept * edge, kept * pair)
        lanes = -(-lanes // LANES) * LANES
        return (waves + (edge if kept else 0), lanes)

    def store_exchange(out, left, right, in_cols, out_rows):
        lanes = out.shape[1]
        out[:waves] = pad_lanes(jnp.concatenate([left, right] + in_cols, axis=1), lanes)
        if out_rows:
            out[waves:] = pad_lanes(jnp.concatenate(out_rows, axis=1), lanes)

    def start_body(load_ref, map_ref, xo_ref, xi_ref, h_ref, out_ref):
        h = dot_t(load_ref[...], map_ref[...])
        h_ref[...] = h
        is_right = bit(my_column(), 0) == 1
        in_cols, out_rows = [], []
        for k in range(x_levels - 1):
            xo, xi = xo_ref[k], xi_ref[k]
            in_cols.append(jnp.where(is_right, edge_of(xi, 1), edge_of(xi, 3)))
            out_rows.append(jnp.where(is_right, xo[edge : 2 * edge], xo[3 * edge :]))
        store_exchange(out_ref, edge_of(h, 3), edge_of(h, 1), in_cols, out_rows)

    h0, to_send = fused(
        start_body,
        [(waves, leaf), exchange_shape(0)],
        load_here,
        leaf_load_map[0, 0],
        x_out[:, 0, 0],
        x_in[:, 0, 0],
    )
    from_load = jnp.einsum(
        "wk,ik->wi", load_here, leaf_field_map[0, 0, :, leaf:], precision=lax.Precision.HIGH
    )

    def x_body(level, h_ref, own_ref, got_ref, solve_ref, xo_ref, h_out, w_out, *rest):
        kept = x_levels - 1 - level
        is_right = bit(my_column(), level) == 1
        own, got = own_ref[:waves], got_ref[:waves]
        left_child = jnp.where(is_right, got, own)
        right_child = jnp.where(is_right, own, got)
        v = jnp.concatenate([left_child[:, edge:pair], right_child[:, :edge]], axis=1)
        w = dot_t(v, solve_ref[...])
        w_out[...] = w
        if kept:
            next_ref, ends_ref = rest
            left_rows = jnp.where(is_right, got_ref[waves:], own_ref[waves:])
            right_rows = jnp.where(is_right, own_ref[waves:], got_ref[waves:])
            spread = dot_t(
                w, jnp.concatenate([xo_ref[...], left_rows[:, :pair], right_rows[:, :pair]], axis=0)
            )
            h_out[...] = h_ref[...] + spread[:, :leaf]
            left = left_child[:, :edge] + spread[:, leaf : leaf + edge]
            right = right_child[:, edge:pair] + spread[:, leaf + edge :]
            ends_ref[...] = jnp.concatenate(
                [left_child[:, pair : pair + edge], right_child[:, pair : pair + edge]], axis=1
            )
            next_right = bit(my_column(), level + 1) == 1
            in_all = jnp.where(next_right, right_child, left_child)
            out_all = jnp.where(next_right, right_rows, left_rows)
            store_exchange(
                next_ref,
                left,
                right,
                [in_all[:, pair + k * edge : pair + (k + 1) * edge] for k in range(1, kept)],
                [out_all[:, k * pair : (k + 1) * pair] for k in range(1, kept)],
            )
        else:
            h_out[...] = h_ref[...] + dot_t(w, xo_ref[...])

    h = h0
    x_keep, ends = [], []
    for level in range(x_levels):
        got = lax.ppermute(to_send, "box", [(i, i ^ (1 << level)) for i in range(cols)])
        outs = [(waves, leaf), (waves, pair)]
        if level < x_levels - 1:
            outs += [exchange_shape(level + 1), (pair, pair)]
        h, w, *rest = fused(
            functools.partial(x_body, level),
            outs,
            h,
            to_send,
            got,
            x_solve[level, 0, 0],
            x_out[level, 0, 0],
        )
        x_keep.append(w)
        if rest:
            to_send, end = rest
            ends.append(end)

    def group(level):
        return tuple(row_axes[y_levels - 1 - level :]) + ("box",)

    def span(level):
        return 2 << level

    def swap(x, level):
        return lax.all_to_all(x, group(level), 0, 0, tiled=True)

    def offer_shape(level):
        size = span(level)
        return (size * cols, waves // size * edge // LANES, LANES)

    def store_offer(level, h, out):
        size = span(level)
        share = waves // size
        facing = jnp.where(
            lax.rem(my_row(), size) == size // 2 - 1, edge_of(h, 2), edge_of(h, 0)
        )
        for target in range(size):
            piece = packed(facing[target * share : (target + 1) * share], edge)
            out[target * cols : (target + 1) * cols] = jnp.broadcast_to(piece, (cols,) + piece.shape)

    def offer_body(level, h_ref, out_ref):
        store_offer(level, h_ref[...], out_ref)

    def solve_body(level, got_ref, solve_ref, out_ref, v_ref):
        size = span(level)
        low = (size // 2 - 1) * cols
        run = got_ref.shape[1]
        for side in range(2):
            for c in range(cols):
                piece = got_ref[low + side * cols + c]
                for k in range(LANES // edge):
                    start = c * pair + side * edge
                    v_ref[k * run : (k + 1) * run, start : start + edge] = edge_of(piece, k)
        w = packed(dot_t(v_ref[...], solve_ref[...]), pair)
        out_ref[...] = jnp.broadcast_to(w, out_ref.shape)

    def own_columns(w_all):
        own = w_all[:, :pair]
        for c in range(1, cols):
            own = jnp.where(my_column() == c, w_all[:, c * pair : (c + 1) * pair], own)
        return own

    def gather_w(level, got_ref, w_ref):
        size = span(level)
        share = waves // size
        run = got_ref.shape[1]
        for target in range(size):
            for c in range(cols):
                piece = got_ref[target * cols + c]
                for k in range(LANES // pair):
                    start = target * share + k * run
                    w_ref[start : start + run, c * pair : (c + 1) * pair] = piece[
                        :, k * pair : (k + 1) * pair
                    ]
        return w_ref[...]

    def spread_body(level, h_ref, got_ref, yo_ref, h_out, w_out, next_ref, w_ref):
        w_all = gather_w(level, got_ref, w_ref)
        w_out[...] = own_columns(w_all)
        h = h_ref[...] + dot_t(w_all, yo_ref[...])
        h_out[...] = h
        store_offer(level + 1, h, next_ref)

    def halves(level):
        return span(level) // 2

    def terms_shape(level):
        return (span(level) * cols, waves // halves(level) * edge // LANES, LANES)

    def store_terms(level, g, yi_ref, out):
        terms = dot_t(g, yi_ref[...])
        half = halves(level)
        share = waves // half
        for side in range(2):
            for c in range(cols):
                start = c * pair + side * edge
                piece = terms[:, start : start + edge]
                for part in range(half):
                    out[(side * half + part) * cols + c] = packed(
                        piece[part * share : (part + 1) * share], edge
                    )

    def turn_body(level, h_ref, got_ref, yo_ref, yi_ref, reflect_ref, w_out, g_out, out_ref, w_ref):
        w_all = gather_w(level, got_ref, w_ref)
        w_out[...] = own_columns(w_all)
        h = h_ref[...] + dot_t(w_all, yo_ref[...])
        lane = lax.broadcasted_iota(jnp.int32, (1, leaf), 1)

        def side(number):
            return (lane >= number * edge) & (lane < (number + 1) * edge)

        outer = (
            side(0) & (my_row() == 0)
            | side(1) & (my_column() == cols - 1)
            | side(2) & (my_row() == rows - 1)
            | side(3) & (my_column() == 0)
        )
        g = jnp.where(outer, h * reflect_ref[...], 0.0)
        g_out[...] = g
        store_terms(level, g, yi_ref, out_ref)

    def sum_body(got_ref, out_ref):
        out_ref[...] = jnp.sum(got_ref[...], axis=0)

    def with_row_edge(level, g, w, q):
        size = span(level)
        place = lax.rem(my_row(), size)
        is_low = place == size // 2 - 1
        is_high = place == size // 2
        value = jnp.where(place < size // 2, w[:, :edge], w[:, edge:]) + q
        bottom = jnp.where(is_high, value, edge_of(g, 0))
        top = jnp.where(is_low, value, edge_of(g, 2))
        return jnp.concatenate([bottom, edge_of(g, 1), top, edge_of(g, 3)], axis=1)

    def row_down_body(level, g_ref, w_ref, sum_ref, yi_ref, g_out, out_ref):
        g = with_row_edge(level, g_ref[...], w_ref[...], unpacked_parts(level, sum_ref))
        g_out[...] = g
        store_terms(level - 1, g, yi_ref, out_ref)

    def unpacked_parts(level, sum_ref):
        run = waves // halves(level) * edge // LANES
        return jnp.concatenate(
            [unpacked(sum_ref[i * run : (i + 1) * run], edge) for i in range(halves(level))], axis=0
        )

    def collect(total, level):
        for axis_no in range(level):
            axis = row_axes[y_levels - 1 - axis_no]
            other = lax.ppermute(total, axis, [(0, 1), (1, 0)])
            first = lax.axis_index(axis) == 0
            total = jnp.concatenate(
                [jnp.where(first, total, other), jnp.where(first, other, total)], axis=0
            )
        return total

    x_lanes = -(-x_levels * edge // LANES) * LANES

    def x_terms_body(g_ref, w_ref, sum_ref, xi_ref, g_out, out_ref):
        g = with_row_edge(0, g_ref[...], w_ref[...], unpacked_parts(0, sum_ref))
        g_out[...] = g
        terms = [dot_t(g, xi_ref[k]) for k in range(x_levels)]
        for c in range(cols):
            picked = []
            for k in range(x_levels):
                start = bit(c, k) * edge
                same = my_column() >> (k + 1) == c >> (k + 1)
                picked.append(jnp.where(same, terms[k][:, start : start + edge], 0.0))
            out_ref[c] = pad_lanes(jnp.concatenate(picked, axis=1), x_lanes)

    def finish_body(g_ref, h0_ref, got_ref, keep_ref, ends_ref, lo_ref, g_out, t_out, *faces):
        g = g_ref[...]
        q = jnp.sum(got_ref[...], axis=0)
        gl = jnp.zeros((waves, edge), f32)
        gr = gl
        for level in reversed(range(x_levels)):
            is_right = bit(my_column(), level) == 1
            keep = keep_ref[level]
            value = edge_of(q, level) + jnp.where(is_right, keep[:, edge:], keep[:, :edge])
            if level < x_levels - 1:
                end = ends_ref[level]
                end = jnp.where(is_right, end[edge:], end[:edge])
                value = value + dot_t(jnp.concatenate([gl, gr], axis=1), end)
            gl = jnp.where(is_right, value, gl)
            gr = jnp.where(is_right, gr, value)
        g = jnp.concatenate(
            [edge_of(g, 0), edge_of(g, 1) + gr, edge_of(g, 2), edge_of(g, 3) + gl], axis=1
        )
        g_out[...] = g
        t = g - (dot_t(g, lo_ref[...]) + h0_ref[...])
        t_out[...] = t
        odd_col = bit(my_column(), 0) == 1
        odd_row = bit(my_row(), 0) == 1
        bottom, right, top, left = (packed(edge_of(t, i), edge) for i in range(4))
        faces[0][...] = jnp.where(odd_col, left, right)
        faces[1][...] = jnp.where(odd_col, right, left)
        faces[2][...] = jnp.where(odd_row, bottom, top)
        faces[3][...] = jnp.where(odd_row, top, bottom)

    def trace_body(t_ref, a_ref, b_ref, c_ref, d_ref, out_ref):
        t = t_ref[...]
        odd_col = bit(my_column(), 0) == 1
        odd_row = bit(my_row(), 0) == 1
        near_x, far_x, near_y, far_y = (
            unpacked(ref[...], edge) for ref in (a_ref, b_ref, c_ref, d_ref)
        )
        east = jnp.where(odd_col, far_x, near_x)
        west = jnp.where(odd_col, near_x, far_x)
        north = jnp.where(odd_row, far_y, near_y)
        south = jnp.where(odd_row, near_y, far_y)

        def mean(shared, own, other):
            return jnp.where(shared, 0.5 * (own + other), own)

        out_ref[...] = jnp.concatenate(
            [
                mean(my_row() > 0, edge_of(t, 0), south),
                mean(my_column() < cols - 1, edge_of(t, 1), east),
                mean(my_row() < rows - 1, edge_of(t, 2), north),
                mean(my_column() > 0, edge_of(t, 3), west),
            ],
            axis=1,
        )

    (offer,) = fused(functools.partial(offer_body, 0), [offer_shape(0)], h)
    y_keep = []
    for level in range(y_levels):
        share = waves // span(level)
        (w_offer,) = fused(
            functools.partial(solve_body, level),
            [(span(level) * cols, share * pair // LANES, LANES)],
            swap(offer, level),
            y_solve[level, 0, 0],
            scratch=[(share, iface)],
        )
        got = swap(w_offer, level)
        if level < y_levels - 1:
            h, w, offer = fused(
                functools.partial(spread_body, level),
                [(waves, leaf), (waves, pair), offer_shape(level + 1)],
                h,
                got,
                y_out[level, 0, 0],
                scratch=[(waves, iface)],
            )
        else:
            w, g, terms = fused(
                functools.partial(turn_body, level),
                [(waves, pair), (waves, leaf), terms_shape(level)],
                h,
                got,
                y_out[level, 0, 0],
                y_in[level, 0, 0],
                reflect[0],
                scratch=[(waves, iface)],
            )
        y_keep.append(w)
    for level in reversed(range(y_levels)):
        (total,) = fused(sum_body, [terms_shape(level)[1:]], swap(terms, level))
        total = collect(total, level)
        if level > 0:
            g, terms = fused(
                functools.partial(row_down_body, level),
                [(waves, leaf), terms_shape(level - 1)],
                g,
                y_keep[level],
                total,
                y_in[level - 1, 0, 0],
            )
    g, terms = fused(
        x_terms_body,
        [(waves, leaf), (cols, waves, x_lanes)],
        g,
        y_keep[0],
        total,
        x_in[:, 0, 0],
    )
    got = lax.all_to_all(terms, "box", 0, 0, tiled=True)
    face = (waves * edge // LANES, LANES)
    g, t, *faces = fused(
        finish_body,
        [(waves, leaf), (waves, leaf)] + [face] * 4,
        g,
        h0,
        got,
        jnp.stack(x_keep),
        jnp.stack(ends),
        leaf_out_map[0, 0],
    )

    def near(count):
        return [(i, i ^ 1) for i in range(count)]

    def far(count):
        one_way = [(i, i + 1) for i in range(1, count - 1, 2)]
        return one_way + [(j, i) for i, j in one_way]

    seen = [
        lax.ppermute(faces[0], "box", near(cols)),
        lax.ppermute(faces[1], "box", far(cols)),
        lax.ppermute(faces[2], row_axes, near(rows)),
        lax.ppermute(faces[3], row_axes, far(rows)),
    ]
    field_vals = from_load + jnp.einsum(
        "wk,ik->wi", g, leaf_field_map[0, 0, :, :leaf], precision=lax.Precision.HIGH
    )
    (edge_trace,) = fused(trace_body, [(waves, leaf)], t, *seen)
    return (field_vals[:, None, None, :], edge_trace[:, None, None, :])


def solution(mesh):
    rows, cols = mesh.devices.shape
    bits = rows.bit_length() - 1
    row_axes = tuple(f"row{i}" for i in reversed(range(bits)))
    split = Mesh(mesh.devices.reshape((2,) * bits + (cols,)), row_axes + ("box",))
    late = P(None, row_axes, "box")
    early = P(row_axes, "box")
    return jax.shard_map(
        functools.partial(local, row_axes),
        mesh=split,
        in_specs=(late, early, early, early) + (late,) * 6 + (early,),
        out_specs=(late, late),
        check_vma=False,
    )
```

```python
import functools
import math

import jax
import jax.numpy as jnp
from jax import lax
from jax.experimental import pallas as pl
from jax.experimental.pallas import tpu as pltpu
from jax.sharding import Mesh, PartitionSpec as P

f32 = jnp.float32
LANES = 128
START_ROOM = 60 << 20


def dot(a, b, over=0):
    dims = (((1,), (over,)), ((), ()))

    def parts(x):
        high = x.astype(jnp.bfloat16)
        return high, (x - high.astype(f32)).astype(jnp.bfloat16)

    def product(x, y):
        return lax.dot_general(x, y, dims, preferred_element_type=f32)

    a_high, a_low = parts(a)
    b_high, b_low = parts(b)
    return product(a_high, b_high) + (product(a_high, b_low) + product(a_low, b_high))


def dot_t(a, b):
    return dot(a, b, 1)


def fused(body, outs, *args, scratch=()):
    vmem = pl.BlockSpec(memory_space=pltpu.VMEM)
    return pl.pallas_call(
        body,
        out_shape=[pltpu.VMEM(s, f32) for s in outs],
        in_specs=[vmem] * len(args),
        out_specs=[vmem] * len(outs),
        scratch_shapes=[pltpu.VMEM(s, f32) for s in scratch],
        compiler_params=pltpu.CompilerParams(vmem_limit_bytes=12 << 20),
    )(*args)


def packed(x, width):
    runs = LANES // width
    rows = x.shape[0] // runs
    return jnp.concatenate([x[i * rows : (i + 1) * rows] for i in range(runs)], axis=1)


def unpacked(x, width):
    return jnp.concatenate(
        [x[:, i * width : (i + 1) * width] for i in range(x.shape[1] // width)], axis=0
    )


def pad_lanes(x, lanes):
    if x.shape[1] == lanes:
        return x
    return jnp.concatenate([x, jnp.zeros((x.shape[0], lanes - x.shape[1]), f32)], axis=1)


def local(
    row_axes,
    load,
    leaf_load_map,
    leaf_out_map,
    leaf_field_map,
    x_solve,
    x_out,
    x_in,
    y_solve,
    y_out,
    y_in,
    reflect,
):
    edge = leaf_out_map.shape[-1] // 4
    cols = lax.axis_size("box")
    rows = 1
    for axis in row_axes:
        rows *= lax.axis_size(axis)
    x_levels = x_solve.shape[0]
    y_levels = y_solve.shape[0]
    waves = load.shape[0]
    leaf = 4 * edge
    pair = 2 * edge
    iface = cols * pair
    load_here = load[:, 0, 0, :]
    inner = load_here.shape[1]

    def my_column():
        return lax.axis_index("box")

    def my_row():
        return lax.axis_index(row_axes)

    def bit(value, level):
        return (value >> level) & 1

    def edge_of(x, number):
        return x[:, number * edge : (number + 1) * edge]

    def exchange_shape(level):
        lanes = (2 + 2 * (x_levels - 1 - level)) * edge
        return (pair, -(-lanes // LANES) * LANES)

    def pieces_of(x, first, count):
        return [edge_of(x, first + i) for i in range(count)]

    kept_from_start = [x_solve, jnp.swapaxes(x_out, 3, 4), x_in, y_solve, y_out, y_in]
    kept_from_start = [x[:, 0, 0] for x in kept_from_start] + [leaf_out_map[0, 0]]

    def start_body(load_any, map_any, *refs):
        count = len(kept_from_start)
        sources, (h_ref, out_ref) = refs[:count], refs[count : count + 2]
        targets = refs[count + 2 : 2 * count + 2]
        load_v, map_v, sems = refs[2 * count + 2 :]
        pairs = [(load_any, load_v), (map_any, map_v)] + list(zip(sources, targets))
        order = [0, 1, 4, 3, 2, 5, 6, 7, 8]
        copies = [pltpu.make_async_copy(a, b, sems.at[i]) for i, (a, b) in enumerate(pairs)]
        for i in order:
            copies[i].start()
        copies[0].wait()
        copies[1].wait()
        h = dot_t(load_v[...].reshape(waves, inner), map_v[...])
        h_ref[...] = h
        copies[4].wait()
        copies[3].wait()
        xo, xi = targets[1], targets[2]
        is_right = bit(my_column(), 0) == 1
        travelling = [
            jnp.where(is_right, edge_of(x[k], 1), edge_of(x[k], 3))
            for x in (xi, xo)
            for k in range(x_levels - 1)
        ]
        out_ref[...] = pad_lanes(
            jnp.concatenate([edge_of(h, 3), edge_of(h, 1)] + travelling, axis=1), out_ref.shape[1]
        )
        for i in order[4:]:
            copies[i].wait()

    anywhere, vmem = (pl.BlockSpec(memory_space=m) for m in (pl.ANY, pltpu.VMEM))
    count = len(kept_from_start)
    outs = [(waves, leaf), exchange_shape(0)] + [x.shape for x in kept_from_start]
    h0, to_send, *placed = pl.pallas_call(
        start_body,
        out_shape=[pltpu.VMEM(s, f32) for s in outs],
        in_specs=[anywhere] * (count + 2),
        out_specs=[vmem] * (count + 2),
        scratch_shapes=[
            pltpu.VMEM(load.shape, f32),
            pltpu.VMEM((leaf, inner), f32),
            pltpu.SemaphoreType.DMA((count + 2,)),
        ],
        compiler_params=pltpu.CompilerParams(
            vmem_limit_bytes=START_ROOM - sum(4 * math.prod(s) for s in outs)
        ),
    )(load, leaf_load_map[0, 0], *kept_from_start)
    xs_all, xo_all, xi_all, ys_all, yo_all, yi_all, out_map = placed
    from_load = jnp.einsum(
        "wk,ik->wi", load_here, leaf_field_map[0, 0, :, leaf:], precision=lax.Precision.HIGH
    )

    def x_body(level, h_ref, own_ref, got_ref, solve_ref, xo_ref, h_out, w_out, *rest):
        kept = x_levels - 1 - level
        is_right = bit(my_column(), level) == 1
        own, got = own_ref[...], got_ref[...]
        left_child = jnp.where(is_right, got, own)
        right_child = jnp.where(is_right, own, got)
        v = jnp.concatenate([edge_of(left_child, 1), edge_of(right_child, 0)], axis=1)
        w = dot_t(v, solve_ref[level])
        w_out[...] = w
        if kept:
            next_ref, ends_ref = rest
            outer = [edge_of(x, 2 + kept) for x in (left_child, right_child)]
            spread = dot(w, jnp.concatenate([xo_ref[level]] + outer, axis=1))
            h_out[...] = h_ref[...] + spread[:, :leaf]
            left = edge_of(left_child, 0) + edge_of(spread, 4)
            right = edge_of(right_child, 1) + edge_of(spread, 5)
            ends_ref[...] = jnp.concatenate(
                [edge_of(left_child, 2), edge_of(right_child, 2)], axis=1
            )
            mine = jnp.where(bit(my_column(), level + 1) == 1, right_child, left_child)
            travelling = pieces_of(mine, 3, kept - 1) + pieces_of(mine, 3 + kept, kept - 1)
            next_ref[...] = pad_lanes(
                jnp.concatenate([left, right] + travelling, axis=1), next_ref.shape[1]
            )
        else:
            h_out[...] = h_ref[...] + dot(w, xo_ref[level])

    h = h0
    x_keep, ends = [], []
    for level in range(x_levels):
        got = lax.ppermute(to_send, "box", [(i, i ^ (1 << level)) for i in range(cols)])
        outs = [(waves, leaf), (waves, pair)]
        if level < x_levels - 1:
            outs += [exchange_shape(level + 1), (pair, pair)]
        h, w, *rest = fused(
            functools.partial(x_body, level), outs, h, to_send, got, xs_all, xo_all
        )
        x_keep.append(w)
        if rest:
            to_send, end = rest
            ends.append(end)

    def group(level):
        return tuple(row_axes[y_levels - 1 - level :]) + ("box",)

    def span(level):
        return 2 << level

    def swap(x, level):
        return lax.all_to_all(x, group(level), 0, 0, tiled=True)

    def offer_shape(level):
        size = span(level)
        return (size * cols, waves // size * edge // LANES, LANES)

    def store_offer(level, h, out):
        size = span(level)
        share = waves // size
        facing = jnp.where(
            lax.rem(my_row(), size) == size // 2 - 1, edge_of(h, 2), edge_of(h, 0)
        )
        for target in range(size):
            piece = packed(facing[target * share : (target + 1) * share], edge)
            out[target * cols : (target + 1) * cols] = jnp.broadcast_to(piece, (cols,) + piece.shape)

    def offer_body(level, h_ref, out_ref):
        store_offer(level, h_ref[...], out_ref)

    def solve_body(level, got_ref, solve_ref, out_ref, v_ref):
        size = span(level)
        low = (size // 2 - 1) * cols
        run = got_ref.shape[1]
        for side in range(2):
            for c in range(cols):
                piece = got_ref[low + side * cols + c]
                for k in range(LANES // edge):
                    start = c * pair + side * edge
                    v_ref[k * run : (k + 1) * run, start : start + edge] = edge_of(piece, k)
        w = packed(dot_t(v_ref[...], solve_ref[level]), pair)
        out_ref[...] = jnp.broadcast_to(w, out_ref.shape)

    def own_columns(w_all):
        own = w_all[:, :pair]
        for c in range(1, cols):
            own = jnp.where(my_column() == c, w_all[:, c * pair : (c + 1) * pair], own)
        return own

    def gather_w(level, got_ref, w_ref):
        size = span(level)
        share = waves // size
        run = got_ref.shape[1]
        for target in range(size):
            for c in range(cols):
                piece = got_ref[target * cols + c]
                for k in range(LANES // pair):
                    start = target * share + k * run
                    w_ref[start : start + run, c * pair : (c + 1) * pair] = piece[
                        :, k * pair : (k + 1) * pair
                    ]
        return w_ref[...]

    def spread_body(level, h_ref, got_ref, yo_ref, h_out, w_out, next_ref, w_ref):
        w_all = gather_w(level, got_ref, w_ref)
        w_out[...] = own_columns(w_all)
        h = h_ref[...] + dot_t(w_all, yo_ref[level])
        h_out[...] = h
        store_offer(level + 1, h, next_ref)

    def halves(level):
        return span(level) // 2

    def terms_shape(level):
        return (span(level) * cols, waves // halves(level) * edge // LANES, LANES)

    def store_terms(level, g, yi_ref, out):
        terms = dot_t(g, yi_ref[level])
        half = halves(level)
        share = waves // half
        for side in range(2):
            for c in range(cols):
                start = c * pair + side * edge
                piece = terms[:, start : start + edge]
                for part in range(half):
                    out[(side * half + part) * cols + c] = packed(
                        piece[part * share : (part + 1) * share], edge
                    )

    def turn_body(level, h_ref, got_ref, yo_ref, yi_ref, reflect_ref, w_out, g_out, out_ref, w_ref):
        w_all = gather_w(level, got_ref, w_ref)
        w_out[...] = own_columns(w_all)
        h = h_ref[...] + dot_t(w_all, yo_ref[level])
        lane = lax.broadcasted_iota(jnp.int32, (1, leaf), 1)

        def side(number):
            return (lane >= number * edge) & (lane < (number + 1) * edge)

        outer = (
            side(0) & (my_row() == 0)
            | side(1) & (my_column() == cols - 1)
            | side(2) & (my_row() == rows - 1)
            | side(3) & (my_column() == 0)
        )
        g = jnp.where(outer, h * reflect_ref[...], 0.0)
        g_out[...] = g
        store_terms(level, g, yi_ref, out_ref)

    def sum_body(got_ref, out_ref):
        out_ref[...] = jnp.sum(got_ref[...], axis=0)

    def with_row_edge(level, g, w, q):
        size = span(level)
        place = lax.rem(my_row(), size)
        is_low = place == size // 2 - 1
        is_high = place == size // 2
        value = jnp.where(place < size // 2, w[:, :edge], w[:, edge:]) + q
        bottom = jnp.where(is_high, value, edge_of(g, 0))
        top = jnp.where(is_low, value, edge_of(g, 2))
        return jnp.concatenate([bottom, edge_of(g, 1), top, edge_of(g, 3)], axis=1)

    def row_down_body(level, g_ref, w_ref, sum_ref, yi_ref, g_out, out_ref):
        g = with_row_edge(level, g_ref[...], w_ref[...], unpacked_parts(level, sum_ref))
        g_out[...] = g
        store_terms(level - 1, g, yi_ref, out_ref)

    def unpacked_parts(level, sum_ref):
        run = waves // halves(level) * edge // LANES
        return jnp.concatenate(
            [unpacked(sum_ref[i * run : (i + 1) * run], edge) for i in range(halves(level))], axis=0
        )

    def collect(total, level):
        for axis_no in range(level):
            axis = row_axes[y_levels - 1 - axis_no]
            other = lax.ppermute(total, axis, [(0, 1), (1, 0)])
            first = lax.axis_index(axis) == 0
            total = jnp.concatenate(
                [jnp.where(first, total, other), jnp.where(first, other, total)], axis=0
            )
        return total

    x_lanes = -(-x_levels * edge // LANES) * LANES

    def x_terms_body(g_ref, w_ref, sum_ref, xi_ref, g_out, out_ref):
        g = with_row_edge(0, g_ref[...], w_ref[...], unpacked_parts(0, sum_ref))
        g_out[...] = g
        terms = [dot_t(g, xi_ref[k]) for k in range(x_levels)]
        for c in range(cols):
            picked = []
            for k in range(x_levels):
                start = bit(c, k) * edge
                same = my_column() >> (k + 1) == c >> (k + 1)
                picked.append(jnp.where(same, terms[k][:, start : start + edge], 0.0))
            out_ref[c] = pad_lanes(jnp.concatenate(picked, axis=1), x_lanes)

    def finish_body(g_ref, h0_ref, got_ref, lo_ref, *refs):
        keep_ref, ends_ref = refs[:x_levels], refs[x_levels : 2 * x_levels - 1]
        g_out, t_out, *faces = refs[2 * x_levels - 1 :]
        g = g_ref[...]
        q = jnp.sum(got_ref[...], axis=0)
        gl = jnp.zeros((waves, edge), f32)
        gr = gl
        for level in reversed(range(x_levels)):
            is_right = bit(my_column(), level) == 1
            keep = keep_ref[level][...]
            value = edge_of(q, level) + jnp.where(is_right, keep[:, edge:], keep[:, :edge])
            if level < x_levels - 1:
                end = ends_ref[level][...]
                end = jnp.where(is_right, end[edge:], end[:edge])
                value = value + dot_t(jnp.concatenate([gl, gr], axis=1), end)
            gl = jnp.where(is_right, value, gl)
            gr = jnp.where(is_right, gr, value)
        g = jnp.concatenate(
            [edge_of(g, 0), edge_of(g, 1) + gr, edge_of(g, 2), edge_of(g, 3) + gl], axis=1
        )
        g_out[...] = g
        t = g - (dot_t(g, lo_ref[...]) + h0_ref[...])
        t_out[...] = t
        odd_col = bit(my_column(), 0) == 1
        odd_row = bit(my_row(), 0) == 1
        bottom, right, top, left = (packed(edge_of(t, i), edge) for i in range(4))
        faces[0][...] = jnp.where(odd_col, left, right)
        faces[1][...] = jnp.where(odd_col, right, left)
        faces[2][...] = jnp.where(odd_row, bottom, top)
        faces[3][...] = jnp.where(odd_row, top, bottom)

    def trace_body(t_ref, a_ref, b_ref, c_ref, d_ref, out_ref):
        t = t_ref[...]
        odd_col = bit(my_column(), 0) == 1
        odd_row = bit(my_row(), 0) == 1
        near_x, far_x, near_y, far_y = (
            unpacked(ref[...], edge) for ref in (a_ref, b_ref, c_ref, d_ref)
        )
        east = jnp.where(odd_col, far_x, near_x)
        west = jnp.where(odd_col, near_x, far_x)
        north = jnp.where(odd_row, far_y, near_y)
        south = jnp.where(odd_row, near_y, far_y)

        def mean(shared, own, other):
            return jnp.where(shared, 0.5 * (own + other), own)

        out_ref[...] = jnp.concatenate(
            [
                mean(my_row() > 0, edge_of(t, 0), south),
                mean(my_column() < cols - 1, edge_of(t, 1), east),
                mean(my_row() < rows - 1, edge_of(t, 2), north),
                mean(my_column() > 0, edge_of(t, 3), west),
            ],
            axis=1,
        )

    (offer,) = fused(functools.partial(offer_body, 0), [offer_shape(0)], h)
    y_keep = []
    for level in range(y_levels):
        share = waves // span(level)
        (w_offer,) = fused(
            functools.partial(solve_body, level),
            [(span(level) * cols, share * pair // LANES, LANES)],
            swap(offer, level),
            ys_all,
            scratch=[(share, iface)],
        )
        got = swap(w_offer, level)
        if level < y_levels - 1:
            h, w, offer = fused(
                functools.partial(spread_body, level),
                [(waves, leaf), (waves, pair), offer_shape(level + 1)],
                h,
                got,
                yo_all,
                scratch=[(waves, iface)],
            )
        else:
            w, g, terms = fused(
                functools.partial(turn_body, level),
                [(waves, pair), (waves, leaf), terms_shape(level)],
                h,
                got,
                yo_all,
                yi_all,
                reflect[0],
                scratch=[(waves, iface)],
            )
        y_keep.append(w)
    for level in reversed(range(y_levels)):
        (total,) = fused(sum_body, [terms_shape(level)[1:]], swap(terms, level))
        total = collect(total, level)
        if level > 0:
            g, terms = fused(
                functools.partial(row_down_body, level),
                [(waves, leaf), terms_shape(level - 1)],
                g,
                y_keep[level],
                total,
                yi_all,
            )
    g, terms = fused(
        x_terms_body,
        [(waves, leaf), (cols, waves, x_lanes)],
        g,
        y_keep[0],
        total,
        xi_all,
    )
    got = lax.all_to_all(terms, "box", 0, 0, tiled=True)
    face = (waves * edge // LANES, LANES)
    g, t, *faces = fused(
        finish_body,
        [(waves, leaf), (waves, leaf)] + [face] * 4,
        g,
        h0,
        got,
        out_map,
        *x_keep,
        *ends,
    )

    def near(count):
        return [(i, i ^ 1) for i in range(count)]

    def far(count):
        one_way = [(i, i + 1) for i in range(1, count - 1, 2)]
        return one_way + [(j, i) for i, j in one_way]

    seen = [
        lax.ppermute(faces[0], "box", near(cols)),
        lax.ppermute(faces[1], "box", far(cols)),
        lax.ppermute(faces[2], row_axes, near(rows)),
        lax.ppermute(faces[3], row_axes, far(rows)),
    ]
    field_vals = from_load + jnp.einsum(
        "wk,ik->wi", g, leaf_field_map[0, 0, :, :leaf], precision=lax.Precision.HIGH
    )
    (edge_trace,) = fused(trace_body, [(waves, leaf)], t, *seen)
    return (field_vals[:, None, None, :], edge_trace[:, None, None, :])


def solution(mesh):
    rows, cols = mesh.devices.shape
    bits = rows.bit_length() - 1
    row_axes = tuple(f"row{i}" for i in reversed(range(bits)))
    split = Mesh(mesh.devices.reshape((2,) * bits + (cols,)), row_axes + ("box",))
    late = P(None, row_axes, "box")
    early = P(row_axes, "box")
    return jax.shard_map(
        functools.partial(local, row_axes),
        mesh=split,
        in_specs=(late, early, early, early) + (late,) * 6 + (early,),
        out_specs=(late, late),
        check_vma=False,
    )
```

```python
import functools
import math

import jax
import jax.numpy as jnp
from jax import lax
from jax.experimental import pallas as pl
from jax.experimental.pallas import tpu as pltpu
from jax.sharding import Mesh, PartitionSpec as P

f32 = jnp.float32
LANES = 128
START_ROOM = 60 << 20


def dot(a, b, over=0):
    dims = (((1,), (over,)), ((), ()))

    def parts(x):
        high = x.astype(jnp.bfloat16)
        return high, (x - high.astype(f32)).astype(jnp.bfloat16)

    def product(x, y):
        return lax.dot_general(x, y, dims, preferred_element_type=f32)

    a_high, a_low = parts(a)
    b_high, b_low = parts(b)
    return product(a_high, b_high) + (product(a_high, b_low) + product(a_low, b_high))


def dot_t(a, b):
    return dot(a, b, 1)


def fused(body, outs, *args, scratch=()):
    vmem = pl.BlockSpec(memory_space=pltpu.VMEM)
    return pl.pallas_call(
        body,
        out_shape=[pltpu.VMEM(s, f32) for s in outs],
        in_specs=[vmem] * len(args),
        out_specs=[vmem] * len(outs),
        scratch_shapes=[pltpu.VMEM(s, f32) for s in scratch],
        compiler_params=pltpu.CompilerParams(vmem_limit_bytes=12 << 20),
    )(*args)


def packed(x, width):
    runs = LANES // width
    rows = x.shape[0] // runs
    return jnp.concatenate([x[i * rows : (i + 1) * rows] for i in range(runs)], axis=1)


def unpacked(x, width):
    return jnp.concatenate(
        [x[:, i * width : (i + 1) * width] for i in range(x.shape[1] // width)], axis=0
    )


def pad_lanes(x, lanes):
    if x.shape[1] == lanes:
        return x
    return jnp.concatenate([x, jnp.zeros((x.shape[0], lanes - x.shape[1]), f32)], axis=1)


def local(
    row_axes,
    load,
    leaf_load_map,
    leaf_out_map,
    leaf_field_map,
    x_solve,
    x_out,
    x_in,
    y_solve,
    y_out,
    y_in,
    reflect,
):
    edge = leaf_out_map.shape[-1] // 4
    cols = lax.axis_size("box")
    rows = 1
    for axis in row_axes:
        rows *= lax.axis_size(axis)
    x_levels = x_solve.shape[0]
    y_levels = y_solve.shape[0]
    waves = load.shape[0]
    leaf = 4 * edge
    pair = 2 * edge
    iface = cols * pair
    load_here = load[:, 0, 0, :]
    inner = load_here.shape[1]

    def my_column():
        return lax.axis_index("box")

    def my_row():
        return lax.axis_index(row_axes)

    def bit(value, level):
        return (value >> level) & 1

    def edge_of(x, number):
        return x[:, number * edge : (number + 1) * edge]

    def exchange_shape(level):
        kept = x_levels - 1 - level
        lanes = (2 + 2 * kept + (x_levels << level if kept else 0)) * edge
        return (pair, -(-lanes // LANES) * LANES)

    def pieces_of(x, first, count):
        return [edge_of(x, first + i) for i in range(count)]

    kept_from_start = [x_solve, jnp.swapaxes(x_out, 3, 4), x_in, y_solve, y_out, y_in]
    kept_from_start = [x[:, 0, 0] for x in kept_from_start] + [leaf_out_map[0, 0]]

    def start_body(load_any, map_any, *refs):
        count = len(kept_from_start)
        sources, (h_ref, out_ref) = refs[:count], refs[count : count + 2]
        targets = refs[count + 2 : 2 * count + 2]
        load_v, map_v, sems = refs[2 * count + 2 :]
        pairs = [(load_any, load_v), (map_any, map_v)] + list(zip(sources, targets))
        order = [0, 1, 4, 3, 2, 5, 6, 7, 8]
        copies = [pltpu.make_async_copy(a, b, sems.at[i]) for i, (a, b) in enumerate(pairs)]
        for i in order:
            copies[i].start()
        copies[0].wait()
        copies[1].wait()
        h = dot_t(load_v[...].reshape(waves, inner), map_v[...])
        h_ref[...] = h
        copies[4].wait()
        copies[3].wait()
        xo, xi = targets[1], targets[2]
        is_right = bit(my_column(), 0) == 1
        travelling = [
            jnp.where(is_right, edge_of(x[k], 1), edge_of(x[k], 3))
            for x in (xi, xo)
            for k in range(x_levels - 1)
        ]
        odd_row = bit(my_row(), 0) == 1
        travelling += [
            jnp.where(odd_row, edge_of(xi[k], 0), edge_of(xi[k], 2)) for k in range(x_levels)
        ]
        out_ref[...] = pad_lanes(
            jnp.concatenate([edge_of(h, 3), edge_of(h, 1)] + travelling, axis=1), out_ref.shape[1]
        )
        for i in order[4:]:
            copies[i].wait()

    anywhere, vmem = (pl.BlockSpec(memory_space=m) for m in (pl.ANY, pltpu.VMEM))
    count = len(kept_from_start)
    outs = [(waves, leaf), exchange_shape(0)] + [x.shape for x in kept_from_start]
    h0, to_send, *placed = pl.pallas_call(
        start_body,
        out_shape=[pltpu.VMEM(s, f32) for s in outs],
        in_specs=[anywhere] * (count + 2),
        out_specs=[vmem] * (count + 2),
        scratch_shapes=[
            pltpu.VMEM(load.shape, f32),
            pltpu.VMEM((leaf, inner), f32),
            pltpu.SemaphoreType.DMA((count + 2,)),
        ],
        compiler_params=pltpu.CompilerParams(
            vmem_limit_bytes=START_ROOM - sum(4 * math.prod(s) for s in outs)
        ),
    )(load, leaf_load_map[0, 0], *kept_from_start)
    xs_all, xo_all, xi_all, ys_all, yo_all, yi_all, out_map = placed
    from_load = jnp.einsum(
        "wk,ik->wi", load_here, leaf_field_map[0, 0, :, leaf:], precision=lax.Precision.HIGH
    )

    def x_body(level, h_ref, own_ref, got_ref, solve_ref, xo_ref, h_out, w_out, *rest):
        kept = x_levels - 1 - level
        is_right = bit(my_column(), level) == 1
        own, got = own_ref[...], got_ref[...]
        left_child = jnp.where(is_right, got, own)
        right_child = jnp.where(is_right, own, got)
        v = jnp.concatenate([edge_of(left_child, 1), edge_of(right_child, 0)], axis=1)
        w = dot_t(v, solve_ref[level])
        w_out[...] = w
        if kept:
            next_ref, ends_ref, row_ref = rest
            outer = [edge_of(x, 2 + kept) for x in (left_child, right_child)]
            spread = dot(w, jnp.concatenate([xo_ref[level]] + outer, axis=1))
            h_out[...] = h_ref[...] + spread[:, :leaf]
            left = edge_of(left_child, 0) + edge_of(spread, 4)
            right = edge_of(right_child, 1) + edge_of(spread, 5)
            ends_ref[...] = jnp.concatenate(
                [edge_of(left_child, 2), edge_of(right_child, 2)], axis=1
            )
            mine = jnp.where(bit(my_column(), level + 1) == 1, right_child, left_child)
            travelling = pieces_of(mine, 3, kept - 1) + pieces_of(mine, 3 + kept, kept - 1)
            known = x_levels << level
            row = pieces_of(left_child, 2 + 2 * kept, known)
            row += pieces_of(right_child, 2 + 2 * kept, known)
            if kept > 1:
                travelling += row
                row_ref[...] = jnp.zeros_like(row_ref)
            else:
                row_ref[...] = jnp.concatenate(row, axis=1)
            next_ref[...] = pad_lanes(
                jnp.concatenate([left, right] + travelling, axis=1), next_ref.shape[1]
            )
        else:
            h_out[...] = h_ref[...] + dot(w, xo_ref[level])

    h = h0
    x_keep, ends = [], []
    for level in range(x_levels):
        got = lax.ppermute(to_send, "box", [(i, i ^ (1 << level)) for i in range(cols)])
        outs = [(waves, leaf), (waves, pair)]
        if level < x_levels - 1:
            last = level == x_levels - 2
            outs += [exchange_shape(level + 1), (pair, pair)]
            outs += [(pair, iface * x_levels // 4) if last else (8, LANES)]
        h, w, *rest = fused(
            functools.partial(x_body, level), outs, h, to_send, got, xs_all, xo_all
        )
        x_keep.append(w)
        if rest:
            to_send, end, row_in = rest
            ends.append(end)
    top = x_levels - 1
    other_in = lax.ppermute(row_in, "box", [(i, i ^ (1 << top)) for i in range(cols)])

    def group(level):
        return tuple(row_axes[y_levels - 1 - level :]) + ("box",)

    def span(level):
        return 2 << level

    def swap(x, level):
        return lax.all_to_all(x, group(level), 0, 0, tiled=True)

    def offer_shape(level):
        size = span(level)
        return (size * cols, waves // size * edge // LANES, LANES)

    def store_offer(level, h, out):
        size = span(level)
        share = waves // size
        facing = jnp.where(
            lax.rem(my_row(), size) == size // 2 - 1, edge_of(h, 2), edge_of(h, 0)
        )
        for target in range(size):
            piece = packed(facing[target * share : (target + 1) * share], edge)
            out[target * cols : (target + 1) * cols] = jnp.broadcast_to(piece, (cols,) + piece.shape)

    def offer_body(level, h_ref, early_ref, out_ref):
        store_offer(level, h_ref[...], out_ref)

    def solve_body(level, got_ref, solve_ref, out_ref, v_ref):
        size = span(level)
        low = (size // 2 - 1) * cols
        run = got_ref.shape[1]
        for side in range(2):
            for c in range(cols):
                piece = got_ref[low + side * cols + c]
                for k in range(LANES // edge):
                    start = c * pair + side * edge
                    v_ref[k * run : (k + 1) * run, start : start + edge] = edge_of(piece, k)
        w = packed(dot_t(v_ref[...], solve_ref[level]), pair)
        out_ref[...] = jnp.broadcast_to(w, out_ref.shape)

    def own_columns(w_all):
        own = w_all[:, :pair]
        for c in range(1, cols):
            own = jnp.where(my_column() == c, w_all[:, c * pair : (c + 1) * pair], own)
        return own

    def gather_w(level, got_ref, w_ref):
        size = span(level)
        share = waves // size
        run = got_ref.shape[1]
        for target in range(size):
            for c in range(cols):
                piece = got_ref[target * cols + c]
                for k in range(LANES // pair):
                    start = target * share + k * run
                    w_ref[start : start + run, c * pair : (c + 1) * pair] = piece[
                        :, k * pair : (k + 1) * pair
                    ]
        return w_ref[...]

    def spread_body(level, h_ref, got_ref, yo_ref, h_out, w_out, next_ref, w_ref):
        w_all = gather_w(level, got_ref, w_ref)
        w_out[...] = own_columns(w_all)
        h = h_ref[...] + dot_t(w_all, yo_ref[level])
        h_out[...] = h
        store_offer(level + 1, h, next_ref)

    def halves(level):
        return span(level) // 2

    def terms_shape(level):
        return (span(level) * cols, waves // halves(level) * edge // LANES, LANES)

    def store_terms(level, g, yi_ref, out):
        terms = dot_t(g, yi_ref[level])
        half = halves(level)
        share = waves // half
        for side in range(2):
            for c in range(cols):
                start = c * pair + side * edge
                piece = terms[:, start : start + edge]
                for part in range(half):
                    out[(side * half + part) * cols + c] = packed(
                        piece[part * share : (part + 1) * share], edge
                    )

    def turn_body(level, h_ref, got_ref, yo_ref, yi_ref, reflect_ref, w_out, g_out, out_ref, w_ref):
        w_all = gather_w(level, got_ref, w_ref)
        w_out[...] = own_columns(w_all)
        h = h_ref[...] + dot_t(w_all, yo_ref[level])
        lane = lax.broadcasted_iota(jnp.int32, (1, leaf), 1)

        def side(number):
            return (lane >= number * edge) & (lane < (number + 1) * edge)

        outer = (
            side(0) & (my_row() == 0)
            | side(1) & (my_column() == cols - 1)
            | side(2) & (my_row() == rows - 1)
            | side(3) & (my_column() == 0)
        )
        g = jnp.where(outer, h * reflect_ref[...], 0.0)
        g_out[...] = g
        store_terms(level, g, yi_ref, out_ref)

    def sum_body(got_ref, out_ref):
        out_ref[...] = jnp.sum(got_ref[...], axis=0)

    def with_row_edge(level, g, w, q):
        size = span(level)
        place = lax.rem(my_row(), size)
        is_low = place == size // 2 - 1
        is_high = place == size // 2
        value = jnp.where(place < size // 2, w[:, :edge], w[:, edge:]) + q
        bottom = jnp.where(is_high, value, edge_of(g, 0))
        top = jnp.where(is_low, value, edge_of(g, 2))
        return jnp.concatenate([bottom, edge_of(g, 1), top, edge_of(g, 3)], axis=1)

    def row_down_body(level, g_ref, w_ref, sum_ref, yi_ref, g_out, out_ref):
        g = with_row_edge(level, g_ref[...], w_ref[...], unpacked_parts(level, sum_ref))
        g_out[...] = g
        store_terms(level - 1, g, yi_ref, out_ref)

    def unpacked_parts(level, sum_ref):
        run = waves // halves(level) * edge // LANES
        return jnp.concatenate(
            [unpacked(sum_ref[i * run : (i + 1) * run], edge) for i in range(halves(level))], axis=0
        )

    def collect(total, level):
        for axis_no in range(level):
            axis = row_axes[y_levels - 1 - axis_no]
            other = lax.ppermute(total, axis, [(0, 1), (1, 0)])
            first = lax.axis_index(axis) == 0
            total = jnp.concatenate(
                [jnp.where(first, total, other), jnp.where(first, other, total)], axis=0
            )
        return total

    x_lanes = -(-(x_levels + 1) * edge // LANES) * LANES

    def split_body(g_ref, w_ref, sum_ref, yi_ref, g_out, own_out, other_out):
        g = with_row_edge(1, g_ref[...], w_ref[...], unpacked_parts(1, sum_ref))
        g_out[...] = g
        terms = dot_t(g, yi_ref[0])
        odd_row = bit(my_row(), 0) == 1
        low, high = (
            jnp.concatenate(
                [terms[:, c * pair + side * edge :][:, :edge] for c in range(cols)], axis=1
            )
            for side in range(2)
        )
        own_out[...] = jnp.where(odd_row, high, low)
        other_out[...] = jnp.where(odd_row, low, high)

    def x_terms_body(g_ref, w_ref, own_ref, got_ref, xi_ref, row_ref, other_ref, out_ref):
        q = own_ref[...] + got_ref[...]
        g = with_row_edge(0, g_ref[...], w_ref[...], 0.0)
        is_right = bit(my_column(), top) == 1
        row, other = row_ref[...], other_ref[...]
        matrices = [jnp.where(is_right, other, row), jnp.where(is_right, row, other)]
        half = cols // 2
        parts = []
        for k in range(x_levels):
            known = dot_t(g, xi_ref[k])
            size = 2 << k
            nodes = []
            for first in range(0, cols, size):
                matrix = jnp.concatenate(
                    [
                        edge_of(matrices[c // half], c % half * x_levels + k)
                        for c in range(first, first + size)
                    ],
                    axis=1,
                )
                terms = dot_t(q[:, first * edge : (first + size) * edge], matrix)
                inside = my_column() >> (k + 1) == first >> (k + 1)
                nodes.append(terms + jnp.where(inside, known, 0.0))
            parts.append(nodes)
        for c in range(cols):
            picked = [edge_of(parts[k][c >> (k + 1)], bit(c, k)) for k in range(x_levels)]
            out_ref[c] = pad_lanes(jnp.concatenate(picked + [edge_of(q, c)], axis=1), x_lanes)

    def finish_body(g_ref, w_ref, h0_ref, got_ref, lo_ref, *refs):
        keep_ref, ends_ref = refs[:x_levels], refs[x_levels : 2 * x_levels - 1]
        g_out, t_out, *faces = refs[2 * x_levels - 1 :]
        q = jnp.sum(got_ref[...], axis=0)
        g = with_row_edge(0, g_ref[...], w_ref[...], edge_of(q, x_levels))
        gl = jnp.zeros((waves, edge), f32)
        gr = gl
        for level in reversed(range(x_levels)):
            is_right = bit(my_column(), level) == 1
            keep = keep_ref[level][...]
            value = edge_of(q, level) + jnp.where(is_right, keep[:, edge:], keep[:, :edge])
            if level < x_levels - 1:
                end = ends_ref[level][...]
                end = jnp.where(is_right, end[edge:], end[:edge])
                value = value + dot_t(jnp.concatenate([gl, gr], axis=1), end)
            gl = jnp.where(is_right, value, gl)
            gr = jnp.where(is_right, gr, value)
        g = jnp.concatenate(
            [edge_of(g, 0), edge_of(g, 1) + gr, edge_of(g, 2), edge_of(g, 3) + gl], axis=1
        )
        g_out[...] = g
        t = g - (dot_t(g, lo_ref[...]) + h0_ref[...])
        t_out[...] = t
        odd_col = bit(my_column(), 0) == 1
        odd_row = bit(my_row(), 0) == 1
        bottom, right, top, left = (packed(edge_of(t, i), edge) for i in range(4))
        faces[0][...] = jnp.where(odd_col, left, right)
        faces[1][...] = jnp.where(odd_col, right, left)
        faces[2][...] = jnp.where(odd_row, bottom, top)
        faces[3][...] = jnp.where(odd_row, top, bottom)

    def trace_body(t_ref, a_ref, b_ref, c_ref, d_ref, out_ref):
        t = t_ref[...]
        odd_col = bit(my_column(), 0) == 1
        odd_row = bit(my_row(), 0) == 1
        near_x, far_x, near_y, far_y = (
            unpacked(ref[...], edge) for ref in (a_ref, b_ref, c_ref, d_ref)
        )
        east = jnp.where(odd_col, far_x, near_x)
        west = jnp.where(odd_col, near_x, far_x)
        north = jnp.where(odd_row, far_y, near_y)
        south = jnp.where(odd_row, near_y, far_y)

        def mean(shared, own, other):
            return jnp.where(shared, 0.5 * (own + other), own)

        out_ref[...] = jnp.concatenate(
            [
                mean(my_row() > 0, edge_of(t, 0), south),
                mean(my_column() < cols - 1, edge_of(t, 1), east),
                mean(my_row() < rows - 1, edge_of(t, 2), north),
                mean(my_column() > 0, edge_of(t, 3), west),
            ],
            axis=1,
        )

    (offer,) = fused(functools.partial(offer_body, 0), [offer_shape(0)], h, other_in)
    y_keep = []
    for level in range(y_levels):
        share = waves // span(level)
        (w_offer,) = fused(
            functools.partial(solve_body, level),
            [(span(level) * cols, share * pair // LANES, LANES)],
            swap(offer, level),
            ys_all,
            scratch=[(share, iface)],
        )
        got = swap(w_offer, level)
        if level < y_levels - 1:
            h, w, offer = fused(
                functools.partial(spread_body, level),
                [(waves, leaf), (waves, pair), offer_shape(level + 1)],
                h,
                got,
                yo_all,
                scratch=[(waves, iface)],
            )
        else:
            w, g, terms = fused(
                functools.partial(turn_body, level),
                [(waves, pair), (waves, leaf), terms_shape(level)],
                h,
                got,
                yo_all,
                yi_all,
                reflect[0],
                scratch=[(waves, iface)],
            )
        y_keep.append(w)
    for level in reversed(range(1, y_levels)):
        (total,) = fused(sum_body, [terms_shape(level)[1:]], swap(terms, level))
        total = collect(total, level)
        if level > 1:
            g, terms = fused(
                functools.partial(row_down_body, level),
                [(waves, leaf), terms_shape(level - 1)],
                g,
                y_keep[level],
                total,
                yi_all,
            )
    share = (waves, iface // 2)
    g, own, other = fused(
        split_body, [(waves, leaf), share, share], g, y_keep[1], total, yi_all
    )
    got = lax.ppermute(other, row_axes[-1], [(0, 1), (1, 0)])
    (terms,) = fused(
        x_terms_body,
        [(cols, waves, x_lanes)],
        g,
        y_keep[0],
        own,
        got,
        xi_all,
        row_in,
        other_in,
    )
    got = lax.all_to_all(terms, "box", 0, 0, tiled=True)
    face = (waves * edge // LANES, LANES)
    g, t, *faces = fused(
        finish_body,
        [(waves, leaf), (waves, leaf)] + [face] * 4,
        g,
        y_keep[0],
        h0,
        got,
        out_map,
        *x_keep,
        *ends,
    )

    def near(count):
        return [(i, i ^ 1) for i in range(count)]

    def far(count):
        one_way = [(i, i + 1) for i in range(1, count - 1, 2)]
        return one_way + [(j, i) for i, j in one_way]

    seen = [
        lax.ppermute(faces[0], "box", near(cols)),
        lax.ppermute(faces[1], "box", far(cols)),
        lax.ppermute(faces[2], row_axes, near(rows)),
        lax.ppermute(faces[3], row_axes, far(rows)),
    ]
    field_vals = from_load + jnp.einsum(
        "wk,ik->wi", g, leaf_field_map[0, 0, :, :leaf], precision=lax.Precision.HIGH
    )
    (edge_trace,) = fused(trace_body, [(waves, leaf)], t, *seen)
    return (field_vals[:, None, None, :], edge_trace[:, None, None, :])


def solution(mesh):
    rows, cols = mesh.devices.shape
    bits = rows.bit_length() - 1
    row_axes = tuple(f"row{i}" for i in reversed(range(bits)))
    split = Mesh(mesh.devices.reshape((2,) * bits + (cols,)), row_axes + ("box",))
    late = P(None, row_axes, "box")
    early = P(row_axes, "box")
    return jax.shard_map(
        functools.partial(local, row_axes),
        mesh=split,
        in_specs=(late, early, early, early) + (late,) * 6 + (early,),
        out_specs=(late, late),
        check_vma=False,
    )
```

```python
import functools
import math

import jax
import jax.numpy as jnp
from jax import lax
from jax.experimental import pallas as pl
from jax.experimental.pallas import tpu as pltpu
from jax.sharding import Mesh, PartitionSpec as P

f32 = jnp.float32
LANES = 128
START_ROOM = 60 << 20


def dot(a, b, over=0):
    dims = (((1,), (over,)), ((), ()))

    def parts(x):
        high = x.astype(jnp.bfloat16)
        return high, (x - high.astype(f32)).astype(jnp.bfloat16)

    def product(x, y):
        return lax.dot_general(x, y, dims, preferred_element_type=f32)

    a_high, a_low = parts(a)
    b_high, b_low = parts(b)
    return product(a_high, b_high) + (product(a_high, b_low) + product(a_low, b_high))


def dot_t(a, b):
    return dot(a, b, 1)


def fused(body, outs, *args, scratch=(), aliases=None):
    vmem = pl.BlockSpec(memory_space=pltpu.VMEM)
    return pl.pallas_call(
        body,
        out_shape=[pltpu.VMEM(s, f32) for s in outs],
        in_specs=[vmem] * len(args),
        out_specs=[vmem] * len(outs),
        scratch_shapes=[pltpu.VMEM(s, f32) for s in scratch],
        input_output_aliases=aliases or {},
        compiler_params=pltpu.CompilerParams(vmem_limit_bytes=12 << 20),
    )(*args)


def packed(x, width):
    runs = LANES // width
    rows = x.shape[0] // runs
    return jnp.concatenate([x[i * rows : (i + 1) * rows] for i in range(runs)], axis=1)


def unpacked(x, width):
    return jnp.concatenate(
        [x[:, i * width : (i + 1) * width] for i in range(x.shape[1] // width)], axis=0
    )


def pad_lanes(x, lanes):
    if x.shape[1] == lanes:
        return x
    return jnp.concatenate([x, jnp.zeros((x.shape[0], lanes - x.shape[1]), f32)], axis=1)


def local(
    row_axes,
    load,
    leaf_load_map,
    leaf_out_map,
    leaf_field_map,
    x_solve,
    x_out,
    x_in,
    y_solve,
    y_out,
    y_in,
    reflect,
):
    edge = leaf_out_map.shape[-1] // 4
    cols = lax.axis_size("box")
    rows = 1
    for axis in row_axes:
        rows *= lax.axis_size(axis)
    x_levels = x_solve.shape[0]
    y_levels = y_solve.shape[0]
    waves = load.shape[0]
    leaf = 4 * edge
    pair = 2 * edge
    iface = cols * pair
    load_here = load[:, 0, 0, :]
    inner = load_here.shape[1]

    def my_column():
        return lax.axis_index("box")

    def my_row():
        return lax.axis_index(row_axes)

    def bit(value, level):
        return (value >> level) & 1

    def edge_of(x, number):
        return x[:, number * edge : (number + 1) * edge]

    def exchange_shape(level):
        kept = x_levels - 1 - level
        lanes = (2 + 2 * kept) * edge
        return (pair, -(-lanes // LANES) * LANES)

    def pieces_of(x, first, count):
        return [edge_of(x, first + i) for i in range(count)]

    kept_from_start = [x_solve, jnp.swapaxes(x_out, 3, 4), x_in, y_solve, y_out, y_in]
    kept_from_start = [x[:, 0, 0] for x in kept_from_start] + [leaf_out_map[0, 0]]

    whole_solve = iface * iface <= 1 << 18
    in_lanes = -(-x_levels * edge // LANES) * LANES
    width = iface if whole_solve else 4 * in_lanes
    runs = width // in_lanes
    in_rows = pair // runs
    solve_rows = edge if whole_solve else 0

    def held_shape(count):
        return (count, solve_rows + in_rows, width)

    def passed_on(held, bit_no):
        return lax.ppermute(held, "box", [(i, i ^ (1 << bit_no)) for i in range(cols)])

    steps = [x_levels - 1] + list(range(x_levels - 1))
    joined_at = [0] + list(range(2, x_levels))

    def held_of(c, held_ref, moved_ref):
        place = sum(bit(c, b) << k for k, b in enumerate(steps[:-1]))
        same = bit(my_column(), steps[-1]) == bit(c, steps[-1])
        return jnp.where(same, held_ref[place], moved_ref[place])

    def join(step, held_ref, moved_ref, both_ref):
        high = bit(my_column(), steps[step]) == 1
        both_ref[: 1 << step] = jnp.where(high, moved_ref[...], held_ref[...])
        both_ref[1 << step :] = jnp.where(high, held_ref[...], moved_ref[...])

    def start_body(load_any, map_any, *refs):
        count = len(kept_from_start)
        sources, (h_ref, out_ref, shared_ref) = refs[:count], refs[count : count + 3]
        targets = refs[count + 3 : 2 * count + 3]
        load_v, map_v, sems = refs[2 * count + 3 :]
        odd_row = bit(my_row(), 0)
        sent = []
        if whole_solve:
            sent = [
                pltpu.make_async_copy(
                    sources[3].at[0, pl.ds(odd_row * edge, edge)],
                    shared_ref.at[0, pl.ds(0, edge)],
                    sems.at[count + 2],
                )
            ]
        pairs = [(load_any, load_v), (map_any, map_v)] + list(zip(sources, targets))
        order = [0, 1, 4, 3, 2, 5, 6, 7, 8]
        copies = [pltpu.make_async_copy(a, b, sems.at[i]) for i, (a, b) in enumerate(pairs)]
        for i in order[:4]:
            copies[i].start()
        for copy in sent:
            copy.start()
        for i in order[4:]:
            copies[i].start()
        copies[0].wait()
        copies[1].wait()
        h = dot_t(load_v[...].reshape(waves, inner), map_v[...])
        h_ref[...] = h
        copies[4].wait()
        copies[3].wait()
        xo, xi = targets[1], targets[2]
        is_right = bit(my_column(), 0) == 1
        travelling = [
            jnp.where(is_right, edge_of(x[k], 1), edge_of(x[k], 3))
            for x in (xi, xo)
            for k in range(x_levels - 1)
        ]
        out_ref[...] = pad_lanes(
            jnp.concatenate([edge_of(h, 3), edge_of(h, 1)] + travelling, axis=1), out_ref.shape[1]
        )
        row_in = pad_lanes(
            jnp.concatenate(
                [
                    jnp.where(odd_row == 1, edge_of(xi[k], 0), edge_of(xi[k], 2))
                    for k in range(x_levels)
                ],
                axis=1,
            ),
            in_lanes,
        )
        row_in = jnp.concatenate(
            [row_in[i * in_rows : (i + 1) * in_rows] for i in range(runs)], axis=1
        )
        shared_ref[0, solve_rows:] = row_in
        for copy in sent:
            copy.wait()
        for i in order[4:]:
            copies[i].wait()

    anywhere, vmem = (pl.BlockSpec(memory_space=m) for m in (pl.ANY, pltpu.VMEM))
    count = len(kept_from_start)
    outs = [(waves, leaf), exchange_shape(0), held_shape(1)] + [x.shape for x in kept_from_start]
    h0, to_send, held, *placed = pl.pallas_call(
        start_body,
        out_shape=[pltpu.VMEM(s, f32) for s in outs],
        in_specs=[anywhere] * (count + 2),
        out_specs=[vmem] * len(outs),
        scratch_shapes=[
            pltpu.VMEM(load.shape, f32),
            pltpu.VMEM((leaf, inner), f32),
            pltpu.SemaphoreType.DMA((count + 3,)),
        ],
        compiler_params=pltpu.CompilerParams(
            vmem_limit_bytes=START_ROOM - sum(4 * math.prod(s) for s in outs)
        ),
    )(load, leaf_load_map[0, 0], *kept_from_start)
    xs_all, xo_all, xi_all, ys_all, yo_all, yi_all, out_map = placed
    from_load = jnp.einsum(
        "wk,ik->wi", load_here, leaf_field_map[0, 0, :, leaf:], precision=lax.Precision.HIGH
    )

    def x_body(level, h_ref, own_ref, got_ref, solve_ref, xo_ref, *rest):
        kept = x_levels - 1 - level
        rest = list(rest)
        if level in joined_at:
            join(joined_at.index(level), rest.pop(0), rest.pop(0), rest.pop())
        h_out, w_out, *rest = rest
        is_right = bit(my_column(), level) == 1
        own, got = own_ref[...], got_ref[...]
        left_child = jnp.where(is_right, got, own)
        right_child = jnp.where(is_right, own, got)
        v = jnp.concatenate([edge_of(left_child, 1), edge_of(right_child, 0)], axis=1)
        w = dot_t(v, solve_ref[level])
        w_out[...] = w
        if kept:
            next_ref, ends_ref = rest
            outer = [edge_of(x, 2 + kept) for x in (left_child, right_child)]
            spread = dot(w, jnp.concatenate([xo_ref[level]] + outer, axis=1))
            h_out[...] = h_ref[...] + spread[:, :leaf]
            left = edge_of(left_child, 0) + edge_of(spread, 4)
            right = edge_of(right_child, 1) + edge_of(spread, 5)
            ends_ref[...] = jnp.concatenate(
                [edge_of(left_child, 2), edge_of(right_child, 2)], axis=1
            )
            mine = jnp.where(bit(my_column(), level + 1) == 1, right_child, left_child)
            travelling = pieces_of(mine, 3, kept - 1) + pieces_of(mine, 3 + kept, kept - 1)
            next_ref[...] = pad_lanes(
                jnp.concatenate([left, right] + travelling, axis=1), next_ref.shape[1]
            )
        else:
            h_out[...] = h_ref[...] + dot(w, xo_ref[level])

    h = h0
    x_keep, ends = [], []
    moved = passed_on(held, steps[0])
    for level in range(x_levels):
        got = lax.ppermute(to_send, "box", [(i, i ^ (1 << level)) for i in range(cols)])
        outs = [(waves, leaf), (waves, pair)]
        args = [h, to_send, got, xs_all, xo_all]
        if level < x_levels - 1:
            outs += [exchange_shape(level + 1), (pair, pair)]
        if level in joined_at:
            step = joined_at.index(level)
            outs.append(held_shape(2 << step))
            args += [held, moved]
        h, w, *rest = fused(functools.partial(x_body, level), outs, *args)
        x_keep.append(w)
        if level in joined_at:
            held = rest.pop()
            moved = passed_on(held, steps[step + 1])
        if rest:
            to_send, end = rest
            ends.append(end)

    def group(level):
        return tuple(row_axes[y_levels - 1 - level :]) + ("box",)

    def span(level):
        return 2 << level

    def swap(x, level):
        return lax.all_to_all(x, group(level), 0, 0, tiled=True)

    def shares(level):
        return 1 if level == 0 and whole_solve else span(level)

    def offer_shape(level):
        return (span(level) * cols, waves // shares(level) * edge // LANES, LANES)

    def store_offer(level, h, out):
        size = span(level)
        share = waves // shares(level)
        facing = jnp.where(
            lax.rem(my_row(), size) == size // 2 - 1, edge_of(h, 2), edge_of(h, 0)
        )
        for target in range(size):
            start = target * share % waves
            piece = packed(facing[start : start + share], edge)
            out[target * cols : (target + 1) * cols] = jnp.broadcast_to(piece, (cols,) + piece.shape)

    def offer_body(level, h_ref, out_ref):
        store_offer(level, h_ref[...], out_ref)

    def gather_v(level, got_ref, v_ref):
        size = span(level)
        low = (size // 2 - 1) * cols
        run = got_ref.shape[1]
        for side in range(2):
            for c in range(cols):
                piece = got_ref[low + side * cols + c]
                for k in range(LANES // edge):
                    start = c * pair + side * edge
                    v_ref[k * run : (k + 1) * run, start : start + edge] = edge_of(piece, k)

    def solve_body(level, got_ref, solve_ref, out_ref, v_ref):
        gather_v(level, got_ref, v_ref)
        w = packed(dot_t(v_ref[...], solve_ref[level]), pair)
        out_ref[...] = jnp.broadcast_to(w, out_ref.shape)

    def own_columns(w_all):
        own = w_all[:, :pair]
        for c in range(1, cols):
            own = jnp.where(my_column() == c, w_all[:, c * pair : (c + 1) * pair], own)
        return own

    def gather_w(level, got_ref, w_ref):
        size = span(level)
        share = waves // size
        run = got_ref.shape[1]
        for target in range(size):
            for c in range(cols):
                piece = got_ref[target * cols + c]
                for k in range(LANES // pair):
                    start = target * share + k * run
                    w_ref[start : start + run, c * pair : (c + 1) * pair] = piece[
                        :, k * pair : (k + 1) * pair
                    ]
        return w_ref[...]

    def half_body(got_ref, held_ref, moved_ref, out_ref, v_ref):
        gather_v(0, got_ref, v_ref)
        solve = jnp.concatenate(
            [held_of(c, held_ref, moved_ref)[:solve_rows] for c in range(cols)], axis=0
        )
        out_ref[...] = dot_t(v_ref[...], solve)

    def whole_body(h_ref, mine_ref, other_ref, yo_ref, h_out, w_out, next_ref, w_ref):
        mine, other = mine_ref[...], other_ref[...]
        odd_row = bit(my_row(), 0) == 1
        for side, half in enumerate(
            (jnp.where(odd_row, other, mine), jnp.where(odd_row, mine, other))
        ):
            for c in range(cols):
                start = c * pair + side * edge
                w_ref[:, start : start + edge] = edge_of(half, c)
        w_all = w_ref[...]
        w_out[...] = own_columns(w_all)
        h = h_ref[...] + dot_t(w_all, yo_ref[0])
        h_out[...] = h
        store_offer(1, h, next_ref)

    def spread_body(level, h_ref, got_ref, yo_ref, h_out, w_out, next_ref, w_ref):
        w_all = gather_w(level, got_ref, w_ref)
        w_out[...] = own_columns(w_all)
        h = h_ref[...] + dot_t(w_all, yo_ref[level])
        h_out[...] = h
        store_offer(level + 1, h, next_ref)

    def halves(level):
        return span(level) // 2

    def terms_shape(level):
        return (span(level) * cols, waves // halves(level) * edge // LANES, LANES)

    def store_terms(level, g, yi_ref, out):
        terms = dot_t(g, yi_ref[level])
        half = halves(level)
        share = waves // half
        for side in range(2):
            for c in range(cols):
                start = c * pair + side * edge
                piece = terms[:, start : start + edge]
                for part in range(half):
                    out[(side * half + part) * cols + c] = packed(
                        piece[part * share : (part + 1) * share], edge
                    )

    def turn_body(level, h_ref, got_ref, yo_ref, yi_ref, reflect_ref, w_out, g_out, out_ref, w_ref):
        w_all = gather_w(level, got_ref, w_ref)
        w_out[...] = own_columns(w_all)
        h = h_ref[...] + dot_t(w_all, yo_ref[level])
        lane = lax.broadcasted_iota(jnp.int32, (1, leaf), 1)

        def side(number):
            return (lane >= number * edge) & (lane < (number + 1) * edge)

        outer = (
            side(0) & (my_row() == 0)
            | side(1) & (my_column() == cols - 1)
            | side(2) & (my_row() == rows - 1)
            | side(3) & (my_column() == 0)
        )
        g = jnp.where(outer, h * reflect_ref[...], 0.0)
        g_out[...] = g
        store_terms(level, g, yi_ref, out_ref)

    def sum_body(got_ref, out_ref):
        out_ref[...] = jnp.sum(got_ref[...], axis=0)

    def with_row_edge(level, g, w, q):
        size = span(level)
        place = lax.rem(my_row(), size)
        is_low = place == size // 2 - 1
        is_high = place == size // 2
        value = jnp.where(place < size // 2, w[:, :edge], w[:, edge:]) + q
        bottom = jnp.where(is_high, value, edge_of(g, 0))
        top = jnp.where(is_low, value, edge_of(g, 2))
        return jnp.concatenate([bottom, edge_of(g, 1), top, edge_of(g, 3)], axis=1)

    def row_down_body(level, g_ref, w_ref, sum_ref, yi_ref, g_out, out_ref):
        g = with_row_edge(level, g_ref[...], w_ref[...], unpacked_parts(level, sum_ref))
        g_out[...] = g
        store_terms(level - 1, g, yi_ref, out_ref)

    def unpacked_parts(level, sum_ref):
        run = waves // halves(level) * edge // LANES
        return jnp.concatenate(
            [unpacked(sum_ref[i * run : (i + 1) * run], edge) for i in range(halves(level))], axis=0
        )

    def collect(total, level):
        for axis_no in range(level):
            axis = row_axes[y_levels - 1 - axis_no]
            other = lax.ppermute(total, axis, [(0, 1), (1, 0)])
            first = lax.axis_index(axis) == 0
            total = jnp.concatenate(
                [jnp.where(first, total, other), jnp.where(first, other, total)], axis=0
            )
        return total

    x_lanes = -(-(x_levels + 1) * edge // LANES) * LANES

    def split_body(g_ref, w_ref, sum_ref, yi_ref, g_out, own_out, other_out):
        g = with_row_edge(1, g_ref[...], w_ref[...], unpacked_parts(1, sum_ref))
        g_out[...] = g
        terms = dot_t(g, yi_ref[0])
        odd_row = bit(my_row(), 0) == 1
        low, high = (
            jnp.concatenate(
                [terms[:, c * pair + side * edge :][:, :edge] for c in range(cols)], axis=1
            )
            for side in range(2)
        )
        own_out[...] = jnp.where(odd_row, high, low)
        other_out[...] = jnp.where(odd_row, low, high)

    def x_terms_body(g_ref, w_ref, own_ref, got_ref, xi_ref, held_ref, moved_ref, out_ref):
        q = own_ref[...] + got_ref[...]
        g = with_row_edge(0, g_ref[...], w_ref[...], 0.0)
        row_in = []
        for c in range(cols):
            held = held_of(c, held_ref, moved_ref)[solve_rows:]
            row_in.append(
                jnp.concatenate(
                    [held[:, i * in_lanes : (i + 1) * in_lanes] for i in range(runs)], axis=0
                )
            )
        parts = []
        for k in range(x_levels):
            known = dot_t(g, xi_ref[k])
            size = 2 << k
            nodes = []
            for first in range(0, cols, size):
                matrix = jnp.concatenate(
                    [edge_of(row_in[c], k) for c in range(first, first + size)], axis=1
                )
                terms = dot_t(q[:, first * edge : (first + size) * edge], matrix)
                inside = my_column() >> (k + 1) == first >> (k + 1)
                nodes.append(terms + jnp.where(inside, known, 0.0))
            parts.append(nodes)
        for c in range(cols):
            picked = [edge_of(parts[k][c >> (k + 1)], bit(c, k)) for k in range(x_levels)]
            out_ref[c] = pad_lanes(jnp.concatenate(picked + [edge_of(q, c)], axis=1), x_lanes)

    def finish_body(g_ref, w_ref, h0_ref, got_ref, lo_ref, *refs):
        keep_ref, ends_ref = refs[:x_levels], refs[x_levels : 2 * x_levels - 1]
        g_out, t_out, *faces = refs[2 * x_levels - 1 :]
        q = jnp.sum(got_ref[...], axis=0)
        g = with_row_edge(0, g_ref[...], w_ref[...], edge_of(q, x_levels))
        gl = jnp.zeros((waves, edge), f32)
        gr = gl
        for level in reversed(range(x_levels)):
            is_right = bit(my_column(), level) == 1
            keep = keep_ref[level][...]
            value = edge_of(q, level) + jnp.where(is_right, keep[:, edge:], keep[:, :edge])
            if level < x_levels - 1:
                end = ends_ref[level][...]
                end = jnp.where(is_right, end[edge:], end[:edge])
                value = value + dot_t(jnp.concatenate([gl, gr], axis=1), end)
            gl = jnp.where(is_right, value, gl)
            gr = jnp.where(is_right, gr, value)
        g = jnp.concatenate(
            [edge_of(g, 0), edge_of(g, 1) + gr, edge_of(g, 2), edge_of(g, 3) + gl], axis=1
        )
        g_out[...] = g
        t = g - (dot_t(g, lo_ref[...]) + h0_ref[...])
        t_out[...] = t
        odd_col = bit(my_column(), 0) == 1
        odd_row = bit(my_row(), 0) == 1
        bottom, right, top, left = (packed(edge_of(t, i), edge) for i in range(4))
        faces[0][...] = jnp.where(odd_col, left, right)
        faces[1][...] = jnp.where(odd_col, right, left)
        faces[2][...] = jnp.where(odd_row, bottom, top)
        faces[3][...] = jnp.where(odd_row, top, bottom)

    def trace_body(t_ref, a_ref, b_ref, c_ref, d_ref, out_ref):
        t = t_ref[...]
        odd_col = bit(my_column(), 0) == 1
        odd_row = bit(my_row(), 0) == 1
        near_x, far_x, near_y, far_y = (
            unpacked(ref[...], edge) for ref in (a_ref, b_ref, c_ref, d_ref)
        )
        east = jnp.where(odd_col, far_x, near_x)
        west = jnp.where(odd_col, near_x, far_x)
        north = jnp.where(odd_row, far_y, near_y)
        south = jnp.where(odd_row, near_y, far_y)

        def mean(shared, own, other):
            return jnp.where(shared, 0.5 * (own + other), own)

        out_ref[...] = jnp.concatenate(
            [
                mean(my_row() > 0, edge_of(t, 0), south),
                mean(my_column() < cols - 1, edge_of(t, 1), east),
                mean(my_row() < rows - 1, edge_of(t, 2), north),
                mean(my_column() > 0, edge_of(t, 3), west),
            ],
            axis=1,
        )

    (offer,) = fused(functools.partial(offer_body, 0), [offer_shape(0)], h)
    y_keep = []
    for level in range(y_levels):
        if level == 0 and whole_solve:
            (mine,) = fused(
                half_body,
                [(waves, iface // 2)],
                swap(offer, 0),
                held,
                moved,
                scratch=[(waves, iface)],
            )
            h, w, offer = fused(
                whole_body,
                [(waves, leaf), (waves, pair), offer_shape(1)],
                h,
                mine,
                lax.ppermute(mine, row_axes[-1], [(0, 1), (1, 0)]),
                yo_all,
                scratch=[(waves, iface)],
            )
            y_keep.append(w)
            continue
        share = waves // span(level)
        (w_offer,) = fused(
            functools.partial(solve_body, level),
            [(span(level) * cols, share * pair // LANES, LANES)],
            swap(offer, level),
            ys_all,
            scratch=[(share, iface)],
        )
        got = swap(w_offer, level)
        if level < y_levels - 1:
            h, w, offer = fused(
                functools.partial(spread_body, level),
                [(waves, leaf), (waves, pair), offer_shape(level + 1)],
                h,
                got,
                yo_all,
                scratch=[(waves, iface)],
            )
        else:
            w, g, terms = fused(
                functools.partial(turn_body, level),
                [(waves, pair), (waves, leaf), terms_shape(level)],
                h,
                got,
                yo_all,
                yi_all,
                reflect[0],
                scratch=[(waves, iface)],
            )
        y_keep.append(w)
    for level in reversed(range(1, y_levels)):
        (total,) = fused(sum_body, [terms_shape(level)[1:]], swap(terms, level))
        total = collect(total, level)
        if level > 1:
            g, terms = fused(
                functools.partial(row_down_body, level),
                [(waves, leaf), terms_shape(level - 1)],
                g,
                y_keep[level],
                total,
                yi_all,
            )
    share = (waves, iface // 2)
    g, own, other = fused(
        split_body, [(waves, leaf), share, share], g, y_keep[1], total, yi_all
    )
    got = lax.ppermute(other, row_axes[-1], [(0, 1), (1, 0)])
    (terms,) = fused(
        x_terms_body,
        [(cols, waves, x_lanes)],
        g,
        y_keep[0],
        own,
        got,
        xi_all,
        held,
        moved,
    )
    got = lax.all_to_all(terms, "box", 0, 0, tiled=True)
    face = (waves * edge // LANES, LANES)
    g, t, *faces = fused(
        finish_body,
        [(waves, leaf), (waves, leaf)] + [face] * 4,
        g,
        y_keep[0],
        h0,
        got,
        out_map,
        *x_keep,
        *ends,
    )

    def near(count):
        return [(i, i ^ 1) for i in range(count)]

    def far(count):
        one_way = [(i, i + 1) for i in range(1, count - 1, 2)]
        return one_way + [(j, i) for i, j in one_way]

    seen = [
        lax.ppermute(faces[0], "box", near(cols)),
        lax.ppermute(faces[1], "box", far(cols)),
        lax.ppermute(faces[2], row_axes, near(rows)),
        lax.ppermute(faces[3], row_axes, far(rows)),
    ]
    field_vals = from_load + jnp.einsum(
        "wk,ik->wi", g, leaf_field_map[0, 0, :, :leaf], precision=lax.Precision.HIGH
    )
    (edge_trace,) = fused(trace_body, [(waves, leaf)], t, *seen)
    return (field_vals[:, None, None, :], edge_trace[:, None, None, :])


def solution(mesh):
    rows, cols = mesh.devices.shape
    bits = rows.bit_length() - 1
    row_axes = tuple(f"row{i}" for i in reversed(range(bits)))
    split = Mesh(mesh.devices.reshape((2,) * bits + (cols,)), row_axes + ("box",))
    late = P(None, row_axes, "box")
    early = P(row_axes, "box")
    return jax.shard_map(
        functools.partial(local, row_axes),
        mesh=split,
        in_specs=(late, early, early, early) + (late,) * 6 + (early,),
        out_specs=(late, late),
        check_vma=False,
    )
```

```python
import functools
import math

import jax
import jax.numpy as jnp
from jax import lax
from jax.experimental import pallas as pl
from jax.experimental.pallas import tpu as pltpu
from jax.sharding import Mesh, PartitionSpec as P

f32 = jnp.float32
LANES = 128
START_ROOM = 60 << 20


def dot(a, b, over=0):
    dims = (((1,), (over,)), ((), ()))

    def parts(x):
        high = x.astype(jnp.bfloat16)
        return high, (x - high.astype(f32)).astype(jnp.bfloat16)

    def product(x, y):
        return lax.dot_general(x, y, dims, preferred_element_type=f32)

    a_high, a_low = parts(a)
    b_high, b_low = parts(b)
    return product(a_high, b_high) + (product(a_high, b_low) + product(a_low, b_high))


def dot_t(a, b):
    return dot(a, b, 1)


def fused(body, outs, *args, scratch=(), aliases=None):
    vmem = pl.BlockSpec(memory_space=pltpu.VMEM)
    return pl.pallas_call(
        body,
        out_shape=[pltpu.VMEM(s, f32) for s in outs],
        in_specs=[vmem] * len(args),
        out_specs=[vmem] * len(outs),
        scratch_shapes=[pltpu.VMEM(s, f32) for s in scratch],
        input_output_aliases=aliases or {},
        compiler_params=pltpu.CompilerParams(vmem_limit_bytes=12 << 20),
    )(*args)


def packed(x, width):
    runs = LANES // width
    rows = x.shape[0] // runs
    return jnp.concatenate([x[i * rows : (i + 1) * rows] for i in range(runs)], axis=1)


def unpacked(x, width):
    return jnp.concatenate(
        [x[:, i * width : (i + 1) * width] for i in range(x.shape[1] // width)], axis=0
    )


def pad_lanes(x, lanes):
    if x.shape[1] == lanes:
        return x
    return jnp.concatenate([x, jnp.zeros((x.shape[0], lanes - x.shape[1]), f32)], axis=1)


def local(
    row_axes,
    load,
    leaf_load_map,
    leaf_out_map,
    leaf_field_map,
    x_solve,
    x_out,
    x_in,
    y_solve,
    y_out,
    y_in,
    reflect,
):
    edge = leaf_out_map.shape[-1] // 4
    cols = lax.axis_size("box")
    rows = 1
    for axis in row_axes:
        rows *= lax.axis_size(axis)
    x_levels = x_solve.shape[0]
    y_levels = y_solve.shape[0]
    waves = load.shape[0]
    leaf = 4 * edge
    pair = 2 * edge
    iface = cols * pair
    load_here = load[:, 0, 0, :]
    inner = load_here.shape[1]

    def my_column():
        return lax.axis_index("box")

    def my_row():
        return lax.axis_index(row_axes)

    def bit(value, level):
        return (value >> level) & 1

    def edge_of(x, number):
        return x[:, number * edge : (number + 1) * edge]

    def exchange_shape(level):
        kept = x_levels - 1 - level
        lanes = (2 + 2 * kept) * edge
        return (pair, -(-lanes // LANES) * LANES)

    def pieces_of(x, first, count):
        return [edge_of(x, first + i) for i in range(count)]

    whole_solve = y_levels == 2 and iface * iface <= 1 << 18
    in_lanes = -(-x_levels * edge // LANES) * LANES
    width = iface if whole_solve else 4 * in_lanes
    runs = width // in_lanes
    in_rows = pair // runs
    solve_rows = edge if whole_solve else 0

    def held_shape(count, first=True, second=True):
        first_rows = solve_rows + in_rows
        return (count, first_rows * first + solve_rows * second, width)

    def passed_on(held, bit_no):
        return lax.ppermute(held, "box", [(i, i ^ (1 << bit_no)) for i in range(cols)])

    steps = [x_levels - 1] + list(range(x_levels - 1))
    joined_at = [0] + list(range(2, x_levels))

    def held_of(c, held_ref, moved_ref):
        place = sum(bit(c, b) << k for k, b in enumerate(steps[:-1]))
        same = bit(my_column(), steps[-1]) == bit(c, steps[-1])
        return jnp.where(same, held_ref[place], moved_ref[place])

    def join(step, held_ref, moved_ref, *both_refs):
        high = bit(my_column(), steps[step]) == 1
        start = 0
        for both_ref in both_refs:
            rows = slice(start, start + both_ref.shape[1])
            start = rows.stop
            held, moved = held_ref[:, rows], moved_ref[:, rows]
            both_ref[: 1 << step] = jnp.where(high, moved, held)
            both_ref[1 << step :] = jnp.where(high, held, moved)

    def joined_shapes(step):
        if whole_solve and step == len(joined_at) - 1:
            return [held_shape(2 << step, True, False), held_shape(2 << step, False, True)]
        return [held_shape(2 << step)]

    def placing(body, shapes, *args, scratch=()):
        return pl.pallas_call(
            body,
            out_shape=[pltpu.VMEM(s, f32) for s in shapes],
            in_specs=[pl.BlockSpec(memory_space=pl.ANY)] * len(args),
            out_specs=[pl.BlockSpec(memory_space=pltpu.VMEM)] * len(shapes),
            scratch_shapes=[pltpu.VMEM(s, f32) for s in scratch]
            + [pltpu.SemaphoreType.DMA((len(args) + 1,))],
            compiler_params=pltpu.CompilerParams(
                vmem_limit_bytes=START_ROOM - sum(4 * math.prod(s) for s in shapes)
            ),
        )(*args)

    def hold_body(solve_any, xi_any, held_ref, solve, xi, sems):
        copies = [
            pltpu.make_async_copy(solve_any, solve, sems.at[0]),
            pltpu.make_async_copy(xi_any, xi, sems.at[1]),
        ]
        for copy in copies:
            copy.start()
        for copy in copies:
            copy.wait()
        odd_row = bit(my_row(), 0) == 1
        row_in = pad_lanes(
            jnp.concatenate(
                [
                    jnp.where(odd_row, edge_of(xi[k], 0), edge_of(xi[k], 2))
                    for k in range(x_levels)
                ],
                axis=1,
            ),
            in_lanes,
        )
        held_ref[0, solve_rows : solve_rows + in_rows] = jnp.concatenate(
            [row_in[i * in_rows : (i + 1) * in_rows] for i in range(runs)], axis=1
        )
        if whole_solve:
            for level, start in ((0, 0), (1, solve_rows + in_rows)):
                low, high = (
                    jnp.concatenate(
                        [edge_of(solve[level], 2 * c + side) for c in range(cols)], axis=1
                    )
                    for side in range(2)
                )
                mine = jnp.where(odd_row == (level == 0), high, low)
                held_ref[0, start : start + edge] = jnp.concatenate(
                    [mine[:edge], mine[edge:]], axis=1
                )

    ys_here, xi_here = y_solve[:, 0, 0], x_in[:, 0, 0]
    (held,) = placing(
        hold_body, [held_shape(1)], ys_here, xi_here, scratch=[ys_here.shape, xi_here.shape]
    )

    kept_from_start = [jnp.swapaxes(x_out, 3, 4), x_in, x_solve, y_solve, y_out, y_in]
    kept_from_start = [x[:, 0, 0] for x in kept_from_start] + [leaf_out_map[0, 0]]
    placed_shapes = [x.shape for x in kept_from_start] + [(inner, leaf), (inner, inner)]
    kept_from_start.append(leaf_field_map[0, 0])

    def start_body(load_any, map_any, *refs):
        *sources, field_any = refs[: len(kept_from_start)]
        sources += [field_any.at[:, pl.ds(0, leaf)], field_any.at[:, pl.ds(leaf, inner)]]
        h_ref, out_ref, load_out, *refs = refs[len(kept_from_start) :]
        targets, (load_v, map_v, sems) = refs[: len(sources)], refs[len(sources) :]
        pairs = [(load_any, load_v), (map_any, map_v)] + list(zip(sources, targets))
        copies = [pltpu.make_async_copy(a, b, sems.at[i]) for i, (a, b) in enumerate(pairs)]
        for copy in copies:
            copy.start()
        copies[0].wait()
        copies[1].wait()
        loaded = load_v[...].reshape(waves, inner)
        load_out[...] = loaded
        h = dot_t(loaded, map_v[...])
        h_ref[...] = h
        copies[2].wait()
        copies[3].wait()
        xo, xi = targets[:2]
        is_right = bit(my_column(), 0) == 1
        travelling = [
            jnp.where(is_right, edge_of(x[k], 1), edge_of(x[k], 3))
            for x in (xi, xo)
            for k in range(x_levels - 1)
        ]
        out_ref[...] = pad_lanes(
            jnp.concatenate([edge_of(h, 3), edge_of(h, 1)] + travelling, axis=1), out_ref.shape[1]
        )
        for copy in copies[4:]:
            copy.wait()

    h0, to_send, loaded, *placed = placing(
        start_body,
        [(waves, leaf), exchange_shape(0), (waves, inner)] + placed_shapes,
        load,
        leaf_load_map[0, 0],
        *kept_from_start,
        scratch=[load.shape, (leaf, inner)],
    )
    xo_all, xi_all, xs_all, ys_all, yo_all, yi_all, out_map, field_edges, field_inner = placed

    def product_body(a_ref, b_ref, out_ref):
        out_ref[...] = dot_t(a_ref[...], b_ref[...])

    (from_load,) = fused(product_body, [(waves, inner)], loaded, field_inner)

    def x_body(level, h_ref, own_ref, got_ref, solve_ref, xo_ref, *rest):
        kept = x_levels - 1 - level
        rest = list(rest)
        if level == 1:
            rest.pop(0)
        if level in joined_at:
            step = joined_at.index(level)
            both = [rest.pop() for _ in joined_shapes(step)]
            join(step, rest.pop(0), rest.pop(0), *reversed(both))
        h_out, w_out, *rest = rest
        is_right = bit(my_column(), level) == 1
        own, got = own_ref[...], got_ref[...]
        left_child = jnp.where(is_right, got, own)
        right_child = jnp.where(is_right, own, got)
        v = jnp.concatenate([edge_of(left_child, 1), edge_of(right_child, 0)], axis=1)
        w = dot_t(v, solve_ref[level])
        w_out[...] = w
        if kept:
            next_ref, ends_ref = rest
            outer = [edge_of(x, 2 + kept) for x in (left_child, right_child)]
            spread = dot(w, jnp.concatenate([xo_ref[level]] + outer, axis=1))
            h_out[...] = h_ref[...] + spread[:, :leaf]
            left = edge_of(left_child, 0) + edge_of(spread, 4)
            right = edge_of(right_child, 1) + edge_of(spread, 5)
            ends_ref[...] = jnp.concatenate(
                [edge_of(left_child, 2), edge_of(right_child, 2)], axis=1
            )
            mine = jnp.where(bit(my_column(), level + 1) == 1, right_child, left_child)
            travelling = pieces_of(mine, 3, kept - 1) + pieces_of(mine, 3 + kept, kept - 1)
            next_ref[...] = pad_lanes(
                jnp.concatenate([left, right] + travelling, axis=1), next_ref.shape[1]
            )
        else:
            h_out[...] = h_ref[...] + dot(w, xo_ref[level])

    h = h0
    x_keep, ends = [], []
    moved = passed_on(held, steps[0])
    for level in range(x_levels):
        got = lax.ppermute(to_send, "box", [(i, i ^ (1 << level)) for i in range(cols)])
        outs = [(waves, leaf), (waves, pair)]
        args = [h, to_send, got, xs_all, xo_all]
        if level < x_levels - 1:
            outs += [exchange_shape(level + 1), (pair, pair)]
        if level == 1:
            args.append(from_load)
        if level in joined_at:
            step = joined_at.index(level)
            outs += joined_shapes(step)
            args += [held, moved]
        h, w, *rest = fused(functools.partial(x_body, level), outs, *args)
        x_keep.append(w)
        if level in joined_at:
            second = rest.pop() if len(joined_shapes(step)) == 2 else None
            held = rest.pop()
            moved = passed_on(held, steps[step + 1])
        if rest:
            to_send, end = rest
            ends.append(end)

    def group(level):
        return tuple(row_axes[y_levels - 1 - level :]) + ("box",)

    def span(level):
        return 2 << level

    def swap(x, level):
        return lax.all_to_all(x, group(level), 0, 0, tiled=True)

    def offer_shape(level):
        if whole_solve:
            return ((1 + level) * cols, waves * edge // LANES, LANES)
        return (span(level) * cols, waves // span(level) * edge // LANES, LANES)

    def store_offer(level, h, out):
        size = span(level)
        share = waves // size
        facing = jnp.where(
            lax.rem(my_row(), size) == size // 2 - 1, edge_of(h, 2), edge_of(h, 0)
        )
        if whole_solve:
            out[...] = jnp.broadcast_to(packed(facing, edge), out.shape)
            return
        for target in range(size):
            piece = packed(facing[target * share : (target + 1) * share], edge)
            out[target * cols : (target + 1) * cols] = jnp.broadcast_to(piece, (cols,) + piece.shape)

    def offer_body(level, h_ref, out_ref):
        store_offer(level, h_ref[...], out_ref)

    def gather_v(level, got_ref, v_ref):
        size = span(level)
        low = (size // 2 - 1) * cols
        run = got_ref.shape[1]
        for side in range(2):
            for c in range(cols):
                piece = got_ref[low + side * cols + c]
                for k in range(LANES // edge):
                    start = c * pair + side * edge
                    v_ref[k * run : (k + 1) * run, start : start + edge] = edge_of(piece, k)

    def solve_body(level, got_ref, solve_ref, out_ref, v_ref):
        gather_v(level, got_ref, v_ref)
        w = packed(dot_t(v_ref[...], solve_ref[level]), pair)
        out_ref[...] = jnp.broadcast_to(w, out_ref.shape)

    def own_columns(w_all):
        own = w_all[:, :pair]
        for c in range(1, cols):
            own = jnp.where(my_column() == c, w_all[:, c * pair : (c + 1) * pair], own)
        return own

    def gather_w(level, got_ref, w_ref):
        size = span(level)
        share = waves // size
        run = got_ref.shape[1]
        for target in range(size):
            for c in range(cols):
                piece = got_ref[target * cols + c]
                for k in range(LANES // pair):
                    start = target * share + k * run
                    w_ref[start : start + run, c * pair : (c + 1) * pair] = piece[
                        :, k * pair : (k + 1) * pair
                    ]
        return w_ref[...]

    def half_body(level, got_ref, held_ref, moved_ref, *refs):
        out_ref, v_ref = (refs[1], refs[3]) if level == 0 else refs
        odd_row = bit(my_row(), 0) == 1
        run = got_ref.shape[1]
        for c in range(cols):
            piece = got_ref[c] if level == 0 else jnp.where(odd_row, got_ref[c], got_ref[cols + c])
            for k in range(LANES // edge):
                v_ref[k * run : (k + 1) * run, c * edge : (c + 1) * edge] = edge_of(piece, k)
        solve = []
        for c in range(cols):
            block = held_of(c, held_ref, moved_ref)[:edge]
            solve += [block[:, : iface // 2], block[:, iface // 2 :]]
        out_ref[...] = dot_t(v_ref[...], jnp.concatenate(solve, axis=0))

    def whole_body(h_ref, mine_ref, other_ref, yo_ref, h_out, w_out, next_ref):
        w_all = mine_ref[...] + other_ref[...]
        w_out[...] = own_columns(w_all)
        h = h_ref[...] + dot_t(w_all, yo_ref[0])
        h_out[...] = h
        store_offer(1, h, next_ref)

    def spread_body(level, h_ref, got_ref, yo_ref, h_out, w_out, next_ref, w_ref):
        w_all = gather_w(level, got_ref, w_ref)
        w_out[...] = own_columns(w_all)
        h = h_ref[...] + dot_t(w_all, yo_ref[level])
        h_out[...] = h
        store_offer(level + 1, h, next_ref)

    def halves(level):
        return span(level) // 2

    def terms_shape(level):
        return (span(level) * cols, waves // halves(level) * edge // LANES, LANES)

    def store_terms(level, g, yi_ref, out):
        terms = dot_t(g, yi_ref[level])
        half = halves(level)
        share = waves // half
        for side in range(2):
            for c in range(cols):
                start = c * pair + side * edge
                piece = terms[:, start : start + edge]
                for part in range(half):
                    out[(side * half + part) * cols + c] = packed(
                        piece[part * share : (part + 1) * share], edge
                    )

    def turn_body(level, h_ref, got_ref, *refs):
        if whole_solve:
            other_ref, yo_ref, yi_ref, reflect_ref, w_out, g_out, out_ref = refs
            w_all = got_ref[...] + other_ref[...]
        else:
            yo_ref, yi_ref, reflect_ref, w_out, g_out, out_ref, w_ref = refs
            w_all = gather_w(level, got_ref, w_ref)
        w_out[...] = own_columns(w_all)
        h = h_ref[...] + dot_t(w_all, yo_ref[level])
        lane = lax.broadcasted_iota(jnp.int32, (1, leaf), 1)

        def side(number):
            return (lane >= number * edge) & (lane < (number + 1) * edge)

        outer = (
            side(0) & (my_row() == 0)
            | side(1) & (my_column() == cols - 1)
            | side(2) & (my_row() == rows - 1)
            | side(3) & (my_column() == 0)
        )
        g = jnp.where(outer, h * reflect_ref[...], 0.0)
        g_out[...] = g
        store_terms(level, g, yi_ref, out_ref)

    def sum_body(got_ref, out_ref):
        out_ref[...] = jnp.sum(got_ref[...], axis=0)

    def with_row_edge(level, g, w, q):
        size = span(level)
        place = lax.rem(my_row(), size)
        is_low = place == size // 2 - 1
        is_high = place == size // 2
        value = jnp.where(place < size // 2, w[:, :edge], w[:, edge:]) + q
        bottom = jnp.where(is_high, value, edge_of(g, 0))
        top = jnp.where(is_low, value, edge_of(g, 2))
        return jnp.concatenate([bottom, edge_of(g, 1), top, edge_of(g, 3)], axis=1)

    def row_down_body(level, g_ref, w_ref, sum_ref, yi_ref, g_out, out_ref):
        g = with_row_edge(level, g_ref[...], w_ref[...], unpacked_parts(level, sum_ref))
        g_out[...] = g
        store_terms(level - 1, g, yi_ref, out_ref)

    def unpacked_parts(level, sum_ref):
        run = waves // halves(level) * edge // LANES
        return jnp.concatenate(
            [unpacked(sum_ref[i * run : (i + 1) * run], edge) for i in range(halves(level))], axis=0
        )

    def collect(total, level):
        for axis_no in range(level):
            axis = row_axes[y_levels - 1 - axis_no]
            other = lax.ppermute(total, axis, [(0, 1), (1, 0)])
            first = lax.axis_index(axis) == 0
            total = jnp.concatenate(
                [jnp.where(first, total, other), jnp.where(first, other, total)], axis=0
            )
        return total

    x_lanes = -(-(x_levels + 1) * edge // LANES) * LANES

    def split_body(g_ref, w_ref, sum_ref, yi_ref, g_out, own_out, other_out):
        g = with_row_edge(1, g_ref[...], w_ref[...], unpacked_parts(1, sum_ref))
        g_out[...] = g
        terms = dot_t(g, yi_ref[0])
        odd_row = bit(my_row(), 0) == 1
        low, high = (
            jnp.concatenate(
                [terms[:, c * pair + side * edge :][:, :edge] for c in range(cols)], axis=1
            )
            for side in range(2)
        )
        own_out[...] = jnp.where(odd_row, high, low)
        other_out[...] = jnp.where(odd_row, low, high)

    node_starts = []
    for k in range(x_levels):
        node_starts.append(sum(cols >> (i + 1) for i in range(k)) * pair)
    node_lanes = (cols - 1) * pair

    def prepare_body(g_ref, w_ref, xi_ref, held_ref, moved_ref, matrix_out, known_out):
        g = with_row_edge(0, g_ref[...], w_ref[...], 0.0)
        row = []
        for c in range(cols):
            held = held_of(c, held_ref, moved_ref)[solve_rows : solve_rows + in_rows]
            row.append(
                jnp.concatenate(
                    [held[:, i * in_lanes : (i + 1) * in_lanes] for i in range(runs)], axis=0
                )
            )
        matrix_out[...] = jnp.zeros_like(matrix_out)
        for k in range(x_levels):
            known = dot_t(g, xi_ref[k])
            for node in range(cols >> (k + 1)):
                start = node_starts[k] + node * pair
                inside = my_column() >> (k + 1) == node
                known_out[:, start : start + pair] = jnp.where(inside, known, 0.0)
                for c in range(node << (k + 1), (node + 1) << (k + 1)):
                    matrix_out[start : start + pair, c * edge : (c + 1) * edge] = edge_of(row[c], k)

    def x_terms_body(own_ref, got_ref, matrix_ref, known_ref, out_ref):
        q = own_ref[...] + got_ref[...]
        terms = dot_t(q, matrix_ref[...]) + known_ref[...]
        for c in range(cols):
            picked = []
            for k in range(x_levels):
                start = node_starts[k] + (c >> (k + 1)) * pair + bit(c, k) * edge
                picked.append(terms[:, start : start + edge])
            out_ref[c] = pad_lanes(jnp.concatenate(picked + [edge_of(q, c)], axis=1), x_lanes)

    def finish_body(g_ref, w_ref, h0_ref, got_ref, lo_ref, *refs):
        keep_ref, ends_ref = refs[:x_levels], refs[x_levels : 2 * x_levels - 1]
        g_out, t_out, *faces = refs[2 * x_levels - 1 :]
        q = jnp.sum(got_ref[...], axis=0)
        g = with_row_edge(0, g_ref[...], w_ref[...], edge_of(q, x_levels))
        gl = jnp.zeros((waves, edge), f32)
        gr = gl
        for level in reversed(range(x_levels)):
            is_right = bit(my_column(), level) == 1
            keep = keep_ref[level][...]
            value = edge_of(q, level) + jnp.where(is_right, keep[:, edge:], keep[:, :edge])
            if level < x_levels - 1:
                end = ends_ref[level][...]
                end = jnp.where(is_right, end[edge:], end[:edge])
                value = value + dot_t(jnp.concatenate([gl, gr], axis=1), end)
            gl = jnp.where(is_right, value, gl)
            gr = jnp.where(is_right, gr, value)
        g = jnp.concatenate(
            [edge_of(g, 0), edge_of(g, 1) + gr, edge_of(g, 2), edge_of(g, 3) + gl], axis=1
        )
        g_out[...] = g
        t = g - (dot_t(g, lo_ref[...]) + h0_ref[...])
        t_out[...] = t
        odd_col = bit(my_column(), 0) == 1
        odd_row = bit(my_row(), 0) == 1
        bottom, right, top, left = (packed(edge_of(t, i), edge) for i in range(4))
        faces[0][...] = jnp.where(odd_col, left, right)
        faces[1][...] = jnp.where(odd_col, right, left)
        faces[2][...] = jnp.where(odd_row, bottom, top)
        faces[3][...] = jnp.where(odd_row, top, bottom)

    def trace_body(t_ref, a_ref, b_ref, c_ref, d_ref, out_ref):
        t = t_ref[...]
        odd_col = bit(my_column(), 0) == 1
        odd_row = bit(my_row(), 0) == 1
        near_x, far_x, near_y, far_y = (
            unpacked(ref[...], edge) for ref in (a_ref, b_ref, c_ref, d_ref)
        )
        east = jnp.where(odd_col, far_x, near_x)
        west = jnp.where(odd_col, near_x, far_x)
        north = jnp.where(odd_row, far_y, near_y)
        south = jnp.where(odd_row, near_y, far_y)

        def mean(shared, own, other):
            return jnp.where(shared, 0.5 * (own + other), own)

        trace = jnp.concatenate(
            [
                mean(my_row() > 0, edge_of(t, 0), south),
                mean(my_column() < cols - 1, edge_of(t, 1), east),
                mean(my_row() < rows - 1, edge_of(t, 2), north),
                mean(my_column() > 0, edge_of(t, 3), west),
            ],
            axis=1,
        )
        out_ref[...] = trace.reshape(out_ref.shape)

    (offer,) = fused(functools.partial(offer_body, 0), [offer_shape(0)], h)
    y_keep = []
    for level in range(y_levels):
        if whole_solve:
            got = lax.all_to_all(offer, ("box",) if level == 0 else (row_axes[0], "box"), 0, 0, tiled=True)
            pass_on = [second] if level == 0 else []
            mine, *pass_on = fused(
                functools.partial(half_body, level),
                [(waves, iface)] + [x.shape for x in pass_on],
                got,
                *((held, moved) if level == 0 else (second, second_moved)),
                *pass_on,
                scratch=[(waves, cols * edge)],
                aliases={3: 1} if level == 0 else None,
            )
            if level == 0:
                second = pass_on[0]
                second_moved = passed_on(second, steps[-1])
            other = lax.ppermute(mine, row_axes[-1], [(0, 1), (1, 0)])
            if level == 0:
                h, w, offer = fused(
                    whole_body,
                    [(waves, leaf), (waves, pair), offer_shape(1)],
                    h,
                    mine,
                    other,
                    yo_all,
                )
            else:
                w, g, terms = fused(
                    functools.partial(turn_body, level),
                    [(waves, pair), (waves, leaf), terms_shape(level)],
                    h,
                    mine,
                    other,
                    yo_all,
                    yi_all,
                    reflect[0],
                )
            y_keep.append(w)
            continue
        share = waves // span(level)
        (w_offer,) = fused(
            functools.partial(solve_body, level),
            [(span(level) * cols, share * pair // LANES, LANES)],
            swap(offer, level),
            ys_all,
            scratch=[(share, iface)],
        )
        got = swap(w_offer, level)
        if level < y_levels - 1:
            h, w, offer = fused(
                functools.partial(spread_body, level),
                [(waves, leaf), (waves, pair), offer_shape(level + 1)],
                h,
                got,
                yo_all,
                scratch=[(waves, iface)],
            )
        else:
            w, g, terms = fused(
                functools.partial(turn_body, level),
                [(waves, pair), (waves, leaf), terms_shape(level)],
                h,
                got,
                yo_all,
                yi_all,
                reflect[0],
                scratch=[(waves, iface)],
            )
        y_keep.append(w)
    for level in reversed(range(1, y_levels)):
        (total,) = fused(sum_body, [terms_shape(level)[1:]], swap(terms, level))
        total = collect(total, level)
        if level > 1:
            g, terms = fused(
                functools.partial(row_down_body, level),
                [(waves, leaf), terms_shape(level - 1)],
                g,
                y_keep[level],
                total,
                yi_all,
            )
    share = (waves, iface // 2)
    g, own, other = fused(
        split_body, [(waves, leaf), share, share], g, y_keep[1], total, yi_all
    )
    got = lax.ppermute(other, row_axes[-1], [(0, 1), (1, 0)])
    matrix, known = fused(
        prepare_body,
        [(node_lanes, cols * edge), (waves, node_lanes)],
        g,
        y_keep[0],
        xi_all,
        held,
        moved,
    )
    (terms,) = fused(x_terms_body, [(cols, waves, x_lanes)], own, got, matrix, known)
    got = lax.all_to_all(terms, "box", 0, 0, tiled=True)
    face = (waves * edge // LANES, LANES)
    g, t, *faces = fused(
        finish_body,
        [(waves, leaf), (waves, leaf)] + [face] * 4,
        g,
        y_keep[0],
        h0,
        got,
        out_map,
        *x_keep,
        *ends,
    )

    def near(count):
        return [(i, i ^ 1) for i in range(count)]

    def far(count):
        one_way = [(i, i + 1) for i in range(1, count - 1, 2)]
        return one_way + [(j, i) for i, j in one_way]

    seen = [
        lax.ppermute(faces[0], "box", near(cols)),
        lax.ppermute(faces[1], "box", far(cols)),
        lax.ppermute(faces[2], row_axes, near(rows)),
        lax.ppermute(faces[3], row_axes, far(rows)),
    ]
    def field_body(g_ref, map_ref, from_load_ref, out_ref):
        field = from_load_ref[...] + dot_t(g_ref[...], map_ref[...])
        out_ref[...] = field.reshape(out_ref.shape)

    (field_vals,) = fused(
        field_body, [(waves, 1, 1, inner)], g, field_edges, from_load
    )
    (edge_trace,) = fused(trace_body, [(waves, 1, 1, leaf)], t, *seen)
    return field_vals, edge_trace


def solution(mesh):
    rows, cols = mesh.devices.shape
    bits = rows.bit_length() - 1
    row_axes = tuple(f"row{i}" for i in reversed(range(bits)))
    split = Mesh(mesh.devices.reshape((2,) * bits + (cols,)), row_axes + ("box",))
    late = P(None, row_axes, "box")
    early = P(row_axes, "box")
    return jax.shard_map(
        functools.partial(local, row_axes),
        mesh=split,
        in_specs=(late, early, early, early) + (late,) * 6 + (early,),
        out_specs=(late, late),
        check_vma=False,
    )
```

```python
import functools
import math

import jax
import jax.numpy as jnp
from jax import lax
from jax.experimental import pallas as pl
from jax.experimental.pallas import tpu as pltpu
from jax.sharding import Mesh, PartitionSpec as P

f32 = jnp.float32
LANES = 128
START_ROOM = 60 << 20


def dot(a, b, over=0):
    dims = (((1,), (over,)), ((), ()))

    def parts(x):
        high = x.astype(jnp.bfloat16)
        return high, (x - high.astype(f32)).astype(jnp.bfloat16)

    def product(x, y):
        return lax.dot_general(x, y, dims, preferred_element_type=f32)

    a_high, a_low = parts(a)
    b_high, b_low = parts(b)
    return product(a_high, b_high) + (product(a_high, b_low) + product(a_low, b_high))


def dot_t(a, b):
    return dot(a, b, 1)


def fused(body, outs, *args, scratch=(), aliases=None):
    vmem = pl.BlockSpec(memory_space=pltpu.VMEM)
    return pl.pallas_call(
        body,
        out_shape=[pltpu.VMEM(s, f32) for s in outs],
        in_specs=[vmem] * len(args),
        out_specs=[vmem] * len(outs),
        scratch_shapes=[pltpu.VMEM(s, f32) for s in scratch],
        input_output_aliases=aliases or {},
        compiler_params=pltpu.CompilerParams(vmem_limit_bytes=12 << 20),
    )(*args)


def packed(x, width):
    runs = LANES // width
    rows = x.shape[0] // runs
    return jnp.concatenate([x[i * rows : (i + 1) * rows] for i in range(runs)], axis=1)


def unpacked(x, width):
    return jnp.concatenate(
        [x[:, i * width : (i + 1) * width] for i in range(x.shape[1] // width)], axis=0
    )


def pad_lanes(x, lanes):
    if x.shape[1] == lanes:
        return x
    return jnp.concatenate([x, jnp.zeros((x.shape[0], lanes - x.shape[1]), f32)], axis=1)


def local(
    row_axes,
    load,
    leaf_load_map,
    leaf_out_map,
    leaf_field_map,
    x_solve,
    x_out,
    x_in,
    y_solve,
    y_out,
    y_in,
    reflect,
):
    edge = leaf_out_map.shape[-1] // 4
    cols = lax.axis_size("box")
    rows = 1
    for axis in row_axes:
        rows *= lax.axis_size(axis)
    x_levels = x_solve.shape[0]
    y_levels = y_solve.shape[0]
    waves = load.shape[0]
    leaf = 4 * edge
    pair = 2 * edge
    iface = cols * pair
    load_here = load[:, 0, 0, :]
    inner = load_here.shape[1]

    def my_column():
        return lax.axis_index("box")

    def my_row():
        return lax.axis_index(row_axes)

    def bit(value, level):
        return (value >> level) & 1

    def edge_of(x, number):
        return x[:, number * edge : (number + 1) * edge]

    def exchange_shape(level):
        kept = x_levels - 1 - level
        lanes = (2 + 2 * kept) * edge
        return (pair, -(-lanes // LANES) * LANES)

    def pieces_of(x, first, count):
        return [edge_of(x, first + i) for i in range(count)]

    whole_solve = y_levels == 2 and iface * iface <= 1 << 18
    in_lanes = -(-x_levels * edge // LANES) * LANES
    width = iface if whole_solve else 4 * in_lanes
    runs = width // in_lanes
    in_rows = pair // runs
    solve_rows = edge if whole_solve else 0

    def held_shape(count, first=True, second=True):
        return (count, solve_rows * first + (solve_rows + in_rows) * second, width)

    def passed_on(held, bit_no):
        return lax.ppermute(held, "box", [(i, i ^ (1 << bit_no)) for i in range(cols)])

    steps = [x_levels - 1] + list(range(x_levels - 1))
    joined_at = [0] + list(range(2, x_levels))

    def held_of(c, held_ref, moved_ref):
        place = sum(bit(c, b) << k for k, b in enumerate(steps[:-1]))
        same = bit(my_column(), steps[-1]) == bit(c, steps[-1])
        return jnp.where(same, held_ref[place], moved_ref[place])

    def join(step, held_ref, moved_ref, *both_refs):
        high = bit(my_column(), steps[step]) == 1
        start = 0
        for both_ref in both_refs:
            rows = slice(start, start + both_ref.shape[1])
            start = rows.stop
            held, moved = held_ref[:, rows], moved_ref[:, rows]
            both_ref[: 1 << step] = jnp.where(high, moved, held)
            both_ref[1 << step :] = jnp.where(high, held, moved)

    def joined_shapes(step):
        if whole_solve and step == len(joined_at) - 1:
            return [held_shape(2 << step, True, False), held_shape(2 << step, False, True)]
        return [held_shape(2 << step)]

    def placing(body, shapes, *args, scratch=()):
        return pl.pallas_call(
            body,
            out_shape=[pltpu.VMEM(s, f32) for s in shapes],
            in_specs=[pl.BlockSpec(memory_space=pl.ANY)] * len(args),
            out_specs=[pl.BlockSpec(memory_space=pltpu.VMEM)] * len(shapes),
            scratch_shapes=[pltpu.VMEM(s, f32) for s in scratch]
            + [pltpu.SemaphoreType.DMA((len(args) + 1,))],
            compiler_params=pltpu.CompilerParams(
                vmem_limit_bytes=START_ROOM - sum(4 * math.prod(s) for s in shapes)
            ),
        )(*args)

    def hold_body(solve_any, xi_any, held_ref, solve, xi, sems):
        copies = [
            pltpu.make_async_copy(solve_any, solve, sems.at[0]),
            pltpu.make_async_copy(xi_any, xi, sems.at[1]),
        ]
        for copy in copies:
            copy.start()
        for copy in copies:
            copy.wait()
        odd_row = bit(my_row(), 0) == 1
        row_in = pad_lanes(
            jnp.concatenate(
                [
                    jnp.where(odd_row, edge_of(xi[k], 0), edge_of(xi[k], 2))
                    for k in range(x_levels)
                ],
                axis=1,
            ),
            in_lanes,
        )
        held_ref[0, solve_rows : solve_rows + in_rows] = jnp.concatenate(
            [row_in[i * in_rows : (i + 1) * in_rows] for i in range(runs)], axis=1
        )
        if whole_solve:
            for level, start in ((0, 0), (1, solve_rows + in_rows)):
                low, high = (
                    jnp.concatenate(
                        [edge_of(solve[level], 2 * c + side) for c in range(cols)], axis=1
                    )
                    for side in range(2)
                )
                mine = jnp.where(odd_row == (level == 0), high, low)
                held_ref[0, start : start + edge] = jnp.concatenate(
                    [mine[:edge], mine[edge:]], axis=1
                )

    ys_here, xi_here = y_solve[:, 0, 0], x_in[:, 0, 0]
    (held,) = placing(
        hold_body, [held_shape(1)], ys_here, xi_here, scratch=[ys_here.shape, xi_here.shape]
    )

    kept_from_start = [jnp.swapaxes(x_out, 3, 4), x_in, x_solve, y_solve, y_out, y_in]
    kept_from_start = [x[:, 0, 0] for x in kept_from_start] + [leaf_out_map[0, 0]]
    placed_shapes = [x.shape for x in kept_from_start] + [(inner, leaf), (inner, inner)]
    kept_from_start.append(leaf_field_map[0, 0])

    def start_body(load_any, map_any, *refs):
        *sources, field_any = refs[: len(kept_from_start)]
        sources += [field_any.at[:, pl.ds(0, leaf)], field_any.at[:, pl.ds(leaf, inner)]]
        h_ref, out_ref, load_out, *refs = refs[len(kept_from_start) :]
        targets, (load_v, map_v, sems) = refs[: len(sources)], refs[len(sources) :]
        pairs = [(load_any, load_v), (map_any, map_v)] + list(zip(sources, targets))
        copies = [pltpu.make_async_copy(a, b, sems.at[i]) for i, (a, b) in enumerate(pairs)]
        for copy in copies:
            copy.start()
        copies[0].wait()
        copies[1].wait()
        loaded = load_v[...].reshape(waves, inner)
        load_out[...] = loaded
        h = dot_t(loaded, map_v[...])
        h_ref[...] = h
        copies[2].wait()
        copies[3].wait()
        xo, xi = targets[:2]
        is_right = bit(my_column(), 0) == 1
        travelling = [
            jnp.where(is_right, edge_of(x[k], 1), edge_of(x[k], 3))
            for x in (xi, xo)
            for k in range(x_levels - 1)
        ]
        out_ref[...] = pad_lanes(
            jnp.concatenate([edge_of(h, 3), edge_of(h, 1)] + travelling, axis=1), out_ref.shape[1]
        )
        for copy in copies[4:]:
            copy.wait()

    h0, to_send, loaded, *placed = placing(
        start_body,
        [(waves, leaf), exchange_shape(0), (waves, inner)] + placed_shapes,
        load,
        leaf_load_map[0, 0],
        *kept_from_start,
        scratch=[load.shape, (leaf, inner)],
    )
    xo_all, xi_all, xs_all, ys_all, yo_all, yi_all, out_map, field_edges, field_inner = placed

    def aside_body(load_ref, map_ref, yi_ref, out_ref, columns_ref):
        out_ref[...] = dot_t(load_ref[...], map_ref[...])
        columns_ref[...] = packed(
            jnp.where(my_row() == 1, edge_of(yi_ref[0], 2), edge_of(yi_ref[0], 0)), edge
        )

    from_load, columns = fused(
        aside_body,
        [(waves, inner), (iface * edge // LANES, LANES)],
        loaded,
        field_inner,
        yi_all,
    )

    def x_body(level, h_ref, own_ref, got_ref, solve_ref, xo_ref, *rest):
        kept = x_levels - 1 - level
        rest = list(rest)
        if level == 1:
            rest.pop(0)
        if level in joined_at:
            step = joined_at.index(level)
            both = [rest.pop() for _ in joined_shapes(step)]
            join(step, rest.pop(0), rest.pop(0), *reversed(both))
        h_out, w_out, *rest = rest
        is_right = bit(my_column(), level) == 1
        own, got = own_ref[...], got_ref[...]
        left_child = jnp.where(is_right, got, own)
        right_child = jnp.where(is_right, own, got)
        v = jnp.concatenate([edge_of(left_child, 1), edge_of(right_child, 0)], axis=1)
        w = dot_t(v, solve_ref[level])
        w_out[...] = w
        if kept:
            next_ref, ends_ref = rest
            outer = [edge_of(x, 2 + kept) for x in (left_child, right_child)]
            spread = dot(w, jnp.concatenate([xo_ref[level]] + outer, axis=1))
            h_out[...] = h_ref[...] + spread[:, :leaf]
            left = edge_of(left_child, 0) + edge_of(spread, 4)
            right = edge_of(right_child, 1) + edge_of(spread, 5)
            ends_ref[...] = jnp.concatenate(
                [edge_of(left_child, 2), edge_of(right_child, 2)], axis=1
            )
            mine = jnp.where(bit(my_column(), level + 1) == 1, right_child, left_child)
            travelling = pieces_of(mine, 3, kept - 1) + pieces_of(mine, 3 + kept, kept - 1)
            next_ref[...] = pad_lanes(
                jnp.concatenate([left, right] + travelling, axis=1), next_ref.shape[1]
            )
        else:
            h_out[...] = h_ref[...] + dot(w, xo_ref[level])

    h = h0
    x_keep, ends = [], []
    moved = passed_on(held, steps[0])
    for level in range(x_levels):
        got = lax.ppermute(to_send, "box", [(i, i ^ (1 << level)) for i in range(cols)])
        outs = [(waves, leaf), (waves, pair)]
        args = [h, to_send, got, xs_all, xo_all]
        if level < x_levels - 1:
            outs += [exchange_shape(level + 1), (pair, pair)]
        if level == 1:
            args.append(from_load)
        if level in joined_at:
            step = joined_at.index(level)
            outs += joined_shapes(step)
            args += [held, moved]
        h, w, *rest = fused(functools.partial(x_body, level), outs, *args)
        x_keep.append(w)
        if level in joined_at:
            second = rest.pop() if len(joined_shapes(step)) == 2 else None
            held = rest.pop()
            moved = passed_on(held, steps[step + 1])
        if rest:
            to_send, end = rest
            ends.append(end)

    def group(level):
        return tuple(row_axes[y_levels - 1 - level :]) + ("box",)

    def span(level):
        return 2 << level

    def swap(x, level):
        return lax.all_to_all(x, group(level), 0, 0, tiled=True)

    def offer_shape(level):
        if whole_solve:
            return ((1 + level) * cols, waves * edge // LANES, LANES)
        return (span(level) * cols, waves // span(level) * edge // LANES, LANES)

    def store_offer(level, h, out):
        size = span(level)
        share = waves // size
        facing = jnp.where(
            lax.rem(my_row(), size) == size // 2 - 1, edge_of(h, 2), edge_of(h, 0)
        )
        if whole_solve:
            out[...] = jnp.broadcast_to(packed(facing, edge), out.shape)
            return
        for target in range(size):
            piece = packed(facing[target * share : (target + 1) * share], edge)
            out[target * cols : (target + 1) * cols] = jnp.broadcast_to(piece, (cols,) + piece.shape)

    def offer_body(level, h_ref, out_ref):
        store_offer(level, h_ref[...], out_ref)

    def gather_v(level, got_ref, v_ref):
        size = span(level)
        low = (size // 2 - 1) * cols
        run = got_ref.shape[1]
        for side in range(2):
            for c in range(cols):
                piece = got_ref[low + side * cols + c]
                for k in range(LANES // edge):
                    start = c * pair + side * edge
                    v_ref[k * run : (k + 1) * run, start : start + edge] = edge_of(piece, k)

    def solve_body(level, got_ref, solve_ref, out_ref, v_ref):
        gather_v(level, got_ref, v_ref)
        w = packed(dot_t(v_ref[...], solve_ref[level]), pair)
        out_ref[...] = jnp.broadcast_to(w, out_ref.shape)

    def own_columns(w_all):
        own = w_all[:, :pair]
        for c in range(1, cols):
            own = jnp.where(my_column() == c, w_all[:, c * pair : (c + 1) * pair], own)
        return own

    def gather_w(level, got_ref, w_ref):
        size = span(level)
        share = waves // size
        run = got_ref.shape[1]
        for target in range(size):
            for c in range(cols):
                piece = got_ref[target * cols + c]
                for k in range(LANES // pair):
                    start = target * share + k * run
                    w_ref[start : start + run, c * pair : (c + 1) * pair] = piece[
                        :, k * pair : (k + 1) * pair
                    ]
        return w_ref[...]

    def half_body(level, got_ref, held_ref, moved_ref, *refs):
        out_ref, v_ref = (refs[2], refs[5]) if level == 0 else refs
        odd_row = bit(my_row(), 0) == 1
        run = got_ref.shape[1]
        for c in range(cols):
            piece = got_ref[c] if level == 0 else jnp.where(odd_row, got_ref[c], got_ref[cols + c])
            for k in range(LANES // edge):
                v_ref[k * run : (k + 1) * run, c * edge : (c + 1) * edge] = edge_of(piece, k)
        solve = []
        for c in range(cols):
            start = in_rows * level
            block = held_of(c, held_ref, moved_ref)[start : start + edge]
            solve += [block[:, : iface // 2], block[:, iface // 2 :]]
        out_ref[...] = dot_t(v_ref[...], jnp.concatenate(solve, axis=0))

    def whole_body(h_ref, mine_ref, other_ref, yo_ref, early_ref, h_out, w_out, next_ref):
        w_all = mine_ref[...] + other_ref[...]
        w_out[...] = own_columns(w_all)
        h = h_ref[...] + dot_t(w_all, yo_ref[0])
        h_out[...] = h
        store_offer(1, h, next_ref)

    def spread_body(level, h_ref, got_ref, yo_ref, h_out, w_out, next_ref, w_ref):
        w_all = gather_w(level, got_ref, w_ref)
        w_out[...] = own_columns(w_all)
        h = h_ref[...] + dot_t(w_all, yo_ref[level])
        h_out[...] = h
        store_offer(level + 1, h, next_ref)

    def halves(level):
        return span(level) // 2

    def terms_shape(level):
        return (span(level) * cols, waves // halves(level) * edge // LANES, LANES)

    def store_terms(level, g, yi_ref, out):
        terms = dot_t(g, yi_ref[level])
        half = halves(level)
        share = waves // half
        for side in range(2):
            for c in range(cols):
                start = c * pair + side * edge
                piece = terms[:, start : start + edge]
                for part in range(half):
                    out[(side * half + part) * cols + c] = packed(
                        piece[part * share : (part + 1) * share], edge
                    )

    def turn_body(level, h_ref, got_ref, *refs):
        if whole_solve:
            other_ref, yo_ref, yi_ref, reflect_ref, w_out, g_out, out_ref = refs
            w_all = got_ref[...] + other_ref[...]
        else:
            yo_ref, yi_ref, reflect_ref, w_out, g_out, out_ref, w_ref = refs
            w_all = gather_w(level, got_ref, w_ref)
        w_out[...] = own_columns(w_all)
        h = h_ref[...] + dot_t(w_all, yo_ref[level])
        lane = lax.broadcasted_iota(jnp.int32, (1, leaf), 1)

        def side(number):
            return (lane >= number * edge) & (lane < (number + 1) * edge)

        outer = (
            side(0) & (my_row() == 0)
            | side(1) & (my_column() == cols - 1)
            | side(2) & (my_row() == rows - 1)
            | side(3) & (my_column() == 0)
        )
        g = jnp.where(outer, h * reflect_ref[...], 0.0)
        g_out[...] = g
        store_terms(level, g, yi_ref, out_ref)

    def sum_body(got_ref, out_ref):
        out_ref[...] = jnp.sum(got_ref[...], axis=0)

    def with_row_edge(level, g, w, q):
        size = span(level)
        place = lax.rem(my_row(), size)
        is_low = place == size // 2 - 1
        is_high = place == size // 2
        value = jnp.where(place < size // 2, w[:, :edge], w[:, edge:]) + q
        bottom = jnp.where(is_high, value, edge_of(g, 0))
        top = jnp.where(is_low, value, edge_of(g, 2))
        return jnp.concatenate([bottom, edge_of(g, 1), top, edge_of(g, 3)], axis=1)

    def row_down_body(level, g_ref, w_ref, sum_ref, yi_ref, g_out, out_ref):
        g = with_row_edge(level, g_ref[...], w_ref[...], unpacked_parts(level, sum_ref))
        g_out[...] = g
        store_terms(level - 1, g, yi_ref, out_ref)

    def unpacked_parts(level, sum_ref):
        run = waves // halves(level) * edge // LANES
        return jnp.concatenate(
            [unpacked(sum_ref[i * run : (i + 1) * run], edge) for i in range(halves(level))], axis=0
        )

    def collect(total, level):
        for axis_no in range(level):
            axis = row_axes[y_levels - 1 - axis_no]
            other = lax.ppermute(total, axis, [(0, 1), (1, 0)])
            first = lax.axis_index(axis) == 0
            total = jnp.concatenate(
                [jnp.where(first, total, other), jnp.where(first, other, total)], axis=0
            )
        return total

    x_lanes = -(-(x_levels + 1) * edge // LANES) * LANES

    def sides_of(terms):
        low, high = (
            jnp.concatenate([edge_of(terms, 2 * c + side) for c in range(cols)], axis=1)
            for side in range(2)
        )
        odd_row = bit(my_row(), 0) == 1
        return jnp.where(odd_row, high, low), jnp.where(odd_row, low, high)

    def split_body(g_ref, w_ref, sum_ref, yi_ref, g_out, own_out, other_out):
        g = with_row_edge(1, g_ref[...], w_ref[...], unpacked_parts(1, sum_ref))
        g_out[...] = g
        own_out[...], other_out[...] = sides_of(dot_t(g, yi_ref[0]))

    def at_upper():
        return (my_row() == 1) | (my_row() == 2)

    def upper_body(got_ref, g_ref, w_ref, yi_ref, columns_ref, other_ref, own_out, other_out, half_out):
        q = unpacked(jnp.sum(got_ref[...], axis=0), edge)
        w = w_ref[...]
        w = jnp.where(my_row() < 2, w[:, :edge], w[:, edge:])
        odd_row = bit(my_row(), 0) == 1
        half = waves // 2
        value = jnp.where(odd_row, w[half:], w[:half]) + q
        half_out[...] = value
        columns = unpacked(jnp.where(at_upper(), columns_ref[...], other_ref[...]), edge)
        added = dot_t(value, columns)
        terms = dot_t(g_ref[...], yi_ref[0])
        terms = jnp.concatenate(
            [
                terms[:half] + jnp.where(odd_row, 0.0, added),
                terms[half:] + jnp.where(odd_row, added, 0.0),
            ],
            axis=0,
        )
        own_out[...], other_out[...] = sides_of(terms)

    node_starts = []
    for k in range(x_levels):
        node_starts.append(sum(cols >> (i + 1) for i in range(k)) * pair)
    node_lanes = (cols - 1) * pair

    def prepare_body(g_ref, w_ref, xi_ref, held_ref, moved_ref, matrix_out, known_out):
        g = with_row_edge(0, g_ref[...], w_ref[...], 0.0)
        row = []
        for c in range(cols):
            held = held_of(c, held_ref, moved_ref)[:in_rows]
            row.append(
                jnp.concatenate(
                    [held[:, i * in_lanes : (i + 1) * in_lanes] for i in range(runs)], axis=0
                )
            )
        matrix_out[...] = jnp.zeros_like(matrix_out)
        for k in range(x_levels):
            known = dot_t(g, xi_ref[k])
            for node in range(cols >> (k + 1)):
                start = node_starts[k] + node * pair
                inside = my_column() >> (k + 1) == node
                known_out[:, start : start + pair] = jnp.where(inside, known, 0.0)
                for c in range(node << (k + 1), (node + 1) << (k + 1)):
                    matrix_out[start : start + pair, c * edge : (c + 1) * edge] = edge_of(row[c], k)

    def x_terms_body(own_ref, got_ref, matrix_ref, known_ref, *refs):
        out_ref = refs[-1]
        q = own_ref[...] + got_ref[...]
        terms = dot_t(q, matrix_ref[...]) + known_ref[...]
        if whole_solve:
            g_ref, half_ref, other_half_ref, xi_ref, g_out, _ = refs
            odd_row = bit(my_row(), 0) == 1
            mine, other = half_ref[...], other_half_ref[...]
            value = jnp.concatenate(
                [jnp.where(odd_row, other, mine), jnp.where(odd_row, mine, other)], axis=0
            )
            none = jnp.zeros_like(value)
            upper = jnp.concatenate(
                [
                    jnp.where(my_row() == 2, value, 0.0),
                    none,
                    jnp.where(my_row() == 1, value, 0.0),
                    none,
                ],
                axis=1,
            )
            g_out[...] = g_ref[...] + upper
            added = dot_t(upper, xi_ref[...].reshape(x_levels * pair, leaf))
        for c in range(cols):
            picked = []
            for k in range(x_levels):
                start = node_starts[k] + (c >> (k + 1)) * pair + bit(c, k) * edge
                piece = terms[:, start : start + edge]
                if whole_solve:
                    inside = my_column() >> (k + 1) == c >> (k + 1)
                    piece = piece + jnp.where(inside, edge_of(added, 2 * k + bit(c, k)), 0.0)
                picked.append(piece)
            out_ref[c] = pad_lanes(jnp.concatenate(picked + [edge_of(q, c)], axis=1), x_lanes)

    def finish_body(g_ref, w_ref, h0_ref, got_ref, lo_ref, *refs):
        keep_ref, ends_ref = refs[:x_levels], refs[x_levels : 2 * x_levels - 1]
        g_out, t_out, *faces = refs[2 * x_levels - 1 :]
        q = jnp.sum(got_ref[...], axis=0)
        g = with_row_edge(0, g_ref[...], w_ref[...], edge_of(q, x_levels))
        gl = jnp.zeros((waves, edge), f32)
        gr = gl
        for level in reversed(range(x_levels)):
            is_right = bit(my_column(), level) == 1
            keep = keep_ref[level][...]
            value = edge_of(q, level) + jnp.where(is_right, keep[:, edge:], keep[:, :edge])
            if level < x_levels - 1:
                end = ends_ref[level][...]
                end = jnp.where(is_right, end[edge:], end[:edge])
                value = value + dot_t(jnp.concatenate([gl, gr], axis=1), end)
            gl = jnp.where(is_right, value, gl)
            gr = jnp.where(is_right, gr, value)
        g = jnp.concatenate(
            [edge_of(g, 0), edge_of(g, 1) + gr, edge_of(g, 2), edge_of(g, 3) + gl], axis=1
        )
        g_out[...] = g
        t = g - (dot_t(g, lo_ref[...]) + h0_ref[...])
        t_out[...] = t
        odd_col = bit(my_column(), 0) == 1
        odd_row = bit(my_row(), 0) == 1
        bottom, right, top, left = (packed(edge_of(t, i), edge) for i in range(4))
        faces[0][...] = jnp.where(odd_col, left, right)
        faces[1][...] = jnp.where(odd_col, right, left)
        faces[2][...] = jnp.where(odd_row, bottom, top)
        faces[3][...] = jnp.where(odd_row, top, bottom)

    def trace_body(t_ref, a_ref, b_ref, c_ref, d_ref, out_ref):
        t = t_ref[...]
        odd_col = bit(my_column(), 0) == 1
        odd_row = bit(my_row(), 0) == 1
        near_x, far_x, near_y, far_y = (
            unpacked(ref[...], edge) for ref in (a_ref, b_ref, c_ref, d_ref)
        )
        east = jnp.where(odd_col, far_x, near_x)
        west = jnp.where(odd_col, near_x, far_x)
        north = jnp.where(odd_row, far_y, near_y)
        south = jnp.where(odd_row, near_y, far_y)

        def mean(shared, own, other):
            return jnp.where(shared, 0.5 * (own + other), own)

        trace = jnp.concatenate(
            [
                mean(my_row() > 0, edge_of(t, 0), south),
                mean(my_column() < cols - 1, edge_of(t, 1), east),
                mean(my_row() < rows - 1, edge_of(t, 2), north),
                mean(my_column() > 0, edge_of(t, 3), west),
            ],
            axis=1,
        )
        out_ref[...] = trace.reshape(out_ref.shape)

    (offer,) = fused(functools.partial(offer_body, 0), [offer_shape(0)], h)
    y_keep = []
    for level in range(y_levels):
        if whole_solve:
            got = lax.all_to_all(offer, ("box",) if level == 0 else (row_axes[0], "box"), 0, 0, tiled=True)
            pass_on = [second, columns] if level == 0 else []
            mine, *pass_on = fused(
                functools.partial(half_body, level),
                [(waves, iface)] + [x.shape for x in pass_on],
                got,
                *((held, moved) if level == 0 else (second, second_moved)),
                *pass_on,
                scratch=[(waves, cols * edge)],
                aliases={3: 1, 4: 2} if level == 0 else None,
            )
            if level == 0:
                second, columns = pass_on
                other_columns = lax.ppermute(columns, row_axes[-1], [(0, 1), (1, 0)])
                second_moved = passed_on(second, steps[-1])
            other = lax.ppermute(mine, row_axes[-1], [(0, 1), (1, 0)])
            if level == 0:
                h, w, offer = fused(
                    whole_body,
                    [(waves, leaf), (waves, pair), offer_shape(1)],
                    h,
                    mine,
                    other,
                    yo_all,
                    other_columns,
                )
            else:
                w, g, terms = fused(
                    functools.partial(turn_body, level),
                    [(waves, pair), (waves, leaf), terms_shape(level)],
                    h,
                    mine,
                    other,
                    yo_all,
                    yi_all,
                    reflect[0],
                )
            y_keep.append(w)
            continue
        share = waves // span(level)
        (w_offer,) = fused(
            functools.partial(solve_body, level),
            [(span(level) * cols, share * pair // LANES, LANES)],
            swap(offer, level),
            ys_all,
            scratch=[(share, iface)],
        )
        got = swap(w_offer, level)
        if level < y_levels - 1:
            h, w, offer = fused(
                functools.partial(spread_body, level),
                [(waves, leaf), (waves, pair), offer_shape(level + 1)],
                h,
                got,
                yo_all,
                scratch=[(waves, iface)],
            )
        else:
            w, g, terms = fused(
                functools.partial(turn_body, level),
                [(waves, pair), (waves, leaf), terms_shape(level)],
                h,
                got,
                yo_all,
                yi_all,
                reflect[0],
                scratch=[(waves, iface)],
            )
        y_keep.append(w)
    for level in reversed(range(1, 1 if whole_solve else y_levels)):
        (total,) = fused(sum_body, [terms_shape(level)[1:]], swap(terms, level))
        total = collect(total, level)
        if level > 1:
            g, terms = fused(
                functools.partial(row_down_body, level),
                [(waves, leaf), terms_shape(level - 1)],
                g,
                y_keep[level],
                total,
                yi_all,
            )
    share = (waves, iface // 2)
    core = row_axes[-1]
    swapped = [(0, 1), (1, 0)]
    if whole_solve:
        own, other, half = fused(
            upper_body,
            [share, share, (waves // 2, edge)],
            swap(terms, 1),
            g,
            y_keep[1],
            yi_all,
            columns,
            other_columns,
        )
    else:
        g, own, other = fused(
            split_body, [(waves, leaf), share, share], g, y_keep[1], total, yi_all
        )
    got = lax.ppermute(other, core, swapped)
    matrix, known = fused(
        prepare_body,
        [(node_lanes, cols * edge), (waves, node_lanes)],
        g,
        y_keep[0],
        xi_all,
        *((second, second_moved) if whole_solve else (held, moved)),
    )
    upper = []
    if whole_solve:
        upper = [g, half, lax.ppermute(half, core, swapped), xi_all]
    *g_now, terms = fused(
        x_terms_body,
        [(waves, leaf)] * whole_solve + [(cols, waves, x_lanes)],
        own,
        got,
        matrix,
        known,
        *upper,
    )
    g = g_now[0] if g_now else g
    got = lax.all_to_all(terms, "box", 0, 0, tiled=True)
    face = (waves * edge // LANES, LANES)
    g, t, *faces = fused(
        finish_body,
        [(waves, leaf), (waves, leaf)] + [face] * 4,
        g,
        y_keep[0],
        h0,
        got,
        out_map,
        *x_keep,
        *ends,
    )

    def near(count):
        return [(i, i ^ 1) for i in range(count)]

    def far(count):
        one_way = [(i, i + 1) for i in range(1, count - 1, 2)]
        return one_way + [(j, i) for i, j in one_way]

    seen = [
        lax.ppermute(faces[0], "box", near(cols)),
        lax.ppermute(faces[1], "box", far(cols)),
        lax.ppermute(faces[2], row_axes, near(rows)),
        lax.ppermute(faces[3], row_axes, far(rows)),
    ]
    def field_body(g_ref, map_ref, from_load_ref, out_ref):
        field = from_load_ref[...] + dot_t(g_ref[...], map_ref[...])
        out_ref[...] = field.reshape(out_ref.shape)

    (field_vals,) = fused(
        field_body, [(waves, 1, 1, inner)], g, field_edges, from_load
    )
    (edge_trace,) = fused(trace_body, [(waves, 1, 1, leaf)], t, *seen)
    return field_vals, edge_trace


def solution(mesh):
    rows, cols = mesh.devices.shape
    bits = rows.bit_length() - 1
    row_axes = tuple(f"row{i}" for i in reversed(range(bits)))
    split = Mesh(mesh.devices.reshape((2,) * bits + (cols,)), row_axes + ("box",))
    late = P(None, row_axes, "box")
    early = P(row_axes, "box")
    return jax.shard_map(
        functools.partial(local, row_axes),
        mesh=split,
        in_specs=(late, early, early, early) + (late,) * 6 + (early,),
        out_specs=(late, late),
        check_vma=False,
    )
```

```python
import functools
import math

import jax
import jax.numpy as jnp
from jax import lax
from jax.experimental import pallas as pl
from jax.experimental.pallas import tpu as pltpu
from jax.sharding import Mesh, PartitionSpec as P

f32 = jnp.float32
LANES = 128
START_ROOM = 60 << 20


def dot(a, b, over=0):
    dims = (((1,), (over,)), ((), ()))

    def parts(x):
        high = x.astype(jnp.bfloat16)
        return high, (x - high.astype(f32)).astype(jnp.bfloat16)

    def product(x, y):
        return lax.dot_general(x, y, dims, preferred_element_type=f32)

    a_high, a_low = parts(a)
    b_high, b_low = parts(b)
    return product(a_high, b_high) + (product(a_high, b_low) + product(a_low, b_high))


def dot_t(a, b):
    return dot(a, b, 1)


def fused(body, outs, *args, scratch=(), aliases=None):
    vmem = pl.BlockSpec(memory_space=pltpu.VMEM)
    return pl.pallas_call(
        body,
        out_shape=[pltpu.VMEM(s, f32) for s in outs],
        in_specs=[vmem] * len(args),
        out_specs=[vmem] * len(outs),
        scratch_shapes=[pltpu.VMEM(s, f32) for s in scratch],
        input_output_aliases=aliases or {},
        compiler_params=pltpu.CompilerParams(vmem_limit_bytes=12 << 20),
    )(*args)


def packed(x, width):
    runs = LANES // width
    rows = x.shape[0] // runs
    return jnp.concatenate([x[i * rows : (i + 1) * rows] for i in range(runs)], axis=1)


def unpacked(x, width):
    return jnp.concatenate(
        [x[:, i * width : (i + 1) * width] for i in range(x.shape[1] // width)], axis=0
    )


def pad_lanes(x, lanes):
    if x.shape[1] == lanes:
        return x
    return jnp.concatenate([x, jnp.zeros((x.shape[0], lanes - x.shape[1]), f32)], axis=1)


def local(
    row_axes,
    load,
    leaf_load_map,
    leaf_out_map,
    leaf_field_map,
    x_solve,
    x_out,
    x_in,
    y_solve,
    y_out,
    y_in,
    reflect,
):
    edge = leaf_out_map.shape[-1] // 4
    cols = lax.axis_size("box")
    rows = 1
    for axis in row_axes:
        rows *= lax.axis_size(axis)
    x_levels = x_solve.shape[0]
    y_levels = y_solve.shape[0]
    waves = load.shape[0]
    leaf = 4 * edge
    pair = 2 * edge
    iface = cols * pair
    load_here = load[:, 0, 0, :]
    inner = load_here.shape[1]

    def my_column():
        return lax.axis_index("box")

    def my_row():
        return lax.axis_index(row_axes)

    def bit(value, level):
        return (value >> level) & 1

    def edge_of(x, number):
        return x[:, number * edge : (number + 1) * edge]

    def exchange_shape(level):
        kept = x_levels - 1 - level
        lanes = (2 + 2 * kept) * edge
        return (pair, -(-lanes // LANES) * LANES)

    def pieces_of(x, first, count):
        return [edge_of(x, first + i) for i in range(count)]

    whole_solve = (x_levels, y_levels) == (3, 2) and iface * iface <= 1 << 18
    in_lanes = -(-x_levels * edge // LANES) * LANES
    width = iface if whole_solve else 4 * in_lanes
    runs = width // in_lanes
    in_rows = pair // runs
    solve_rows = edge if whole_solve else 0

    def held_shape(count, *parts):
        return (count, sum(parts), width)

    def passed_on(held, bit_no):
        return lax.ppermute(held, "box", [(i, i ^ (1 << bit_no)) for i in range(cols)])

    steps = [x_levels - 1] + list(range(x_levels - 1))
    joined_at = [0] + list(range(2, x_levels))

    def held_of(c, held_ref, moved_ref):
        place = sum(bit(c, b) << k for k, b in enumerate(steps[:-1]))
        same = bit(my_column(), steps[-1]) == bit(c, steps[-1])
        return jnp.where(same, held_ref[place], moved_ref[place])

    def join(step, held, moved, both_ref):
        high = bit(my_column(), steps[step]) == 1
        both_ref[: 1 << step] = jnp.where(high, moved, held)
        both_ref[1 << step :] = jnp.where(high, held, moved)

    def placing(body, shapes, *args, scratch=(), live=0):
        return pl.pallas_call(
            body,
            out_shape=[pltpu.VMEM(s, f32) for s in shapes],
            in_specs=[pl.BlockSpec(memory_space=pl.ANY)] * len(args),
            out_specs=[pl.BlockSpec(memory_space=pltpu.VMEM)] * len(shapes),
            scratch_shapes=[pltpu.VMEM(s, f32) for s in scratch]
            + [pltpu.SemaphoreType.DMA((len(args) + 1,))],
            compiler_params=pltpu.CompilerParams(
                vmem_limit_bytes=START_ROOM - live - sum(4 * math.prod(s) for s in shapes)
            ),
        )(*args)

    def hold_body(solve_any, xi_any, *refs):
        *held_refs, solve, xi, sems = refs
        copies = [
            pltpu.make_async_copy(solve_any, solve, sems.at[0]),
            pltpu.make_async_copy(xi_any, xi, sems.at[1]),
        ]
        for copy in copies:
            copy.start()
        for copy in copies:
            copy.wait()
        odd_row = bit(my_row(), 0) == 1
        row_in = pad_lanes(
            jnp.concatenate(
                [
                    jnp.where(odd_row, edge_of(xi[k], 0), edge_of(xi[k], 2))
                    for k in range(x_levels)
                ],
                axis=1,
            ),
            in_lanes,
        )
        held_refs[0][0, solve_rows:] = jnp.concatenate(
            [row_in[i * in_rows : (i + 1) * in_rows] for i in range(runs)], axis=1
        )
        if whole_solve:
            for level, held_ref in enumerate(held_refs):
                low, high = (
                    jnp.concatenate(
                        [edge_of(solve[level], 2 * c + side) for c in range(cols)], axis=1
                    )
                    for side in range(2)
                )
                mine = jnp.where(odd_row == (level == 0), high, low)
                held_ref[0, :edge] = jnp.concatenate([mine[:edge], mine[edge:]], axis=1)

    ys_here, xi_here = y_solve[:, 0, 0], x_in[:, 0, 0]
    held, *upper_held = placing(
        hold_body,
        [held_shape(1, solve_rows, in_rows)] + [held_shape(1, solve_rows)] * whole_solve,
        ys_here,
        xi_here,
        scratch=[ys_here.shape, xi_here.shape],
    )

    columns_here = [x[:, 0, 0] for x in (jnp.swapaxes(x_out, 3, 4), x_in, x_solve)]
    rows_here = [x[:, 0, 0] for x in (y_out, y_in)] + [leaf_out_map[0, 0]]
    if not whole_solve:
        rows_here.append(ys_here)

    def start_body(load_any, map_any, xo_any, xi_any, xs_any, h_ref, out_ref, load_out, *refs):
        xo, xi, xs, load_v, map_v, sems = refs
        pairs = zip((load_any, map_any, xo_any, xi_any, xs_any), (load_v, map_v, xo, xi, xs))
        copies = [pltpu.make_async_copy(a, b, sems.at[i]) for i, (a, b) in enumerate(pairs)]
        for copy in copies:
            copy.start()
        copies[0].wait()
        copies[1].wait()
        loaded = load_v[...].reshape(waves, inner)
        load_out[...] = loaded
        h = dot_t(loaded, map_v[...])
        h_ref[...] = h
        copies[2].wait()
        copies[3].wait()
        is_right = bit(my_column(), 0) == 1
        travelling = [
            jnp.where(is_right, edge_of(x[k], 1), edge_of(x[k], 3))
            for x in (xi, xo)
            for k in range(x_levels - 1)
        ]
        out_ref[...] = pad_lanes(
            jnp.concatenate([edge_of(h, 3), edge_of(h, 1)] + travelling, axis=1), out_ref.shape[1]
        )
        copies[4].wait()

    h0, to_send, loaded, xo_all, xi_all, xs_all = placing(
        start_body,
        [(waves, leaf), exchange_shape(0), (waves, inner)] + [x.shape for x in columns_here],
        load,
        leaf_load_map[0, 0],
        *columns_here,
        scratch=[load.shape, (leaf, inner)],
    )

    def place_body(field_any, *refs):
        *refs, sems = refs
        count = len(rows_here)
        sources = [field_any.at[:, pl.ds(0, leaf)], field_any.at[:, pl.ds(leaf, inner)]]
        pairs = zip(sources + list(refs[:count]), refs[count:])
        copies = [pltpu.make_async_copy(a, b, sems.at[i]) for i, (a, b) in enumerate(pairs)]
        for copy in copies:
            copy.start()
        for copy in copies:
            copy.wait()

    field_edges, field_inner, yo_all, yi_all, out_map, *ys_all = placing(
        place_body,
        [(inner, leaf), (inner, inner)] + [x.shape for x in rows_here],
        leaf_field_map[0, 0],
        *rows_here,
        live=2 << 20,
    )

    side_rows = iface * edge // LANES

    def at_upper():
        return (my_row() == 1) | (my_row() == 2)

    def upper_edge(x):
        return jnp.where(my_row() == 1, x[2 * edge : 3 * edge], x[:edge])

    def aside_body(load_ref, map_ref, yi_ref, yo_ref, out_ref, *side_ref):
        out_ref[...] = dot_t(load_ref[...], map_ref[...])
        for ref in side_ref:
            ref[:side_rows] = packed(
                jnp.where(my_row() == 1, edge_of(yi_ref[0], 2), edge_of(yi_ref[0], 0)), edge
            )
            out_rows = upper_edge(yo_ref[0])
            ref[side_rows:] = jnp.concatenate(
                [out_rows[:, i * LANES : (i + 1) * LANES] for i in range(iface // LANES)], axis=0
            )

    from_load, *side = fused(
        aside_body,
        [(waves, inner)] + [(2 * side_rows, LANES)] * whole_solve,
        loaded,
        field_inner,
        yi_all,
        yo_all,
    )

    core = row_axes[-1]
    swapped = [(0, 1), (1, 0)]

    def x_body(level, tasks, h_ref, own_ref, got_ref, solve_ref, xo_ref, *refs):
        kept = x_levels - 1 - level
        count = sum(len(args) for _, args, _ in tasks)
        ins, (h_out, w_out, *rest) = refs[:count], refs[count:]
        rest, outs = rest[: 2 if kept else 0], rest[2 if kept else 0 :]
        for task, args, shapes in tasks:
            task(*ins[: len(args)], *outs[: len(shapes)])
            ins, outs = ins[len(args) :], outs[len(shapes) :]
        is_right = bit(my_column(), level) == 1
        own, got = own_ref[...], got_ref[...]
        left_child = jnp.where(is_right, got, own)
        right_child = jnp.where(is_right, own, got)
        v = jnp.concatenate([edge_of(left_child, 1), edge_of(right_child, 0)], axis=1)
        w = dot_t(v, solve_ref[level])
        w_out[...] = w
        if kept:
            next_ref, ends_ref = rest
            outer = [edge_of(x, 2 + kept) for x in (left_child, right_child)]
            spread = dot(w, jnp.concatenate([xo_ref[level]] + outer, axis=1))
            h_out[...] = h_ref[...] + spread[:, :leaf]
            left = edge_of(left_child, 0) + edge_of(spread, 4)
            right = edge_of(right_child, 1) + edge_of(spread, 5)
            ends_ref[...] = jnp.concatenate(
                [edge_of(left_child, 2), edge_of(right_child, 2)], axis=1
            )
            mine = jnp.where(bit(my_column(), level + 1) == 1, right_child, left_child)
            travelling = pieces_of(mine, 3, kept - 1) + pieces_of(mine, 3 + kept, kept - 1)
            next_ref[...] = pad_lanes(
                jnp.concatenate([left, right] + travelling, axis=1), next_ref.shape[1]
            )
        else:
            h_out[...] = h_ref[...] + dot(w, xo_ref[level])

    def nothing(*refs):
        pass

    def join_first(held_ref, moved_ref, solve_ref, in_ref):
        join(0, held_ref[:, :solve_rows], moved_ref[:, :solve_rows], solve_ref)
        join(0, held_ref[:, solve_rows:], moved_ref[:, solve_rows:], in_ref)

    def join_upper(held_ref, moved_ref, in_ref, both_ref):
        join(0, held_ref[...], moved_ref[...], both_ref.at[:, in_rows : in_rows + solve_rows])
        both_ref[:, :in_rows] = in_ref[...]
        both_ref[:, in_rows + solve_rows :] = jnp.zeros_like(in_ref)

    def join_plain(step, held_ref, moved_ref, both_ref):
        join(step, held_ref[...], moved_ref[...], both_ref)

    h = h0
    x_keep, ends = [], []
    moved = passed_on(held, steps[0])
    upper_moved = [passed_on(x, steps[0]) for x in upper_held]
    for level in range(x_levels):
        got = lax.ppermute(to_send, "box", [(i, i ^ (1 << level)) for i in range(cols)])
        outs = [(waves, leaf), (waves, pair)]
        if level < x_levels - 1:
            outs += [exchange_shape(level + 1), (pair, pair)]
        args = [h, to_send, got, xs_all, xo_all]
        tasks = []
        if level < 2:
            tasks.append((nothing, [(out_map, from_load)[level]], []))
        if whole_solve and level == 0:
            shapes = [held_shape(2, solve_rows), held_shape(2, in_rows)]
            tasks.append((join_first, [held, moved], shapes))
        elif whole_solve and level == 1:
            tasks.append((nothing, side, [x.shape for x in side]))
            shapes = [held_shape(2, in_rows, solve_rows, in_rows)]
            tasks.append((join_upper, upper_held + upper_moved + [shared_in], shapes))
        elif whole_solve:
            tasks.append((nothing, other_side, []))
            shapes = [held_shape(4, solve_rows)]
            tasks.append((functools.partial(join_plain, 1), [held, moved], shapes))
        elif level in joined_at:
            step = joined_at.index(level)
            shape = held_shape(2 << step, in_rows)
            tasks.append((functools.partial(join_plain, step), [held, moved], [shape]))
        aliases = {len(args) + 1: len(outs)} if level == 1 and whole_solve else None
        h, w, *rest = fused(
            functools.partial(x_body, level, tasks),
            outs + [shape for task in tasks for shape in task[2]],
            *args,
            *(x for task in tasks for x in task[1]),
            aliases=aliases,
        )
        x_keep.append(w)
        if level < x_levels - 1:
            to_send, end, *rest = rest
            ends.append(end)
        if whole_solve and level == 0:
            held, shared_in = rest
            moved = passed_on(held, steps[1])
        elif whole_solve and level == 1:
            side, upper_held = rest[:1], rest[1]
            upper_moved = passed_on(upper_held, steps[1])
            other_side = [lax.ppermute(x, core, swapped) for x in side]
        elif whole_solve:
            (held,) = rest
            moved = passed_on(held, steps[2])
        elif level in joined_at:
            (held,) = rest
            moved = passed_on(held, steps[step + 1])

    def group(level):
        return tuple(row_axes[y_levels - 1 - level :]) + ("box",)

    def span(level):
        return 2 << level

    def swap(x, level):
        return lax.all_to_all(x, group(level), 0, 0, tiled=True)

    def offer_shape(level):
        if whole_solve:
            return (rows**level * cols, (waves >> level) * edge // LANES, LANES)
        return (span(level) * cols, waves // span(level) * edge // LANES, LANES)

    def store_offer(level, h, out):
        size = span(level)
        share = waves // size
        facing = jnp.where(
            lax.rem(my_row(), size) == size // 2 - 1, edge_of(h, 2), edge_of(h, 0)
        )
        if whole_solve:
            out[...] = jnp.broadcast_to(packed(facing, edge), out.shape)
            return
        for target in range(size):
            piece = packed(facing[target * share : (target + 1) * share], edge)
            out[target * cols : (target + 1) * cols] = jnp.broadcast_to(piece, (cols,) + piece.shape)

    def offer_body(level, h_ref, out_ref, *face_ref):
        h = h_ref[...]
        store_offer(level, h, out_ref)
        for ref in face_ref:
            ref[...] = packed(jnp.where(my_row() == 1, edge_of(h, 2), edge_of(h, 0)), edge)

    def gather_v(level, got_ref, v_ref):
        size = span(level)
        low = (size // 2 - 1) * cols
        run = got_ref.shape[1]
        for side in range(2):
            for c in range(cols):
                piece = got_ref[low + side * cols + c]
                for k in range(LANES // edge):
                    start = c * pair + side * edge
                    v_ref[k * run : (k + 1) * run, start : start + edge] = edge_of(piece, k)

    def solve_body(level, got_ref, solve_ref, out_ref, v_ref):
        gather_v(level, got_ref, v_ref)
        w = packed(dot_t(v_ref[...], solve_ref[level]), pair)
        out_ref[...] = jnp.broadcast_to(w, out_ref.shape)

    def own_columns(w_all):
        own = w_all[:, :pair]
        for c in range(1, cols):
            own = jnp.where(my_column() == c, w_all[:, c * pair : (c + 1) * pair], own)
        return own

    def gather_w(level, got_ref, w_ref):
        size = span(level)
        share = waves // size
        run = got_ref.shape[1]
        for target in range(size):
            for c in range(cols):
                piece = got_ref[target * cols + c]
                for k in range(LANES // pair):
                    start = target * share + k * run
                    w_ref[start : start + run, c * pair : (c + 1) * pair] = piece[
                        :, k * pair : (k + 1) * pair
                    ]
        return w_ref[...]

    def half_body(level, got_ref, held_ref, moved_ref, *refs):
        if level == 0:
            upper_held_ref, upper_moved_ref, _, out_ref, _, upper_ref, v_ref = refs
            kept = in_rows + solve_rows
            join(1, upper_held_ref[:, :kept], upper_moved_ref[:, :kept], upper_ref)
        else:
            out_ref, v_ref = refs
        odd_row = bit(my_row(), 0) == 1
        run = got_ref.shape[1]
        for c in range(cols):
            for part in range(1 + level):
                piece = got_ref[part * cols + c]
                if level == 1:
                    piece = jnp.where(odd_row, piece, got_ref[(2 + part) * cols + c])
                for k in range(LANES // edge):
                    start = (part * LANES // edge + k) * run
                    v_ref[start : start + run, c * edge : (c + 1) * edge] = edge_of(piece, k)
        solve = []
        for c in range(cols):
            start = in_rows * level
            block = held_of(c, held_ref, moved_ref)[start : start + edge]
            solve += [block[:, : iface // 2], block[:, iface // 2 :]]
        out_ref[...] = dot_t(v_ref[...], jnp.concatenate(solve, axis=0))

    def whole_body(
        h_ref, mine_ref, other_ref, yo_ref, face_ref, other_face_ref, side_ref, h_out, w_out, next_ref
    ):
        w_all = mine_ref[...] + other_ref[...]
        w_out[...] = own_columns(w_all)
        out_rows = side_ref[side_rows:]
        out_rows = jnp.concatenate(
            [out_rows[i * edge : (i + 1) * edge] for i in range(iface // LANES)], axis=1
        )
        out_rows = jnp.where(at_upper(), upper_edge(yo_ref[0]), out_rows)
        spread = dot_t(w_all, jnp.concatenate([yo_ref[0], out_rows], axis=0))
        h_out[...] = h_ref[...] + spread[:, :leaf]
        face = unpacked(jnp.where(at_upper(), face_ref[...], other_face_ref[...]), edge)
        face = face + spread[:, leaf:]
        half = jnp.where(bit(my_row(), 0) == 1, face[waves // 2 :], face[: waves // 2])
        next_ref[...] = jnp.broadcast_to(packed(half, edge), next_ref.shape)

    def spread_body(level, h_ref, got_ref, yo_ref, h_out, w_out, next_ref, w_ref):
        w_all = gather_w(level, got_ref, w_ref)
        w_out[...] = own_columns(w_all)
        h = h_ref[...] + dot_t(w_all, yo_ref[level])
        h_out[...] = h
        store_offer(level + 1, h, next_ref)

    def halves(level):
        return span(level) // 2

    def terms_shape(level):
        return (span(level) * cols, waves // halves(level) * edge // LANES, LANES)

    def store_terms(level, g, yi_ref, out):
        terms = dot_t(g, yi_ref[level])
        half = halves(level)
        share = waves // half
        for side in range(2):
            for c in range(cols):
                start = c * pair + side * edge
                piece = terms[:, start : start + edge]
                for part in range(half):
                    out[(side * half + part) * cols + c] = packed(
                        piece[part * share : (part + 1) * share], edge
                    )

    def turn_body(level, h_ref, got_ref, *refs):
        if whole_solve:
            other_ref, yo_ref, yi_ref, reflect_ref, w_out, g_out, out_ref = refs
            w_all = got_ref[...] + other_ref[...]
        else:
            yo_ref, yi_ref, reflect_ref, w_out, g_out, out_ref, w_ref = refs
            w_all = gather_w(level, got_ref, w_ref)
        w_out[...] = own_columns(w_all)
        h = h_ref[...] + dot_t(w_all, yo_ref[level])
        lane = lax.broadcasted_iota(jnp.int32, (1, leaf), 1)

        def side(number):
            return (lane >= number * edge) & (lane < (number + 1) * edge)

        outer = (
            side(0) & (my_row() == 0)
            | side(1) & (my_column() == cols - 1)
            | side(2) & (my_row() == rows - 1)
            | side(3) & (my_column() == 0)
        )
        g = jnp.where(outer, h * reflect_ref[...], 0.0)
        g_out[...] = g
        store_terms(level, g, yi_ref, out_ref)

    def sum_body(got_ref, out_ref):
        out_ref[...] = jnp.sum(got_ref[...], axis=0)

    def with_row_edge(level, g, w, q):
        size = span(level)
        place = lax.rem(my_row(), size)
        is_low = place == size // 2 - 1
        is_high = place == size // 2
        value = jnp.where(place < size // 2, w[:, :edge], w[:, edge:]) + q
        bottom = jnp.where(is_high, value, edge_of(g, 0))
        top = jnp.where(is_low, value, edge_of(g, 2))
        return jnp.concatenate([bottom, edge_of(g, 1), top, edge_of(g, 3)], axis=1)

    def row_down_body(level, g_ref, w_ref, sum_ref, yi_ref, g_out, out_ref):
        g = with_row_edge(level, g_ref[...], w_ref[...], unpacked_parts(level, sum_ref))
        g_out[...] = g
        store_terms(level - 1, g, yi_ref, out_ref)

    def unpacked_parts(level, sum_ref):
        run = waves // halves(level) * edge // LANES
        return jnp.concatenate(
            [unpacked(sum_ref[i * run : (i + 1) * run], edge) for i in range(halves(level))], axis=0
        )

    def collect(total, level):
        for axis_no in range(level):
            axis = row_axes[y_levels - 1 - axis_no]
            other = lax.ppermute(total, axis, [(0, 1), (1, 0)])
            first = lax.axis_index(axis) == 0
            total = jnp.concatenate(
                [jnp.where(first, total, other), jnp.where(first, other, total)], axis=0
            )
        return total

    x_lanes = -(-(x_levels + 1) * edge // LANES) * LANES

    def sides_of(terms):
        low, high = (
            jnp.concatenate([edge_of(terms, 2 * c + side) for c in range(cols)], axis=1)
            for side in range(2)
        )
        odd_row = bit(my_row(), 0) == 1
        return jnp.where(odd_row, high, low), jnp.where(odd_row, low, high)

    def split_body(g_ref, w_ref, sum_ref, yi_ref, g_out, own_out, other_out):
        g = with_row_edge(1, g_ref[...], w_ref[...], unpacked_parts(1, sum_ref))
        g_out[...] = g
        own_out[...], other_out[...] = sides_of(dot_t(g, yi_ref[0]))

    def upper_body(got_ref, g_ref, w_ref, yi_ref, side_ref, other_ref, own_out, other_out, half_out):
        q = unpacked(jnp.sum(got_ref[...], axis=0), edge)
        w = w_ref[...]
        w = jnp.where(my_row() < 2, w[:, :edge], w[:, edge:])
        odd_row = bit(my_row(), 0) == 1
        half = waves // 2
        value = jnp.where(odd_row, w[half:], w[:half]) + q
        half_out[...] = value
        columns = jnp.where(at_upper(), side_ref[:side_rows], other_ref[:side_rows])
        columns = unpacked(columns, edge)
        added = dot_t(value, columns)
        terms = dot_t(g_ref[...], yi_ref[0])
        terms = jnp.concatenate(
            [
                terms[:half] + jnp.where(odd_row, 0.0, added),
                terms[half:] + jnp.where(odd_row, added, 0.0),
            ],
            axis=0,
        )
        own_out[...], other_out[...] = sides_of(terms)

    node_starts = []
    for k in range(x_levels):
        node_starts.append(sum(cols >> (i + 1) for i in range(k)) * pair)
    node_lanes = (cols - 1) * pair

    def prepare_body(g_ref, w_ref, xi_ref, held_ref, moved_ref, matrix_out, known_out):
        g = with_row_edge(0, g_ref[...], w_ref[...], 0.0)
        row = []
        for c in range(cols):
            held = held_of(c, held_ref, moved_ref)[:in_rows]
            row.append(
                jnp.concatenate(
                    [held[:, i * in_lanes : (i + 1) * in_lanes] for i in range(runs)], axis=0
                )
            )
        matrix_out[...] = jnp.zeros_like(matrix_out)
        for k in range(x_levels):
            known = dot_t(g, xi_ref[k])
            for node in range(cols >> (k + 1)):
                start = node_starts[k] + node * pair
                inside = my_column() >> (k + 1) == node
                known_out[:, start : start + pair] = jnp.where(inside, known, 0.0)
                for c in range(node << (k + 1), (node + 1) << (k + 1)):
                    matrix_out[start : start + pair, c * edge : (c + 1) * edge] = edge_of(row[c], k)

    def x_terms_body(own_ref, got_ref, matrix_ref, known_ref, *refs):
        out_ref = refs[-1]
        q = own_ref[...] + got_ref[...]
        terms = dot_t(q, matrix_ref[...]) + known_ref[...]
        if whole_solve:
            g_ref, half_ref, other_half_ref, xi_ref, g_out, _ = refs
            odd_row = bit(my_row(), 0) == 1
            mine, other = half_ref[...], other_half_ref[...]
            value = jnp.concatenate(
                [jnp.where(odd_row, other, mine), jnp.where(odd_row, mine, other)], axis=0
            )
            none = jnp.zeros_like(value)
            upper = jnp.concatenate(
                [
                    jnp.where(my_row() == 2, value, 0.0),
                    none,
                    jnp.where(my_row() == 1, value, 0.0),
                    none,
                ],
                axis=1,
            )
            g_out[...] = g_ref[...] + upper
            added = dot_t(upper, xi_ref[...].reshape(x_levels * pair, leaf))
        for c in range(cols):
            picked = []
            for k in range(x_levels):
                start = node_starts[k] + (c >> (k + 1)) * pair + bit(c, k) * edge
                piece = terms[:, start : start + edge]
                if whole_solve:
                    inside = my_column() >> (k + 1) == c >> (k + 1)
                    piece = piece + jnp.where(inside, edge_of(added, 2 * k + bit(c, k)), 0.0)
                picked.append(piece)
            out_ref[c] = pad_lanes(jnp.concatenate(picked + [edge_of(q, c)], axis=1), x_lanes)

    def finish_body(g_ref, w_ref, h0_ref, got_ref, lo_ref, *refs):
        keep_ref, ends_ref = refs[:x_levels], refs[x_levels : 2 * x_levels - 1]
        g_out, t_out, *faces = refs[2 * x_levels - 1 :]
        q = jnp.sum(got_ref[...], axis=0)
        g = with_row_edge(0, g_ref[...], w_ref[...], edge_of(q, x_levels))
        gl = jnp.zeros((waves, edge), f32)
        gr = gl
        for level in reversed(range(x_levels)):
            is_right = bit(my_column(), level) == 1
            keep = keep_ref[level][...]
            value = edge_of(q, level) + jnp.where(is_right, keep[:, edge:], keep[:, :edge])
            if level < x_levels - 1:
                end = ends_ref[level][...]
                end = jnp.where(is_right, end[edge:], end[:edge])
                value = value + dot_t(jnp.concatenate([gl, gr], axis=1), end)
            gl = jnp.where(is_right, value, gl)
            gr = jnp.where(is_right, gr, value)
        g = jnp.concatenate(
            [edge_of(g, 0), edge_of(g, 1) + gr, edge_of(g, 2), edge_of(g, 3) + gl], axis=1
        )
        g_out[...] = g
        t = g - (dot_t(g, lo_ref[...]) + h0_ref[...])
        t_out[...] = t
        odd_col = bit(my_column(), 0) == 1
        odd_row = bit(my_row(), 0) == 1
        bottom, right, top, left = (packed(edge_of(t, i), edge) for i in range(4))
        faces[0][...] = jnp.where(odd_col, left, right)
        faces[1][...] = jnp.where(odd_col, right, left)
        faces[2][...] = jnp.where(odd_row, bottom, top)
        faces[3][...] = jnp.where(odd_row, top, bottom)

    def trace_body(t_ref, a_ref, b_ref, c_ref, d_ref, out_ref):
        t = t_ref[...]
        odd_col = bit(my_column(), 0) == 1
        odd_row = bit(my_row(), 0) == 1
        near_x, far_x, near_y, far_y = (
            unpacked(ref[...], edge) for ref in (a_ref, b_ref, c_ref, d_ref)
        )
        east = jnp.where(odd_col, far_x, near_x)
        west = jnp.where(odd_col, near_x, far_x)
        north = jnp.where(odd_row, far_y, near_y)
        south = jnp.where(odd_row, near_y, far_y)

        def mean(shared, own, other):
            return jnp.where(shared, 0.5 * (own + other), own)

        trace = jnp.concatenate(
            [
                mean(my_row() > 0, edge_of(t, 0), south),
                mean(my_column() < cols - 1, edge_of(t, 1), east),
                mean(my_row() < rows - 1, edge_of(t, 2), north),
                mean(my_column() > 0, edge_of(t, 3), west),
            ],
            axis=1,
        )
        out_ref[...] = trace.reshape(out_ref.shape)

    face = (waves * edge // LANES, LANES)
    offer, *upper_face = fused(
        functools.partial(offer_body, 0), [offer_shape(0)] + [face] * whole_solve, h
    )
    y_keep = []
    for level in range(y_levels):
        if whole_solve:
            axes = "box" if level == 0 else group(1)
            got = lax.all_to_all(offer, axes, 0, 0, tiled=True)
            if level == 0:
                (upper_face,) = upper_face
                mine, upper_face, second = fused(
                    functools.partial(half_body, 0),
                    [(waves, iface), upper_face.shape, held_shape(4, in_rows, solve_rows)],
                    got,
                    held,
                    moved,
                    upper_held,
                    upper_moved,
                    upper_face,
                    scratch=[(waves, cols * edge)],
                    aliases={5: 1},
                )
                other_face = lax.ppermute(upper_face, core, swapped)
                second_moved = passed_on(second, steps[2])
            else:
                (mine,) = fused(
                    functools.partial(half_body, 1),
                    [(waves, iface)],
                    got,
                    second,
                    second_moved,
                    scratch=[(waves, cols * edge)],
                )
            other = lax.ppermute(mine, core, swapped)
            if level == 0:
                h, w, offer = fused(
                    whole_body,
                    [(waves, leaf), (waves, pair), offer_shape(1)],
                    h,
                    mine,
                    other,
                    yo_all,
                    upper_face,
                    other_face,
                    *other_side,
                )
            else:
                w, g, terms = fused(
                    functools.partial(turn_body, level),
                    [(waves, pair), (waves, leaf), terms_shape(level)],
                    h,
                    mine,
                    other,
                    yo_all,
                    yi_all,
                    reflect[0],
                )
            y_keep.append(w)
            continue
        share = waves // span(level)
        (w_offer,) = fused(
            functools.partial(solve_body, level),
            [(span(level) * cols, share * pair // LANES, LANES)],
            swap(offer, level),
            *ys_all,
            scratch=[(share, iface)],
        )
        got = swap(w_offer, level)
        if level < y_levels - 1:
            h, w, offer = fused(
                functools.partial(spread_body, level),
                [(waves, leaf), (waves, pair), offer_shape(level + 1)],
                h,
                got,
                yo_all,
                scratch=[(waves, iface)],
            )
        else:
            w, g, terms = fused(
                functools.partial(turn_body, level),
                [(waves, pair), (waves, leaf), terms_shape(level)],
                h,
                got,
                yo_all,
                yi_all,
                reflect[0],
                scratch=[(waves, iface)],
            )
        y_keep.append(w)
    for level in reversed(range(1, 1 if whole_solve else y_levels)):
        (total,) = fused(sum_body, [terms_shape(level)[1:]], swap(terms, level))
        total = collect(total, level)
        if level > 1:
            g, terms = fused(
                functools.partial(row_down_body, level),
                [(waves, leaf), terms_shape(level - 1)],
                g,
                y_keep[level],
                total,
                yi_all,
            )
    share = (waves, iface // 2)
    if whole_solve:
        own, other, half = fused(
            upper_body,
            [share, share, (waves // 2, edge)],
            swap(terms, 1),
            g,
            y_keep[1],
            yi_all,
            *side,
            *other_side,
        )
    else:
        g, own, other = fused(
            split_body, [(waves, leaf), share, share], g, y_keep[1], total, yi_all
        )
    got = lax.ppermute(other, core, swapped)
    matrix, known = fused(
        prepare_body,
        [(node_lanes, cols * edge), (waves, node_lanes)],
        g,
        y_keep[0],
        xi_all,
        *((second, second_moved) if whole_solve else (held, moved)),
    )
    upper = []
    if whole_solve:
        upper = [g, half, lax.ppermute(half, core, swapped), xi_all]
    *g_now, terms = fused(
        x_terms_body,
        [(waves, leaf)] * whole_solve + [(cols, waves, x_lanes)],
        own,
        got,
        matrix,
        known,
        *upper,
    )
    g = g_now[0] if g_now else g
    got = lax.all_to_all(terms, "box", 0, 0, tiled=True)
    g, t, *faces = fused(
        finish_body,
        [(waves, leaf), (waves, leaf)] + [face] * 4,
        g,
        y_keep[0],
        h0,
        got,
        out_map,
        *x_keep,
        *ends,
    )

    def near(count):
        return [(i, i ^ 1) for i in range(count)]

    def far(count):
        one_way = [(i, i + 1) for i in range(1, count - 1, 2)]
        return one_way + [(j, i) for i, j in one_way]

    seen = [
        lax.ppermute(faces[0], "box", near(cols)),
        lax.ppermute(faces[1], "box", far(cols)),
        lax.ppermute(faces[2], row_axes, near(rows)),
        lax.ppermute(faces[3], row_axes, far(rows)),
    ]
    def field_body(g_ref, map_ref, from_load_ref, out_ref):
        field = from_load_ref[...] + dot_t(g_ref[...], map_ref[...])
        out_ref[...] = field.reshape(out_ref.shape)

    (field_vals,) = fused(
        field_body, [(waves, 1, 1, inner)], g, field_edges, from_load
    )
    (edge_trace,) = fused(trace_body, [(waves, 1, 1, leaf)], t, *seen)
    return field_vals, edge_trace


def solution(mesh):
    rows, cols = mesh.devices.shape
    bits = rows.bit_length() - 1
    row_axes = tuple(f"row{i}" for i in reversed(range(bits)))
    split = Mesh(mesh.devices.reshape((2,) * bits + (cols,)), row_axes + ("box",))
    late = P(None, row_axes, "box")
    early = P(row_axes, "box")
    return jax.shard_map(
        functools.partial(local, row_axes),
        mesh=split,
        in_specs=(late, early, early, early) + (late,) * 6 + (early,),
        out_specs=(late, late),
        check_vma=False,
    )
```

```python
import functools
import math

import jax
import jax.numpy as jnp
from jax import lax
from jax.experimental import pallas as pl
from jax.experimental.pallas import tpu as pltpu
from jax.sharding import Mesh, PartitionSpec as P

f32 = jnp.float32
LANES = 128
START_ROOM = 60 << 20


def dot(a, b, over=0):
    dims = (((1,), (over,)), ((), ()))

    def parts(x):
        high = x.astype(jnp.bfloat16)
        return high, (x - high.astype(f32)).astype(jnp.bfloat16)

    def product(x, y):
        return lax.dot_general(x, y, dims, preferred_element_type=f32)

    a_high, a_low = parts(a)
    b_high, b_low = parts(b)
    both = product(jnp.concatenate([a_high, a_low], axis=0), b_high)
    return both[: a.shape[0]] + (product(a_high, b_low) + both[a.shape[0] :])


def dot_t(a, b):
    return dot(a, b, 1)


def fused(body, outs, *args, scratch=(), aliases=None):
    vmem = pl.BlockSpec(memory_space=pltpu.VMEM)
    return pl.pallas_call(
        body,
        out_shape=[pltpu.VMEM(s, f32) for s in outs],
        in_specs=[vmem] * len(args),
        out_specs=[vmem] * len(outs),
        scratch_shapes=[pltpu.VMEM(s, f32) for s in scratch],
        input_output_aliases=aliases or {},
        compiler_params=pltpu.CompilerParams(vmem_limit_bytes=12 << 20),
    )(*args)


def packed(x, width):
    runs = LANES // width
    rows = x.shape[0] // runs
    return jnp.concatenate([x[i * rows : (i + 1) * rows] for i in range(runs)], axis=1)


def unpacked(x, width):
    return jnp.concatenate(
        [x[:, i * width : (i + 1) * width] for i in range(x.shape[1] // width)], axis=0
    )


def pad_lanes(x, lanes):
    if x.shape[1] == lanes:
        return x
    return jnp.concatenate([x, jnp.zeros((x.shape[0], lanes - x.shape[1]), f32)], axis=1)


def local(
    row_axes,
    load,
    leaf_load_map,
    leaf_out_map,
    leaf_field_map,
    x_solve,
    x_out,
    x_in,
    y_solve,
    y_out,
    y_in,
    reflect,
):
    edge = leaf_out_map.shape[-1] // 4
    cols = lax.axis_size("box")
    rows = 1
    for axis in row_axes:
        rows *= lax.axis_size(axis)
    x_levels = x_solve.shape[0]
    y_levels = y_solve.shape[0]
    waves = load.shape[0]
    leaf = 4 * edge
    pair = 2 * edge
    iface = cols * pair
    load_here = load[:, 0, 0, :]
    inner = load_here.shape[1]

    def my_column():
        return lax.axis_index("box")

    def my_row():
        return lax.axis_index(row_axes)

    def bit(value, level):
        return (value >> level) & 1

    def edge_of(x, number):
        return x[:, number * edge : (number + 1) * edge]

    def exchange_shape(level):
        kept = x_levels - 1 - level
        lanes = (2 + 2 * kept) * edge
        return (pair, -(-lanes // LANES) * LANES)

    def pieces_of(x, first, count):
        return [edge_of(x, first + i) for i in range(count)]

    whole_solve = (x_levels, y_levels) == (3, 2) and iface * iface <= 1 << 18
    in_lanes = -(-x_levels * edge // LANES) * LANES
    width = iface if whole_solve else 4 * in_lanes
    runs = width // in_lanes
    in_rows = pair // runs
    solve_rows = edge if whole_solve else 0

    def held_shape(count, *parts):
        return (count, sum(parts), width)

    def passed_on(held, bit_no):
        return lax.ppermute(held, "box", [(i, i ^ (1 << bit_no)) for i in range(cols)])

    steps = [x_levels - 1] + list(range(x_levels - 1))
    joined_at = [0] + list(range(2, x_levels))

    def held_of(c, held_ref, moved_ref):
        place = sum(bit(c, b) << k for k, b in enumerate(steps[:-1]))
        same = bit(my_column(), steps[-1]) == bit(c, steps[-1])
        return jnp.where(same, held_ref[place], moved_ref[place])

    def join(step, held, moved, both_ref):
        high = bit(my_column(), steps[step]) == 1
        both_ref[: 1 << step] = jnp.where(high, moved, held)
        both_ref[1 << step :] = jnp.where(high, held, moved)

    def placing(body, shapes, *args, scratch=(), live=0):
        return pl.pallas_call(
            body,
            out_shape=[pltpu.VMEM(s, f32) for s in shapes],
            in_specs=[pl.BlockSpec(memory_space=pl.ANY)] * len(args),
            out_specs=[pl.BlockSpec(memory_space=pltpu.VMEM)] * len(shapes),
            scratch_shapes=[pltpu.VMEM(s, f32) for s in scratch]
            + [pltpu.SemaphoreType.DMA((len(args) + 1,))],
            compiler_params=pltpu.CompilerParams(
                vmem_limit_bytes=START_ROOM - live - sum(4 * math.prod(s) for s in shapes)
            ),
        )(*args)

    def hold_body(solve_any, xi_any, *refs):
        *held_refs, solve, xi, sems = refs
        copies = [
            pltpu.make_async_copy(solve_any, solve, sems.at[0]),
            pltpu.make_async_copy(xi_any, xi, sems.at[1]),
        ]
        for copy in copies:
            copy.start()
        for copy in copies:
            copy.wait()
        odd_row = bit(my_row(), 0) == 1
        row_in = pad_lanes(
            jnp.concatenate(
                [
                    jnp.where(odd_row, edge_of(xi[k], 0), edge_of(xi[k], 2))
                    for k in range(x_levels)
                ],
                axis=1,
            ),
            in_lanes,
        )
        held_refs[0][0, solve_rows:] = jnp.concatenate(
            [row_in[i * in_rows : (i + 1) * in_rows] for i in range(runs)], axis=1
        )
        if whole_solve:
            for level, held_ref in enumerate(held_refs):
                low, high = (
                    jnp.concatenate(
                        [edge_of(solve[level], 2 * c + side) for c in range(cols)], axis=1
                    )
                    for side in range(2)
                )
                mine = jnp.where(odd_row == (level == 0), high, low)
                held_ref[0, :edge] = jnp.concatenate([mine[:edge], mine[edge:]], axis=1)

    ys_here, xi_here = y_solve[:, 0, 0], x_in[:, 0, 0]
    held, *upper_held = placing(
        hold_body,
        [held_shape(1, solve_rows, in_rows)] + [held_shape(1, solve_rows)] * whole_solve,
        ys_here,
        xi_here,
        scratch=[ys_here.shape, xi_here.shape],
    )

    columns_here = [x[:, 0, 0] for x in (jnp.swapaxes(x_out, 3, 4), x_in, x_solve)]
    rows_here = [x[:, 0, 0] for x in (y_out, y_in)] + [leaf_out_map[0, 0]]
    if not whole_solve:
        rows_here.append(ys_here)

    def start_body(load_any, map_any, xo_any, xi_any, xs_any, h_ref, out_ref, load_out, *refs):
        xo, xi, xs, load_v, map_v, sems = refs
        pairs = zip((load_any, map_any, xo_any, xi_any, xs_any), (load_v, map_v, xo, xi, xs))
        copies = [pltpu.make_async_copy(a, b, sems.at[i]) for i, (a, b) in enumerate(pairs)]
        for copy in copies:
            copy.start()
        copies[0].wait()
        copies[1].wait()
        loaded = load_v[...].reshape(waves, inner)
        load_out[...] = loaded
        h = dot_t(loaded, map_v[...])
        h_ref[...] = h
        copies[2].wait()
        copies[3].wait()
        is_right = bit(my_column(), 0) == 1
        travelling = [
            jnp.where(is_right, edge_of(x[k], 1), edge_of(x[k], 3))
            for x in (xi, xo)
            for k in range(x_levels - 1)
        ]
        out_ref[...] = pad_lanes(
            jnp.concatenate([edge_of(h, 3), edge_of(h, 1)] + travelling, axis=1), out_ref.shape[1]
        )
        copies[4].wait()

    h0, to_send, loaded, xo_all, xi_all, xs_all = placing(
        start_body,
        [(waves, leaf), exchange_shape(0), (waves, inner)] + [x.shape for x in columns_here],
        load,
        leaf_load_map[0, 0],
        *columns_here,
        scratch=[load.shape, (leaf, inner)],
    )

    def place_body(field_any, *refs):
        *refs, sems = refs
        count = len(rows_here)
        sources = [field_any.at[:, pl.ds(0, leaf)], field_any.at[:, pl.ds(leaf, inner)]]
        pairs = zip(sources + list(refs[:count]), refs[count:])
        copies = [pltpu.make_async_copy(a, b, sems.at[i]) for i, (a, b) in enumerate(pairs)]
        for copy in copies:
            copy.start()
        for copy in copies:
            copy.wait()

    field_edges, field_inner, yo_all, yi_all, out_map, *ys_all = placing(
        place_body,
        [(inner, leaf), (inner, inner)] + [x.shape for x in rows_here],
        leaf_field_map[0, 0],
        *rows_here,
        live=2 << 20,
    )

    side_rows = iface * edge // LANES

    def at_upper():
        return (my_row() == 1) | (my_row() == 2)

    def upper_edge(x):
        return jnp.where(my_row() == 1, x[2 * edge : 3 * edge], x[:edge])

    def aside_body(load_ref, map_ref, yi_ref, yo_ref, out_ref, *side_ref):
        out_ref[...] = dot_t(load_ref[...], map_ref[...])
        for ref in side_ref:
            ref[:side_rows] = packed(
                jnp.where(my_row() == 1, edge_of(yi_ref[0], 2), edge_of(yi_ref[0], 0)), edge
            )
            out_rows = upper_edge(yo_ref[0])
            ref[side_rows:] = jnp.concatenate(
                [out_rows[:, i * LANES : (i + 1) * LANES] for i in range(iface // LANES)], axis=0
            )

    from_load, *side = fused(
        aside_body,
        [(waves, inner)] + [(2 * side_rows, LANES)] * whole_solve,
        loaded,
        field_inner,
        yi_all,
        yo_all,
    )

    core = row_axes[-1]
    swapped = [(0, 1), (1, 0)]

    def x_body(level, tasks, h_ref, own_ref, got_ref, solve_ref, xo_ref, *refs):
        kept = x_levels - 1 - level
        count = sum(len(args) for _, args, _ in tasks)
        ins, (h_out, w_out, *rest) = refs[:count], refs[count:]
        rest, outs = rest[: 2 if kept else 0], rest[2 if kept else 0 :]
        for task, args, shapes in tasks:
            task(*ins[: len(args)], *outs[: len(shapes)])
            ins, outs = ins[len(args) :], outs[len(shapes) :]
        is_right = bit(my_column(), level) == 1
        own, got = own_ref[...], got_ref[...]
        left_child = jnp.where(is_right, got, own)
        right_child = jnp.where(is_right, own, got)
        v = jnp.concatenate([edge_of(left_child, 1), edge_of(right_child, 0)], axis=1)
        w = dot_t(v, solve_ref[level])
        w_out[...] = w
        if kept:
            next_ref, ends_ref = rest
            outer = [edge_of(x, 2 + kept) for x in (left_child, right_child)]
            spread = dot(w, jnp.concatenate([xo_ref[level]] + outer, axis=1))
            h_out[...] = h_ref[...] + spread[:, :leaf]
            left = edge_of(left_child, 0) + edge_of(spread, 4)
            right = edge_of(right_child, 1) + edge_of(spread, 5)
            ends_ref[...] = jnp.concatenate(
                [edge_of(left_child, 2), edge_of(right_child, 2)], axis=1
            )
            mine = jnp.where(bit(my_column(), level + 1) == 1, right_child, left_child)
            travelling = pieces_of(mine, 3, kept - 1) + pieces_of(mine, 3 + kept, kept - 1)
            next_ref[...] = pad_lanes(
                jnp.concatenate([left, right] + travelling, axis=1), next_ref.shape[1]
            )
        else:
            h_out[...] = h_ref[...] + dot(w, xo_ref[level])

    def nothing(*refs):
        pass

    def join_first(held_ref, moved_ref, solve_ref, in_ref):
        join(0, held_ref[:, :solve_rows], moved_ref[:, :solve_rows], solve_ref)
        join(0, held_ref[:, solve_rows:], moved_ref[:, solve_rows:], in_ref)

    def join_upper(held_ref, moved_ref, in_ref, both_ref):
        join(0, held_ref[...], moved_ref[...], both_ref.at[:, in_rows : in_rows + solve_rows])
        both_ref[:, :in_rows] = in_ref[...]
        both_ref[:, in_rows + solve_rows :] = jnp.zeros_like(in_ref)

    def join_plain(step, held_ref, moved_ref, both_ref):
        join(step, held_ref[...], moved_ref[...], both_ref)

    h = h0
    x_keep, ends = [], []
    moved = passed_on(held, steps[0])
    upper_moved = [passed_on(x, steps[0]) for x in upper_held]
    for level in range(x_levels):
        got = lax.ppermute(to_send, "box", [(i, i ^ (1 << level)) for i in range(cols)])
        outs = [(waves, leaf), (waves, pair)]
        if level < x_levels - 1:
            outs += [exchange_shape(level + 1), (pair, pair)]
        args = [h, to_send, got, xs_all, xo_all]
        tasks = []
        if level < 2:
            tasks.append((nothing, [(out_map, from_load)[level]], []))
        if whole_solve and level == 0:
            shapes = [held_shape(2, solve_rows), held_shape(2, in_rows)]
            tasks.append((join_first, [held, moved], shapes))
        elif whole_solve and level == 1:
            tasks.append((nothing, side, [x.shape for x in side]))
            shapes = [held_shape(2, in_rows, solve_rows, in_rows)]
            tasks.append((join_upper, upper_held + upper_moved + [shared_in], shapes))
        elif whole_solve:
            tasks.append((nothing, other_side, []))
            shapes = [held_shape(4, solve_rows)]
            tasks.append((functools.partial(join_plain, 1), [held, moved], shapes))
        elif level in joined_at:
            step = joined_at.index(level)
            shape = held_shape(2 << step, in_rows)
            tasks.append((functools.partial(join_plain, step), [held, moved], [shape]))
        aliases = {len(args) + 1: len(outs)} if level == 1 and whole_solve else None
        h, w, *rest = fused(
            functools.partial(x_body, level, tasks),
            outs + [shape for task in tasks for shape in task[2]],
            *args,
            *(x for task in tasks for x in task[1]),
            aliases=aliases,
        )
        x_keep.append(w)
        if level < x_levels - 1:
            to_send, end, *rest = rest
            ends.append(end)
        if whole_solve and level == 0:
            held, shared_in = rest
            moved = passed_on(held, steps[1])
        elif whole_solve and level == 1:
            side, upper_held = rest[:1], rest[1]
            upper_moved = passed_on(upper_held, steps[1])
            other_side = [lax.ppermute(x, core, swapped) for x in side]
        elif whole_solve:
            (held,) = rest
            moved = passed_on(held, steps[2])
        elif level in joined_at:
            (held,) = rest
            moved = passed_on(held, steps[step + 1])

    def group(level):
        return tuple(row_axes[y_levels - 1 - level :]) + ("box",)

    def span(level):
        return 2 << level

    def swap(x, level):
        return lax.all_to_all(x, group(level), 0, 0, tiled=True)

    def offer_shape(level):
        if whole_solve:
            return (rows**level * cols, (waves >> level) * edge // LANES, LANES)
        return (span(level) * cols, waves // span(level) * edge // LANES, LANES)

    def store_offer(level, h, out):
        size = span(level)
        share = waves // size
        facing = jnp.where(
            lax.rem(my_row(), size) == size // 2 - 1, edge_of(h, 2), edge_of(h, 0)
        )
        if whole_solve:
            out[...] = jnp.broadcast_to(packed(facing, edge), out.shape)
            return
        for target in range(size):
            piece = packed(facing[target * share : (target + 1) * share], edge)
            out[target * cols : (target + 1) * cols] = jnp.broadcast_to(piece, (cols,) + piece.shape)

    def offer_body(level, h_ref, out_ref, *face_ref):
        h = h_ref[...]
        store_offer(level, h, out_ref)
        for ref in face_ref:
            ref[...] = packed(jnp.where(my_row() == 1, edge_of(h, 2), edge_of(h, 0)), edge)

    def gather_v(level, got_ref, v_ref):
        size = span(level)
        low = (size // 2 - 1) * cols
        run = got_ref.shape[1]
        for side in range(2):
            for c in range(cols):
                piece = got_ref[low + side * cols + c]
                for k in range(LANES // edge):
                    start = c * pair + side * edge
                    v_ref[k * run : (k + 1) * run, start : start + edge] = edge_of(piece, k)

    def solve_body(level, got_ref, solve_ref, out_ref, v_ref):
        gather_v(level, got_ref, v_ref)
        w = packed(dot_t(v_ref[...], solve_ref[level]), pair)
        out_ref[...] = jnp.broadcast_to(w, out_ref.shape)

    def own_columns(w_all):
        own = w_all[:, :pair]
        for c in range(1, cols):
            own = jnp.where(my_column() == c, w_all[:, c * pair : (c + 1) * pair], own)
        return own

    def gather_w(level, got_ref, w_ref):
        size = span(level)
        share = waves // size
        run = got_ref.shape[1]
        for target in range(size):
            for c in range(cols):
                piece = got_ref[target * cols + c]
                for k in range(LANES // pair):
                    start = target * share + k * run
                    w_ref[start : start + run, c * pair : (c + 1) * pair] = piece[
                        :, k * pair : (k + 1) * pair
                    ]
        return w_ref[...]

    def half_body(level, got_ref, held_ref, moved_ref, *refs):
        if level == 0:
            upper_held_ref, upper_moved_ref, _, out_ref, _, upper_ref, v_ref = refs
            kept = in_rows + solve_rows
            join(1, upper_held_ref[:, :kept], upper_moved_ref[:, :kept], upper_ref)
        else:
            out_ref, v_ref = refs
        odd_row = bit(my_row(), 0) == 1
        run = got_ref.shape[1]
        for c in range(cols):
            for part in range(1 + level):
                piece = got_ref[part * cols + c]
                if level == 1:
                    piece = jnp.where(odd_row, piece, got_ref[(2 + part) * cols + c])
                for k in range(LANES // edge):
                    start = (part * LANES // edge + k) * run
                    v_ref[start : start + run, c * edge : (c + 1) * edge] = edge_of(piece, k)
        solve = []
        for c in range(cols):
            start = in_rows * level
            block = held_of(c, held_ref, moved_ref)[start : start + edge]
            solve += [block[:, : iface // 2], block[:, iface // 2 :]]
        out_ref[...] = dot_t(v_ref[...], jnp.concatenate(solve, axis=0))

    def whole_body(
        h_ref, mine_ref, other_ref, yo_ref, face_ref, other_face_ref, side_ref, h_out, w_out, next_ref
    ):
        w_all = mine_ref[...] + other_ref[...]
        w_out[...] = own_columns(w_all)
        out_rows = side_ref[side_rows:]
        out_rows = jnp.concatenate(
            [out_rows[i * edge : (i + 1) * edge] for i in range(iface // LANES)], axis=1
        )
        out_rows = jnp.where(at_upper(), upper_edge(yo_ref[0]), out_rows)
        spread = dot_t(w_all, jnp.concatenate([yo_ref[0], out_rows], axis=0))
        h_out[...] = h_ref[...] + spread[:, :leaf]
        face = unpacked(jnp.where(at_upper(), face_ref[...], other_face_ref[...]), edge)
        face = face + spread[:, leaf:]
        half = jnp.where(bit(my_row(), 0) == 1, face[waves // 2 :], face[: waves // 2])
        next_ref[...] = jnp.broadcast_to(packed(half, edge), next_ref.shape)

    def spread_body(level, h_ref, got_ref, yo_ref, h_out, w_out, next_ref, w_ref):
        w_all = gather_w(level, got_ref, w_ref)
        w_out[...] = own_columns(w_all)
        h = h_ref[...] + dot_t(w_all, yo_ref[level])
        h_out[...] = h
        store_offer(level + 1, h, next_ref)

    def halves(level):
        return span(level) // 2

    def terms_shape(level):
        return (span(level) * cols, waves // halves(level) * edge // LANES, LANES)

    def store_terms(level, g, yi_ref, out):
        terms = dot_t(g, yi_ref[level])
        half = halves(level)
        share = waves // half
        for side in range(2):
            for c in range(cols):
                start = c * pair + side * edge
                piece = terms[:, start : start + edge]
                for part in range(half):
                    out[(side * half + part) * cols + c] = packed(
                        piece[part * share : (part + 1) * share], edge
                    )

    def turn_body(level, h_ref, got_ref, *refs):
        if whole_solve:
            other_ref, yo_ref, yi_ref, reflect_ref, w_out, g_out, out_ref = refs
            w_all = got_ref[...] + other_ref[...]
        else:
            yo_ref, yi_ref, reflect_ref, w_out, g_out, out_ref, w_ref = refs
            w_all = gather_w(level, got_ref, w_ref)
        w_out[...] = own_columns(w_all)
        h = h_ref[...] + dot_t(w_all, yo_ref[level])
        lane = lax.broadcasted_iota(jnp.int32, (1, leaf), 1)

        def side(number):
            return (lane >= number * edge) & (lane < (number + 1) * edge)

        outer = (
            side(0) & (my_row() == 0)
            | side(1) & (my_column() == cols - 1)
            | side(2) & (my_row() == rows - 1)
            | side(3) & (my_column() == 0)
        )
        g = jnp.where(outer, h * reflect_ref[...], 0.0)
        g_out[...] = g
        store_terms(level, g, yi_ref, out_ref)

    def sum_body(got_ref, out_ref):
        out_ref[...] = jnp.sum(got_ref[...], axis=0)

    def with_row_edge(level, g, w, q):
        size = span(level)
        place = lax.rem(my_row(), size)
        is_low = place == size // 2 - 1
        is_high = place == size // 2
        value = jnp.where(place < size // 2, w[:, :edge], w[:, edge:]) + q
        bottom = jnp.where(is_high, value, edge_of(g, 0))
        top = jnp.where(is_low, value, edge_of(g, 2))
        return jnp.concatenate([bottom, edge_of(g, 1), top, edge_of(g, 3)], axis=1)

    def row_down_body(level, g_ref, w_ref, sum_ref, yi_ref, g_out, out_ref):
        g = with_row_edge(level, g_ref[...], w_ref[...], unpacked_parts(level, sum_ref))
        g_out[...] = g
        store_terms(level - 1, g, yi_ref, out_ref)

    def unpacked_parts(level, sum_ref):
        run = waves // halves(level) * edge // LANES
        return jnp.concatenate(
            [unpacked(sum_ref[i * run : (i + 1) * run], edge) for i in range(halves(level))], axis=0
        )

    def collect(total, level):
        for axis_no in range(level):
            axis = row_axes[y_levels - 1 - axis_no]
            other = lax.ppermute(total, axis, [(0, 1), (1, 0)])
            first = lax.axis_index(axis) == 0
            total = jnp.concatenate(
                [jnp.where(first, total, other), jnp.where(first, other, total)], axis=0
            )
        return total

    x_lanes = -(-(x_levels + 1) * edge // LANES) * LANES

    def sides_of(terms):
        low, high = (
            jnp.concatenate([edge_of(terms, 2 * c + side) for c in range(cols)], axis=1)
            for side in range(2)
        )
        odd_row = bit(my_row(), 0) == 1
        return jnp.where(odd_row, high, low), jnp.where(odd_row, low, high)

    def split_body(g_ref, w_ref, sum_ref, yi_ref, g_out, own_out, other_out):
        g = with_row_edge(1, g_ref[...], w_ref[...], unpacked_parts(1, sum_ref))
        g_out[...] = g
        own_out[...], other_out[...] = sides_of(dot_t(g, yi_ref[0]))

    def upper_body(got_ref, g_ref, w_ref, yi_ref, side_ref, other_ref, own_out, other_out, half_out):
        q = unpacked(jnp.sum(got_ref[...], axis=0), edge)
        w = w_ref[...]
        w = jnp.where(my_row() < 2, w[:, :edge], w[:, edge:])
        odd_row = bit(my_row(), 0) == 1
        half = waves // 2
        value = jnp.where(odd_row, w[half:], w[:half]) + q
        half_out[...] = value
        columns = jnp.where(at_upper(), side_ref[:side_rows], other_ref[:side_rows])
        columns = unpacked(columns, edge)
        added = dot_t(value, columns)
        terms = dot_t(g_ref[...], yi_ref[0])
        terms = jnp.concatenate(
            [
                terms[:half] + jnp.where(odd_row, 0.0, added),
                terms[half:] + jnp.where(odd_row, added, 0.0),
            ],
            axis=0,
        )
        own_out[...], other_out[...] = sides_of(terms)

    node_starts = []
    for k in range(x_levels):
        node_starts.append(sum(cols >> (i + 1) for i in range(k)) * pair)
    node_lanes = (cols - 1) * pair

    inner_lanes = x_levels * edge

    def prepare_body(g_ref, w_ref, xi_ref, held_ref, moved_ref, lo_ref, *refs):
        keep_ref, ends_ref = refs[:x_levels], refs[x_levels : 2 * x_levels - 1]
        matrix_out, known_out, chain_out, keep_out = refs[2 * x_levels - 1 :]
        unit = lax.broadcasted_iota(jnp.int32, (edge, inner_lanes), 0)
        unit = lax.broadcasted_iota(jnp.int32, (edge, inner_lanes), 1) - unit
        gl = jnp.zeros((edge, inner_lanes), f32)
        gr = gl
        for level in reversed(range(x_levels)):
            is_right = bit(my_column(), level) == 1
            keep = keep_ref[level][...]
            keep_out[:, level * edge : (level + 1) * edge] = jnp.where(
                is_right, keep[:, edge:], keep[:, :edge]
            )
            value = jnp.where(unit == level * edge, 1.0, 0.0)
            if level < x_levels - 1:
                end = ends_ref[level][...]
                end = jnp.where(is_right, end[edge:], end[:edge])
                value = value + dot(end, jnp.concatenate([gl, gr], axis=0))
            gl = jnp.where(is_right, value, gl)
            gr = jnp.where(is_right, gr, value)
        none = jnp.zeros((edge, inner_lanes), f32)
        out_map = lo_ref[...]
        added = dot(out_map, jnp.concatenate([none, gr, none, gl], axis=0))
        none = jnp.zeros((pair, leaf), f32)
        chain_out[...] = jnp.concatenate(
            [
                jnp.concatenate([out_map, added], axis=1),
                jnp.concatenate([none, jnp.concatenate([gr, gl], axis=0)], axis=1),
            ],
            axis=0,
        )
        g = with_row_edge(0, g_ref[...], w_ref[...], 0.0)
        row = []
        for c in range(cols):
            held = held_of(c, held_ref, moved_ref)[:in_rows]
            row.append(
                jnp.concatenate(
                    [held[:, i * in_lanes : (i + 1) * in_lanes] for i in range(runs)], axis=0
                )
            )
        matrix_out[...] = jnp.zeros_like(matrix_out)
        for k in range(x_levels):
            known = dot_t(g, xi_ref[k])
            for node in range(cols >> (k + 1)):
                start = node_starts[k] + node * pair
                inside = my_column() >> (k + 1) == node
                known_out[:, start : start + pair] = jnp.where(inside, known, 0.0)
                for c in range(node << (k + 1), (node + 1) << (k + 1)):
                    matrix_out[start : start + pair, c * edge : (c + 1) * edge] = edge_of(row[c], k)

    def x_terms_body(own_ref, got_ref, matrix_ref, known_ref, *refs):
        out_ref = refs[-1]
        q = own_ref[...] + got_ref[...]
        terms = dot_t(q, matrix_ref[...]) + known_ref[...]
        if whole_solve:
            g_ref, half_ref, other_half_ref, xi_ref, g_out, _ = refs
            odd_row = bit(my_row(), 0) == 1
            mine, other = half_ref[...], other_half_ref[...]
            value = jnp.concatenate(
                [jnp.where(odd_row, other, mine), jnp.where(odd_row, mine, other)], axis=0
            )
            none = jnp.zeros_like(value)
            upper = jnp.concatenate(
                [
                    jnp.where(my_row() == 2, value, 0.0),
                    none,
                    jnp.where(my_row() == 1, value, 0.0),
                    none,
                ],
                axis=1,
            )
            g_out[...] = g_ref[...] + upper
            added = dot_t(upper, xi_ref[...].reshape(x_levels * pair, leaf))
        for c in range(cols):
            picked = []
            for k in range(x_levels):
                start = node_starts[k] + (c >> (k + 1)) * pair + bit(c, k) * edge
                piece = terms[:, start : start + edge]
                if whole_solve:
                    inside = my_column() >> (k + 1) == c >> (k + 1)
                    piece = piece + jnp.where(inside, edge_of(added, 2 * k + bit(c, k)), 0.0)
                picked.append(piece)
            out_ref[c] = pad_lanes(jnp.concatenate(picked + [edge_of(q, c)], axis=1), x_lanes)

    def finish_body(g_ref, w_ref, h0_ref, got_ref, chain_ref, keep_ref, g_out, t_out, *faces):
        q = jnp.sum(got_ref[...], axis=0)
        g = with_row_edge(0, g_ref[...], w_ref[...], edge_of(q, x_levels))
        terms = q[:, :inner_lanes] + keep_ref[...]
        result = dot_t(jnp.concatenate([g, terms], axis=1), chain_ref[...])
        gr, gl = edge_of(result, 4), edge_of(result, 5)
        g = jnp.concatenate(
            [edge_of(g, 0), edge_of(g, 1) + gr, edge_of(g, 2), edge_of(g, 3) + gl], axis=1
        )
        g_out[...] = g
        t = g - (result[:, :leaf] + h0_ref[...])
        t_out[...] = t
        odd_col = bit(my_column(), 0) == 1
        odd_row = bit(my_row(), 0) == 1
        bottom, right, top, left = (packed(edge_of(t, i), edge) for i in range(4))
        faces[0][...] = jnp.where(odd_col, left, right)
        faces[1][...] = jnp.where(odd_col, right, left)
        faces[2][...] = jnp.where(odd_row, bottom, top)
        faces[3][...] = jnp.where(odd_row, top, bottom)

    def trace_body(t_ref, a_ref, b_ref, c_ref, d_ref, out_ref):
        t = t_ref[...]
        odd_col = bit(my_column(), 0) == 1
        odd_row = bit(my_row(), 0) == 1
        near_x, far_x, near_y, far_y = (
            unpacked(ref[...], edge) for ref in (a_ref, b_ref, c_ref, d_ref)
        )
        east = jnp.where(odd_col, far_x, near_x)
        west = jnp.where(odd_col, near_x, far_x)
        north = jnp.where(odd_row, far_y, near_y)
        south = jnp.where(odd_row, near_y, far_y)

        def mean(shared, own, other):
            return jnp.where(shared, 0.5 * (own + other), own)

        trace = jnp.concatenate(
            [
                mean(my_row() > 0, edge_of(t, 0), south),
                mean(my_column() < cols - 1, edge_of(t, 1), east),
                mean(my_row() < rows - 1, edge_of(t, 2), north),
                mean(my_column() > 0, edge_of(t, 3), west),
            ],
            axis=1,
        )
        out_ref[...] = trace.reshape(out_ref.shape)

    face = (waves * edge // LANES, LANES)
    offer, *upper_face = fused(
        functools.partial(offer_body, 0), [offer_shape(0)] + [face] * whole_solve, h
    )
    y_keep = []
    for level in range(y_levels):
        if whole_solve:
            axes = "box" if level == 0 else group(1)
            got = lax.all_to_all(offer, axes, 0, 0, tiled=True)
            if level == 0:
                (upper_face,) = upper_face
                mine, upper_face, second = fused(
                    functools.partial(half_body, 0),
                    [(waves, iface), upper_face.shape, held_shape(4, in_rows, solve_rows)],
                    got,
                    held,
                    moved,
                    upper_held,
                    upper_moved,
                    upper_face,
                    scratch=[(waves, cols * edge)],
                    aliases={5: 1},
                )
                other_face = lax.ppermute(upper_face, core, swapped)
                second_moved = passed_on(second, steps[2])
            else:
                (mine,) = fused(
                    functools.partial(half_body, 1),
                    [(waves, iface)],
                    got,
                    second,
                    second_moved,
                    scratch=[(waves, cols * edge)],
                )
            other = lax.ppermute(mine, core, swapped)
            if level == 0:
                h, w, offer = fused(
                    whole_body,
                    [(waves, leaf), (waves, pair), offer_shape(1)],
                    h,
                    mine,
                    other,
                    yo_all,
                    upper_face,
                    other_face,
                    *other_side,
                )
            else:
                w, g, terms = fused(
                    functools.partial(turn_body, level),
                    [(waves, pair), (waves, leaf), terms_shape(level)],
                    h,
                    mine,
                    other,
                    yo_all,
                    yi_all,
                    reflect[0],
                )
            y_keep.append(w)
            continue
        share = waves // span(level)
        (w_offer,) = fused(
            functools.partial(solve_body, level),
            [(span(level) * cols, share * pair // LANES, LANES)],
            swap(offer, level),
            *ys_all,
            scratch=[(share, iface)],
        )
        got = swap(w_offer, level)
        if level < y_levels - 1:
            h, w, offer = fused(
                functools.partial(spread_body, level),
                [(waves, leaf), (waves, pair), offer_shape(level + 1)],
                h,
                got,
                yo_all,
                scratch=[(waves, iface)],
            )
        else:
            w, g, terms = fused(
                functools.partial(turn_body, level),
                [(waves, pair), (waves, leaf), terms_shape(level)],
                h,
                got,
                yo_all,
                yi_all,
                reflect[0],
                scratch=[(waves, iface)],
            )
        y_keep.append(w)
    for level in reversed(range(1, 1 if whole_solve else y_levels)):
        (total,) = fused(sum_body, [terms_shape(level)[1:]], swap(terms, level))
        total = collect(total, level)
        if level > 1:
            g, terms = fused(
                functools.partial(row_down_body, level),
                [(waves, leaf), terms_shape(level - 1)],
                g,
                y_keep[level],
                total,
                yi_all,
            )
    share = (waves, iface // 2)
    if whole_solve:
        own, other, half = fused(
            upper_body,
            [share, share, (waves // 2, edge)],
            swap(terms, 1),
            g,
            y_keep[1],
            yi_all,
            *side,
            *other_side,
        )
    else:
        g, own, other = fused(
            split_body, [(waves, leaf), share, share], g, y_keep[1], total, yi_all
        )
    got = lax.ppermute(other, core, swapped)
    matrix, known, chain, keep = fused(
        prepare_body,
        [
            (node_lanes, cols * edge),
            (waves, node_lanes),
            (leaf + pair, leaf + inner_lanes),
            (waves, inner_lanes),
        ],
        g,
        y_keep[0],
        xi_all,
        *((second, second_moved) if whole_solve else (held, moved)),
        out_map,
        *x_keep,
        *ends,
    )
    upper = []
    if whole_solve:
        upper = [g, half, lax.ppermute(half, core, swapped), xi_all]
    *g_now, terms = fused(
        x_terms_body,
        [(waves, leaf)] * whole_solve + [(cols, waves, x_lanes)],
        own,
        got,
        matrix,
        known,
        *upper,
    )
    g = g_now[0] if g_now else g
    got = lax.all_to_all(terms, "box", 0, 0, tiled=True)
    g, t, *faces = fused(
        finish_body,
        [(waves, leaf), (waves, leaf)] + [face] * 4,
        g,
        y_keep[0],
        h0,
        got,
        chain,
        keep,
    )

    def near(count):
        return [(i, i ^ 1) for i in range(count)]

    def far(count):
        one_way = [(i, i + 1) for i in range(1, count - 1, 2)]
        return one_way + [(j, i) for i, j in one_way]

    seen = [
        lax.ppermute(faces[0], "box", near(cols)),
        lax.ppermute(faces[1], "box", far(cols)),
        lax.ppermute(faces[2], row_axes, near(rows)),
        lax.ppermute(faces[3], row_axes, far(rows)),
    ]
    def field_body(g_ref, map_ref, from_load_ref, out_ref):
        field = from_load_ref[...] + dot_t(g_ref[...], map_ref[...])
        out_ref[...] = field.reshape(out_ref.shape)

    (field_vals,) = fused(
        field_body, [(waves, 1, 1, inner)], g, field_edges, from_load
    )
    (edge_trace,) = fused(trace_body, [(waves, 1, 1, leaf)], t, *seen)
    return field_vals, edge_trace


def solution(mesh):
    rows, cols = mesh.devices.shape
    bits = rows.bit_length() - 1
    row_axes = tuple(f"row{i}" for i in reversed(range(bits)))
    split = Mesh(mesh.devices.reshape((2,) * bits + (cols,)), row_axes + ("box",))
    late = P(None, row_axes, "box")
    early = P(row_axes, "box")
    return jax.shard_map(
        functools.partial(local, row_axes),
        mesh=split,
        in_specs=(late, early, early, early) + (late,) * 6 + (early,),
        out_specs=(late, late),
        check_vma=False,
    )
```

```python
import functools
import math

import jax
import jax.numpy as jnp
from jax import lax
from jax.experimental import pallas as pl
from jax.experimental.pallas import tpu as pltpu
from jax.sharding import Mesh, PartitionSpec as P

f32 = jnp.float32
LANES = 128
START_ROOM = 60 << 20


def dot(a, b, over=0):
    dims = (((1,), (over,)), ((), ()))

    def parts(x):
        high = x.astype(jnp.bfloat16)
        return high, (x - high.astype(f32)).astype(jnp.bfloat16)

    def product(x, y):
        return lax.dot_general(x, y, dims, preferred_element_type=f32)

    a_high, a_low = parts(a)
    b_high, b_low = parts(b)
    both = product(jnp.concatenate([a_high, a_low], axis=0), b_high)
    return both[: a.shape[0]] + (product(a_high, b_low) + both[a.shape[0] :])


def dot_t(a, b):
    return dot(a, b, 1)


def fused(body, outs, *args, scratch=(), aliases=None):
    vmem = pl.BlockSpec(memory_space=pltpu.VMEM)
    return pl.pallas_call(
        body,
        out_shape=[pltpu.VMEM(s, f32) for s in outs],
        in_specs=[vmem] * len(args),
        out_specs=[vmem] * len(outs),
        scratch_shapes=[pltpu.VMEM(s, f32) for s in scratch],
        input_output_aliases=aliases or {},
        compiler_params=pltpu.CompilerParams(vmem_limit_bytes=12 << 20),
    )(*args)


def packed(x, width):
    runs = LANES // width
    rows = x.shape[0] // runs
    return jnp.concatenate([x[i * rows : (i + 1) * rows] for i in range(runs)], axis=1)


def unpacked(x, width):
    return jnp.concatenate(
        [x[:, i * width : (i + 1) * width] for i in range(x.shape[1] // width)], axis=0
    )


def pad_lanes(x, lanes):
    if x.shape[1] == lanes:
        return x
    return jnp.concatenate([x, jnp.zeros((x.shape[0], lanes - x.shape[1]), f32)], axis=1)


def local(
    row_axes,
    load,
    leaf_load_map,
    leaf_out_map,
    leaf_field_map,
    x_solve,
    x_out,
    x_in,
    y_solve,
    y_out,
    y_in,
    reflect,
):
    edge = leaf_out_map.shape[-1] // 4
    cols = lax.axis_size("box")
    rows = 1
    for axis in row_axes:
        rows *= lax.axis_size(axis)
    x_levels = x_solve.shape[0]
    y_levels = y_solve.shape[0]
    waves = load.shape[0]
    leaf = 4 * edge
    pair = 2 * edge
    iface = cols * pair
    load_here = load[:, 0, 0, :]
    inner = load_here.shape[1]

    def my_column():
        return lax.axis_index("box")

    def my_row():
        return lax.axis_index(row_axes)

    def bit(value, level):
        return (value >> level) & 1

    def edge_of(x, number):
        return x[:, number * edge : (number + 1) * edge]

    def exchange_shape(level):
        kept = x_levels - 1 - level
        lanes = (2 + 2 * kept) * edge
        return (pair, -(-lanes // LANES) * LANES)

    def pieces_of(x, first, count):
        return [edge_of(x, first + i) for i in range(count)]

    whole_solve = (x_levels, y_levels) == (3, 2) and iface * iface <= 1 << 18
    in_lanes = -(-x_levels * edge // LANES) * LANES
    width = iface if whole_solve else 4 * in_lanes
    runs = width // in_lanes
    in_rows = pair // runs
    solve_rows = edge if whole_solve else 0

    def held_shape(count, *parts):
        return (count, sum(parts), width)

    def passed_on(held, bit_no):
        return lax.ppermute(held, "box", [(i, i ^ (1 << bit_no)) for i in range(cols)])

    steps = [x_levels - 1] + list(range(x_levels - 1))
    joined_at = [0] + list(range(2, x_levels))

    def held_of(c, held_ref, moved_ref):
        place = sum(bit(c, b) << k for k, b in enumerate(steps[:-1]))
        same = bit(my_column(), steps[-1]) == bit(c, steps[-1])
        return jnp.where(same, held_ref[place], moved_ref[place])

    def join(step, held, moved, both_ref):
        high = bit(my_column(), steps[step]) == 1
        both_ref[: 1 << step] = jnp.where(high, moved, held)
        both_ref[1 << step :] = jnp.where(high, held, moved)

    def placing(body, shapes, *args, scratch=(), live=0):
        return pl.pallas_call(
            body,
            out_shape=[pltpu.VMEM(s, f32) for s in shapes],
            in_specs=[pl.BlockSpec(memory_space=pl.ANY)] * len(args),
            out_specs=[pl.BlockSpec(memory_space=pltpu.VMEM)] * len(shapes),
            scratch_shapes=[pltpu.VMEM(s, f32) for s in scratch]
            + [pltpu.SemaphoreType.DMA((len(args) + 1,))],
            compiler_params=pltpu.CompilerParams(
                vmem_limit_bytes=START_ROOM - live - sum(4 * math.prod(s) for s in shapes)
            ),
        )(*args)

    def hold_body(solve_any, xi_any, *refs):
        *held_refs, solve, xi, sems = refs
        copies = [
            pltpu.make_async_copy(solve_any, solve, sems.at[0]),
            pltpu.make_async_copy(xi_any, xi, sems.at[1]),
        ]
        for copy in copies:
            copy.start()
        for copy in copies:
            copy.wait()
        odd_row = bit(my_row(), 0) == 1
        row_in = pad_lanes(
            jnp.concatenate(
                [
                    jnp.where(odd_row, edge_of(xi[k], 0), edge_of(xi[k], 2))
                    for k in range(x_levels)
                ],
                axis=1,
            ),
            in_lanes,
        )
        held_refs[-1][0, :in_rows] = jnp.concatenate(
            [row_in[i * in_rows : (i + 1) * in_rows] for i in range(runs)], axis=1
        )
        if whole_solve:
            for level, held_ref in enumerate(held_refs[:2]):
                low, high = (
                    jnp.concatenate(
                        [edge_of(solve[level], 2 * c + side) for c in range(cols)], axis=1
                    )
                    for side in range(2)
                )
                mine = jnp.where(odd_row == (level == 0), high, low)
                start = in_rows * level
                held_ref[0, start : start + edge] = jnp.concatenate(
                    [mine[:edge], mine[edge:]], axis=1
                )

    ys_here, xi_here = y_solve[:, 0, 0], x_in[:, 0, 0]
    held, *upper_held = placing(
        hold_body,
        [held_shape(1, solve_rows)] * whole_solve + [held_shape(1, in_rows, solve_rows)],
        ys_here,
        xi_here,
        scratch=[ys_here.shape, xi_here.shape],
    )

    columns_here = [x[:, 0, 0] for x in (jnp.swapaxes(x_out, 3, 4), x_in, x_solve)]
    rows_here = [x[:, 0, 0] for x in (y_out, y_in)] + [leaf_out_map[0, 0]]
    if not whole_solve:
        rows_here.append(ys_here)

    def start_body(load_any, map_any, xo_any, xi_any, xs_any, h_ref, out_ref, load_out, *refs):
        xo, xi, xs, load_v, map_v, sems = refs
        pairs = zip((load_any, map_any, xo_any, xi_any, xs_any), (load_v, map_v, xo, xi, xs))
        copies = [pltpu.make_async_copy(a, b, sems.at[i]) for i, (a, b) in enumerate(pairs)]
        for copy in copies:
            copy.start()
        copies[0].wait()
        copies[1].wait()
        loaded = load_v[...].reshape(waves, inner)
        load_out[...] = loaded
        h = dot_t(loaded, map_v[...])
        h_ref[...] = h
        copies[2].wait()
        copies[3].wait()
        is_right = bit(my_column(), 0) == 1
        travelling = [
            jnp.where(is_right, edge_of(x[k], 1), edge_of(x[k], 3))
            for x in (xi, xo)
            for k in range(x_levels - 1)
        ]
        out_ref[...] = pad_lanes(
            jnp.concatenate([edge_of(h, 3), edge_of(h, 1)] + travelling, axis=1), out_ref.shape[1]
        )
        copies[4].wait()

    h0, to_send, loaded, xo_all, xi_all, xs_all = placing(
        start_body,
        [(waves, leaf), exchange_shape(0), (waves, inner)] + [x.shape for x in columns_here],
        load,
        leaf_load_map[0, 0],
        *columns_here,
        scratch=[load.shape, (leaf, inner)],
    )

    def place_body(field_any, *refs):
        *refs, sems = refs
        count = len(rows_here)
        sources = [field_any.at[:, pl.ds(0, leaf)], field_any.at[:, pl.ds(leaf, inner)]]
        pairs = zip(sources + list(refs[:count]), refs[count:])
        copies = [pltpu.make_async_copy(a, b, sems.at[i]) for i, (a, b) in enumerate(pairs)]
        for copy in copies:
            copy.start()
        for copy in copies:
            copy.wait()

    field_edges, field_inner, yo_all, yi_all, out_map, *ys_all = placing(
        place_body,
        [(inner, leaf), (inner, inner)] + [x.shape for x in rows_here],
        leaf_field_map[0, 0],
        *rows_here,
        live=2 << 20,
    )

    side_rows = iface * edge // LANES

    def at_upper():
        return (my_row() == 1) | (my_row() == 2)

    def upper_edge(x):
        return jnp.where(my_row() == 1, x[2 * edge : 3 * edge], x[:edge])

    def aside_body(load_ref, map_ref, yi_ref, yo_ref, out_ref, *side_ref):
        out_ref[...] = dot_t(load_ref[...], map_ref[...])
        for ref in side_ref:
            ref[:side_rows] = packed(
                jnp.where(my_row() == 1, edge_of(yi_ref[0], 2), edge_of(yi_ref[0], 0)), edge
            )
            out_rows = upper_edge(yo_ref[0])
            ref[side_rows:] = jnp.concatenate(
                [out_rows[:, i * LANES : (i + 1) * LANES] for i in range(iface // LANES)], axis=0
            )

    from_load, *side = fused(
        aside_body,
        [(waves, inner)] + [(2 * side_rows, LANES)] * whole_solve,
        loaded,
        field_inner,
        yi_all,
        yo_all,
    )

    core = row_axes[-1]
    swapped = [(0, 1), (1, 0)]

    def group(level):
        return tuple(row_axes[y_levels - 1 - level :]) + ("box",)

    def span(level):
        return 2 << level

    def swap(x, level):
        return lax.all_to_all(x, group(level), 0, 0, tiled=True)

    def offer_shape(level):
        if whole_solve:
            return (rows**level * cols, (waves >> level) * edge // LANES, LANES)
        return (span(level) * cols, waves // span(level) * edge // LANES, LANES)

    def store_offer(level, h, out):
        size = span(level)
        share = waves // size
        facing = jnp.where(
            lax.rem(my_row(), size) == size // 2 - 1, edge_of(h, 2), edge_of(h, 0)
        )
        if whole_solve:
            out[...] = jnp.broadcast_to(packed(facing, edge), out.shape)
            return
        for target in range(size):
            piece = packed(facing[target * share : (target + 1) * share], edge)
            out[target * cols : (target + 1) * cols] = jnp.broadcast_to(piece, (cols,) + piece.shape)

    def x_body(level, tasks, h_ref, own_ref, got_ref, solve_ref, xo_ref, *refs):
        kept = x_levels - 1 - level
        count = sum(len(args) for _, args, _ in tasks)
        ins, (h_out, w_out, *rest) = refs[:count], refs[count:]
        rest, outs = rest[: 2 if kept else 0], rest[2 if kept else 0 :]
        offer_ref = outs[-1] if outs else None
        for task, args, shapes in tasks:
            task(*ins[: len(args)], *outs[: len(shapes)])
            ins, outs = ins[len(args) :], outs[len(shapes) :]
        is_right = bit(my_column(), level) == 1
        own, got = own_ref[...], got_ref[...]
        left_child = jnp.where(is_right, got, own)
        right_child = jnp.where(is_right, own, got)
        v = jnp.concatenate([edge_of(left_child, 1), edge_of(right_child, 0)], axis=1)
        w = dot_t(v, solve_ref[level])
        w_out[...] = w
        if kept:
            next_ref, ends_ref = rest
            outer = [edge_of(x, 2 + kept) for x in (left_child, right_child)]
            spread = dot(w, jnp.concatenate([xo_ref[level]] + outer, axis=1))
            h_out[...] = h_ref[...] + spread[:, :leaf]
            left = edge_of(left_child, 0) + edge_of(spread, 4)
            right = edge_of(right_child, 1) + edge_of(spread, 5)
            ends_ref[...] = jnp.concatenate(
                [edge_of(left_child, 2), edge_of(right_child, 2)], axis=1
            )
            mine = jnp.where(bit(my_column(), level + 1) == 1, right_child, left_child)
            travelling = pieces_of(mine, 3, kept - 1) + pieces_of(mine, 3 + kept, kept - 1)
            next_ref[...] = pad_lanes(
                jnp.concatenate([left, right] + travelling, axis=1), next_ref.shape[1]
            )
        else:
            h = h_ref[...] + dot(w, xo_ref[level])
            h_out[...] = h
            if whole_solve:
                store_offer(0, h, offer_ref)

    def nothing(*refs):
        pass

    def join_upper(held_ref, moved_ref, both_ref):
        kept = in_rows + solve_rows
        join(0, held_ref[...], moved_ref[...], both_ref.at[:, :kept])
        both_ref[:, kept:] = jnp.zeros((2, in_rows, width), f32)

    def join_plain(step, held_ref, moved_ref, both_ref):
        join(step, held_ref[...], moved_ref[...], both_ref)

    h = h0
    x_keep, ends = [], []
    moved = passed_on(held, steps[0])
    upper_moved = [passed_on(x, steps[0]) for x in upper_held]
    for level in range(x_levels):
        got = lax.ppermute(to_send, "box", [(i, i ^ (1 << level)) for i in range(cols)])
        outs = [(waves, leaf), (waves, pair)]
        if level < x_levels - 1:
            outs += [exchange_shape(level + 1), (pair, pair)]
        args = [h, to_send, got, xs_all, xo_all]
        tasks = []
        if level < 2:
            tasks.append((nothing, [(out_map, from_load)[level]], []))
        if whole_solve and level == 0:
            shapes = [held_shape(2, solve_rows)]
            tasks.append((functools.partial(join_plain, 0), [held, moved], shapes))
        elif whole_solve and level == 1:
            tasks.append((nothing, side, [x.shape for x in side]))
            shapes = [held_shape(2, in_rows, solve_rows, in_rows)]
            tasks.append((join_upper, upper_held + upper_moved, shapes))
        elif whole_solve:
            tasks.append((nothing, other_side, []))
            shapes = [held_shape(4, solve_rows)]
            tasks.append((functools.partial(join_plain, 1), [held, moved], shapes))
            tasks.append((nothing, [], [offer_shape(0)]))
        elif level in joined_at:
            step = joined_at.index(level)
            shape = held_shape(2 << step, in_rows)
            tasks.append((functools.partial(join_plain, step), [held, moved], [shape]))
        aliases = {len(args) + 1: len(outs)} if level == 1 and whole_solve else None
        h, w, *rest = fused(
            functools.partial(x_body, level, tasks),
            outs + [shape for task in tasks for shape in task[2]],
            *args,
            *(x for task in tasks for x in task[1]),
            aliases=aliases,
        )
        x_keep.append(w)
        if level < x_levels - 1:
            to_send, end, *rest = rest
            ends.append(end)
        if whole_solve and level == 0:
            (held,) = rest
            moved = passed_on(held, steps[1])
        elif whole_solve and level == 1:
            side, upper_held = rest[:1], rest[1]
            upper_moved = passed_on(upper_held, steps[1])
            other_side = [lax.ppermute(x, core, swapped) for x in side]
        elif whole_solve:
            held, offer = rest
            moved = passed_on(held, steps[2])
        elif level in joined_at:
            (held,) = rest
            moved = passed_on(held, steps[step + 1])

    def offer_body(level, h_ref, out_ref):
        store_offer(level, h_ref[...], out_ref)

    def folded(x):
        return jnp.concatenate([x[i : i + 8] for i in range(0, x.shape[0], 8)], axis=1)

    def unfolded(x, rows):
        return jnp.concatenate([edge_of(x, i) for i in range(rows // 8)], axis=0)

    def gather_v(level, got_ref, v_ref):
        size = span(level)
        low = (size // 2 - 1) * cols
        run = got_ref.shape[1]
        for side in range(2):
            for c in range(cols):
                piece = got_ref[low + side * cols + c]
                for k in range(LANES // edge):
                    start = c * pair + side * edge
                    v_ref[k * run : (k + 1) * run, start : start + edge] = edge_of(piece, k)

    def solve_body(level, got_ref, solve_ref, out_ref, v_ref):
        gather_v(level, got_ref, v_ref)
        w = packed(dot_t(v_ref[...], solve_ref[level]), pair)
        out_ref[...] = jnp.broadcast_to(w, out_ref.shape)

    def own_columns(w_all):
        own = w_all[:, :pair]
        for c in range(1, cols):
            own = jnp.where(my_column() == c, w_all[:, c * pair : (c + 1) * pair], own)
        return own

    def gather_w(level, got_ref, w_ref):
        size = span(level)
        share = waves // size
        run = got_ref.shape[1]
        for target in range(size):
            for c in range(cols):
                piece = got_ref[target * cols + c]
                for k in range(LANES // pair):
                    start = target * share + k * run
                    w_ref[start : start + run, c * pair : (c + 1) * pair] = piece[
                        :, k * pair : (k + 1) * pair
                    ]
        return w_ref[...]

    def upper_face(h_ref):
        return jnp.where(my_row() == 1, edge_of(h_ref[...], 2), edge_of(h_ref[...], 0))

    def half_body(level, got_ref, held_ref, moved_ref, *refs):
        if level == 0:
            upper_held_ref, upper_moved_ref, h_ref, out_ref, face_ref, upper_ref, v_ref = refs
            face_ref[...] = packed(upper_face(h_ref), edge)
            kept = in_rows + solve_rows
            join(1, upper_held_ref[:, :kept], upper_moved_ref[:, :kept], upper_ref)
        else:
            out_ref, v_ref = refs
        odd_row = bit(my_row(), 0) == 1
        run = got_ref.shape[1]
        for c in range(cols):
            for part in range(1 + level):
                piece = got_ref[part * cols + c]
                if level == 1:
                    piece = jnp.where(odd_row, piece, got_ref[(2 + part) * cols + c])
                for k in range(LANES // edge):
                    start = (part * LANES // edge + k) * run
                    v_ref[start : start + run, c * edge : (c + 1) * edge] = edge_of(piece, k)
        solve = []
        for c in range(cols):
            start = in_rows * level
            block = held_of(c, held_ref, moved_ref)[start : start + edge]
            solve += [block[:, : iface // 2], block[:, iface // 2 :]]
        out_ref[...] = dot_t(v_ref[...], jnp.concatenate(solve, axis=0))

    def whole_body(h_ref, mine_ref, other_ref, yo_ref, face_ref, side_ref, h_out, w_out, next_ref):
        w_all = mine_ref[...] + other_ref[...]
        w_out[...] = own_columns(w_all)
        out_rows = side_ref[side_rows:]
        out_rows = jnp.concatenate(
            [out_rows[i * edge : (i + 1) * edge] for i in range(iface // LANES)], axis=1
        )
        out_rows = jnp.where(at_upper(), upper_edge(yo_ref[0]), out_rows)
        spread = dot_t(w_all, jnp.concatenate([yo_ref[0], out_rows], axis=0))
        h_out[...] = h_ref[...] + spread[:, :leaf]
        face = jnp.where(at_upper(), upper_face(h_ref), unpacked(face_ref[...], edge))
        face = face + spread[:, leaf:]
        half = jnp.where(bit(my_row(), 0) == 1, face[waves // 2 :], face[: waves // 2])
        next_ref[...] = jnp.broadcast_to(packed(half, edge), next_ref.shape)

    def spread_body(level, h_ref, got_ref, yo_ref, h_out, w_out, next_ref, w_ref):
        w_all = gather_w(level, got_ref, w_ref)
        w_out[...] = own_columns(w_all)
        h = h_ref[...] + dot_t(w_all, yo_ref[level])
        h_out[...] = h
        store_offer(level + 1, h, next_ref)

    def halves(level):
        return span(level) // 2

    def terms_shape(level):
        return (span(level) * cols, waves // halves(level) * edge // LANES, LANES)

    def store_terms(level, g, yi_ref, out):
        terms = dot_t(g, yi_ref[level])
        half = halves(level)
        share = waves // half
        for side in range(2):
            for c in range(cols):
                start = c * pair + side * edge
                piece = terms[:, start : start + edge]
                for part in range(half):
                    out[(side * half + part) * cols + c] = packed(
                        piece[part * share : (part + 1) * share], edge
                    )

    def turn_body(level, h_ref, got_ref, *refs):
        if whole_solve:
            other_ref, yo_ref, yi_ref, reflect_ref, w_out, g_out, out_ref = refs
            w_all = got_ref[...] + other_ref[...]
        else:
            yo_ref, yi_ref, reflect_ref, w_out, g_out, out_ref, w_ref = refs
            w_all = gather_w(level, got_ref, w_ref)
        w_out[...] = own_columns(w_all)
        h = h_ref[...] + dot_t(w_all, yo_ref[level])
        lane = lax.broadcasted_iota(jnp.int32, (1, leaf), 1)

        def side(number):
            return (lane >= number * edge) & (lane < (number + 1) * edge)

        outer = (
            side(0) & (my_row() == 0)
            | side(1) & (my_column() == cols - 1)
            | side(2) & (my_row() == rows - 1)
            | side(3) & (my_column() == 0)
        )
        g = jnp.where(outer, h * reflect_ref[...], 0.0)
        g_out[...] = g
        store_terms(level, g, yi_ref, out_ref)

    def sum_body(got_ref, out_ref):
        out_ref[...] = jnp.sum(got_ref[...], axis=0)

    def with_row_edge(level, g, w, q):
        size = span(level)
        place = lax.rem(my_row(), size)
        is_low = place == size // 2 - 1
        is_high = place == size // 2
        value = jnp.where(place < size // 2, w[:, :edge], w[:, edge:]) + q
        bottom = jnp.where(is_high, value, edge_of(g, 0))
        top = jnp.where(is_low, value, edge_of(g, 2))
        return jnp.concatenate([bottom, edge_of(g, 1), top, edge_of(g, 3)], axis=1)

    def row_down_body(level, g_ref, w_ref, sum_ref, yi_ref, g_out, out_ref):
        g = with_row_edge(level, g_ref[...], w_ref[...], unpacked_parts(level, sum_ref))
        g_out[...] = g
        store_terms(level - 1, g, yi_ref, out_ref)

    def unpacked_parts(level, sum_ref):
        run = waves // halves(level) * edge // LANES
        return jnp.concatenate(
            [unpacked(sum_ref[i * run : (i + 1) * run], edge) for i in range(halves(level))], axis=0
        )

    def collect(total, level):
        for axis_no in range(level):
            axis = row_axes[y_levels - 1 - axis_no]
            other = lax.ppermute(total, axis, [(0, 1), (1, 0)])
            first = lax.axis_index(axis) == 0
            total = jnp.concatenate(
                [jnp.where(first, total, other), jnp.where(first, other, total)], axis=0
            )
        return total

    x_lanes = -(-(x_levels + 1) * edge // LANES) * LANES

    def sides_of(terms):
        low, high = (
            jnp.concatenate([edge_of(terms, 2 * c + side) for c in range(cols)], axis=1)
            for side in range(2)
        )
        odd_row = bit(my_row(), 0) == 1
        return jnp.where(odd_row, high, low), jnp.where(odd_row, low, high)

    def split_body(g_ref, w_ref, sum_ref, yi_ref, g_out, own_out, other_out):
        g = with_row_edge(1, g_ref[...], w_ref[...], unpacked_parts(1, sum_ref))
        g_out[...] = g
        own_out[...], other_out[...] = sides_of(dot_t(g, yi_ref[0]))

    def upper_body(got_ref, g_ref, w_ref, yi_ref, side_ref, other_ref, own_out, other_out, half_out):
        q = unpacked(jnp.sum(got_ref[...], axis=0), edge)
        w = w_ref[...]
        w = jnp.where(my_row() < 2, w[:, :edge], w[:, edge:])
        odd_row = bit(my_row(), 0) == 1
        half = waves // 2
        value = jnp.where(odd_row, w[half:], w[:half]) + q
        half_out[...] = value
        columns = jnp.where(at_upper(), side_ref[:side_rows], other_ref[:side_rows])
        columns = unpacked(columns, edge)
        added = dot_t(value, columns)
        terms = dot_t(g_ref[...], yi_ref[0])
        terms = jnp.concatenate(
            [
                terms[:half] + jnp.where(odd_row, 0.0, added),
                terms[half:] + jnp.where(odd_row, added, 0.0),
            ],
            axis=0,
        )
        own_out[...], other_out[:waves] = sides_of(terms)
        other_out[waves:] = jnp.zeros((8, iface // 2), f32)
        other_out[waves:, : half // 8 * edge] = folded(value)

    node_starts = []
    for k in range(x_levels):
        node_starts.append(sum(cols >> (i + 1) for i in range(k)) * pair)
    node_lanes = (cols - 1) * pair

    inner_lanes = x_levels * edge

    def prepare_body(g_ref, w_ref, xi_ref, held_ref, moved_ref, lo_ref, *refs):
        keep_ref, ends_ref = refs[:x_levels], refs[x_levels : 2 * x_levels - 1]
        matrix_out, known_out, chain_out, keep_out = refs[2 * x_levels - 1 :]
        unit = lax.broadcasted_iota(jnp.int32, (edge, inner_lanes), 0)
        unit = lax.broadcasted_iota(jnp.int32, (edge, inner_lanes), 1) - unit
        gl = jnp.zeros((edge, inner_lanes), f32)
        gr = gl
        for level in reversed(range(x_levels)):
            is_right = bit(my_column(), level) == 1
            keep = keep_ref[level][...]
            keep_out[:, level * edge : (level + 1) * edge] = jnp.where(
                is_right, keep[:, edge:], keep[:, :edge]
            )
            value = jnp.where(unit == level * edge, 1.0, 0.0)
            if level < x_levels - 1:
                end = ends_ref[level][...]
                end = jnp.where(is_right, end[edge:], end[:edge])
                value = value + dot(end, jnp.concatenate([gl, gr], axis=0))
            gl = jnp.where(is_right, value, gl)
            gr = jnp.where(is_right, gr, value)
        none = jnp.zeros((edge, inner_lanes), f32)
        out_map = lo_ref[...]
        added = dot(out_map, jnp.concatenate([none, gr, none, gl], axis=0))
        none = jnp.zeros((pair, leaf), f32)
        chain_out[...] = jnp.concatenate(
            [
                jnp.concatenate([out_map, added], axis=1),
                jnp.concatenate([none, jnp.concatenate([gr, gl], axis=0)], axis=1),
            ],
            axis=0,
        )
        g = with_row_edge(0, g_ref[...], w_ref[...], 0.0)
        row = []
        for c in range(cols):
            held = held_of(c, held_ref, moved_ref)[:in_rows]
            row.append(
                jnp.concatenate(
                    [held[:, i * in_lanes : (i + 1) * in_lanes] for i in range(runs)], axis=0
                )
            )
        matrix_out[...] = jnp.zeros_like(matrix_out)
        for k in range(x_levels):
            known = dot_t(g, xi_ref[k])
            for node in range(cols >> (k + 1)):
                start = node_starts[k] + node * pair
                inside = my_column() >> (k + 1) == node
                known_out[:, start : start + pair] = jnp.where(inside, known, 0.0)
                for c in range(node << (k + 1), (node + 1) << (k + 1)):
                    matrix_out[start : start + pair, c * edge : (c + 1) * edge] = edge_of(row[c], k)

    def x_terms_body(own_ref, got_ref, matrix_ref, known_ref, *refs):
        out_ref = refs[-1]
        q = own_ref[...] + got_ref[:waves]
        terms = dot_t(q, matrix_ref[...]) + known_ref[...]
        if whole_solve:
            g_ref, half_ref, xi_ref, g_out, _ = refs
            odd_row = bit(my_row(), 0) == 1
            mine, other = half_ref[...], unfolded(got_ref[waves:], waves // 2)
            value = jnp.concatenate(
                [jnp.where(odd_row, other, mine), jnp.where(odd_row, mine, other)], axis=0
            )
            none = jnp.zeros_like(value)
            upper = jnp.concatenate(
                [
                    jnp.where(my_row() == 2, value, 0.0),
                    none,
                    jnp.where(my_row() == 1, value, 0.0),
                    none,
                ],
                axis=1,
            )
            g_out[...] = g_ref[...] + upper
            added = dot_t(upper, xi_ref[...].reshape(x_levels * pair, leaf))
        for c in range(cols):
            picked = []
            for k in range(x_levels):
                start = node_starts[k] + (c >> (k + 1)) * pair + bit(c, k) * edge
                piece = terms[:, start : start + edge]
                if whole_solve:
                    inside = my_column() >> (k + 1) == c >> (k + 1)
                    piece = piece + jnp.where(inside, edge_of(added, 2 * k + bit(c, k)), 0.0)
                picked.append(piece)
            out_ref[c] = pad_lanes(jnp.concatenate(picked + [edge_of(q, c)], axis=1), x_lanes)

    def finish_body(g_ref, w_ref, h0_ref, got_ref, chain_ref, keep_ref, g_out, t_out, *faces):
        q = jnp.sum(got_ref[...], axis=0)
        g = with_row_edge(0, g_ref[...], w_ref[...], edge_of(q, x_levels))
        terms = q[:, :inner_lanes] + keep_ref[...]
        result = dot_t(jnp.concatenate([g, terms], axis=1), chain_ref[...])
        gr, gl = edge_of(result, 4), edge_of(result, 5)
        g = jnp.concatenate(
            [edge_of(g, 0), edge_of(g, 1) + gr, edge_of(g, 2), edge_of(g, 3) + gl], axis=1
        )
        g_out[...] = g
        t = g - (result[:, :leaf] + h0_ref[...])
        t_out[...] = t
        odd_col = bit(my_column(), 0) == 1
        odd_row = bit(my_row(), 0) == 1
        bottom, right, top, left = (packed(edge_of(t, i), edge) for i in range(4))
        faces[0][...] = jnp.where(odd_col, left, right)
        faces[1][...] = jnp.where(odd_col, right, left)
        faces[2][...] = jnp.where(odd_row, bottom, top)
        faces[3][...] = jnp.where(odd_row, top, bottom)

    def trace_body(t_ref, a_ref, b_ref, c_ref, d_ref, out_ref):
        t = t_ref[...]
        odd_col = bit(my_column(), 0) == 1
        odd_row = bit(my_row(), 0) == 1
        near_x, far_x, near_y, far_y = (
            unpacked(ref[...], edge) for ref in (a_ref, b_ref, c_ref, d_ref)
        )
        east = jnp.where(odd_col, far_x, near_x)
        west = jnp.where(odd_col, near_x, far_x)
        north = jnp.where(odd_row, far_y, near_y)
        south = jnp.where(odd_row, near_y, far_y)

        def mean(shared, own, other):
            return jnp.where(shared, 0.5 * (own + other), own)

        trace = jnp.concatenate(
            [
                mean(my_row() > 0, edge_of(t, 0), south),
                mean(my_column() < cols - 1, edge_of(t, 1), east),
                mean(my_row() < rows - 1, edge_of(t, 2), north),
                mean(my_column() > 0, edge_of(t, 3), west),
            ],
            axis=1,
        )
        out_ref[...] = trace.reshape(out_ref.shape)

    face = (waves * edge // LANES, LANES)
    if not whole_solve:
        (offer,) = fused(functools.partial(offer_body, 0), [offer_shape(0)], h)
    y_keep = []
    for level in range(y_levels):
        if whole_solve:
            axes = "box" if level == 0 else group(1)
            got = lax.all_to_all(offer, axes, 0, 0, tiled=True)
            if level == 0:
                mine, upper, second = fused(
                    functools.partial(half_body, 0),
                    [(waves, iface), face, held_shape(4, in_rows, solve_rows)],
                    got,
                    held,
                    moved,
                    upper_held,
                    upper_moved,
                    h,
                    scratch=[(waves, cols * edge)],
                )
                upper = lax.ppermute(upper, core, swapped)
                second_moved = passed_on(second, steps[2])
            else:
                (mine,) = fused(
                    functools.partial(half_body, 1),
                    [(waves, iface)],
                    got,
                    second,
                    second_moved,
                    scratch=[(waves, cols * edge)],
                )
            other = lax.ppermute(mine, core, swapped)
            if level == 0:
                h, w, offer = fused(
                    whole_body,
                    [(waves, leaf), (waves, pair), offer_shape(1)],
                    h,
                    mine,
                    other,
                    yo_all,
                    upper,
                    *other_side,
                )
            else:
                w, g, terms = fused(
                    functools.partial(turn_body, level),
                    [(waves, pair), (waves, leaf), terms_shape(level)],
                    h,
                    mine,
                    other,
                    yo_all,
                    yi_all,
                    reflect[0],
                )
            y_keep.append(w)
            continue
        share = waves // span(level)
        (w_offer,) = fused(
            functools.partial(solve_body, level),
            [(span(level) * cols, share * pair // LANES, LANES)],
            swap(offer, level),
            *ys_all,
            scratch=[(share, iface)],
        )
        got = swap(w_offer, level)
        if level < y_levels - 1:
            h, w, offer = fused(
                functools.partial(spread_body, level),
                [(waves, leaf), (waves, pair), offer_shape(level + 1)],
                h,
                got,
                yo_all,
                scratch=[(waves, iface)],
            )
        else:
            w, g, terms = fused(
                functools.partial(turn_body, level),
                [(waves, pair), (waves, leaf), terms_shape(level)],
                h,
                got,
                yo_all,
                yi_all,
                reflect[0],
                scratch=[(waves, iface)],
            )
        y_keep.append(w)
    for level in reversed(range(1, 1 if whole_solve else y_levels)):
        (total,) = fused(sum_body, [terms_shape(level)[1:]], swap(terms, level))
        total = collect(total, level)
        if level > 1:
            g, terms = fused(
                functools.partial(row_down_body, level),
                [(waves, leaf), terms_shape(level - 1)],
                g,
                y_keep[level],
                total,
                yi_all,
            )
    share = (waves, iface // 2)
    if whole_solve:
        own, other, half = fused(
            upper_body,
            [share, (waves + 8, iface // 2), (waves // 2, edge)],
            swap(terms, 1),
            g,
            y_keep[1],
            yi_all,
            *side,
            *other_side,
        )
    else:
        g, own, other = fused(
            split_body, [(waves, leaf), share, share], g, y_keep[1], total, yi_all
        )
    got = lax.ppermute(other, core, swapped)
    matrix, known, chain, keep = fused(
        prepare_body,
        [
            (node_lanes, cols * edge),
            (waves, node_lanes),
            (leaf + pair, leaf + inner_lanes),
            (waves, inner_lanes),
        ],
        g,
        y_keep[0],
        xi_all,
        *((second, second_moved) if whole_solve else (held, moved)),
        out_map,
        *x_keep,
        *ends,
    )
    upper = []
    if whole_solve:
        upper = [g, half, xi_all]
    *g_now, terms = fused(
        x_terms_body,
        [(waves, leaf)] * whole_solve + [(cols, waves, x_lanes)],
        own,
        got,
        matrix,
        known,
        *upper,
    )
    g = g_now[0] if g_now else g
    got = lax.all_to_all(terms, "box", 0, 0, tiled=True)
    g, t, *faces = fused(
        finish_body,
        [(waves, leaf), (waves, leaf)] + [face] * 4,
        g,
        y_keep[0],
        h0,
        got,
        chain,
        keep,
    )

    def near(count):
        return [(i, i ^ 1) for i in range(count)]

    def far(count):
        one_way = [(i, i + 1) for i in range(1, count - 1, 2)]
        return one_way + [(j, i) for i, j in one_way]

    seen = [
        lax.ppermute(faces[0], "box", near(cols)),
        lax.ppermute(faces[1], "box", far(cols)),
        lax.ppermute(faces[2], row_axes, near(rows)),
        lax.ppermute(faces[3], row_axes, far(rows)),
    ]
    def field_body(g_ref, map_ref, from_load_ref, out_ref):
        field = from_load_ref[...] + dot_t(g_ref[...], map_ref[...])
        out_ref[...] = field.reshape(out_ref.shape)

    (field_vals,) = fused(
        field_body, [(waves, 1, 1, inner)], g, field_edges, from_load
    )
    (edge_trace,) = fused(trace_body, [(waves, 1, 1, leaf)], t, *seen)
    return field_vals, edge_trace


def solution(mesh):
    rows, cols = mesh.devices.shape
    bits = rows.bit_length() - 1
    row_axes = tuple(f"row{i}" for i in reversed(range(bits)))
    split = Mesh(mesh.devices.reshape((2,) * bits + (cols,)), row_axes + ("box",))
    late = P(None, row_axes, "box")
    early = P(row_axes, "box")
    return jax.shard_map(
        functools.partial(local, row_axes),
        mesh=split,
        in_specs=(late, early, early, early) + (late,) * 6 + (early,),
        out_specs=(late, late),
        check_vma=False,
    )
```

```python
import functools
import math

import jax
import jax.numpy as jnp
from jax import lax
from jax.experimental import pallas as pl
from jax.experimental.pallas import tpu as pltpu
from jax.sharding import Mesh, PartitionSpec as P

f32 = jnp.float32
LANES = 128
PLACING_VMEM = 60 << 20


def dot(a, b, over=0):
    dims = (((1,), (over,)), ((), ()))

    def parts(x):
        high = x.astype(jnp.bfloat16)
        return high, (x - high.astype(f32)).astype(jnp.bfloat16)

    def product(x, y):
        return lax.dot_general(x, y, dims, preferred_element_type=f32)

    a_high, a_low = parts(a)
    b_high, b_low = parts(b)
    both = product(jnp.concatenate([a_high, a_low], axis=0), b_high)
    return both[: a.shape[0]] + (product(a_high, b_low) + both[a.shape[0] :])


def dot_t(a, b):
    return dot(a, b, 1)


def fused(body, outs, *args, scratch=(), aliases=None):
    vmem = pl.BlockSpec(memory_space=pltpu.VMEM)
    return pl.pallas_call(
        body,
        out_shape=[pltpu.VMEM(s, f32) for s in outs],
        in_specs=[vmem] * len(args),
        out_specs=[vmem] * len(outs),
        scratch_shapes=[pltpu.VMEM(s, f32) for s in scratch],
        input_output_aliases=aliases or {},
        compiler_params=pltpu.CompilerParams(vmem_limit_bytes=12 << 20),
    )(*args)


def packed(x, width):
    runs = LANES // width
    rows = x.shape[0] // runs
    return jnp.concatenate([x[i * rows : (i + 1) * rows] for i in range(runs)], axis=1)


def unpacked(x, width):
    return jnp.concatenate(
        [x[:, i * width : (i + 1) * width] for i in range(x.shape[1] // width)], axis=0
    )


def pad_lanes(x, lanes):
    if x.shape[1] == lanes:
        return x
    return jnp.concatenate([x, jnp.zeros((x.shape[0], lanes - x.shape[1]), f32)], axis=1)


def local(
    row_axes,
    load,
    leaf_load_map,
    leaf_out_map,
    leaf_field_map,
    x_solve,
    x_out,
    x_in,
    y_solve,
    y_out,
    y_in,
    reflect,
):
    edge = leaf_out_map.shape[-1] // 4
    cols = lax.axis_size("box")
    rows = 1
    for axis in row_axes:
        rows *= lax.axis_size(axis)
    x_levels = x_solve.shape[0]
    y_levels = y_solve.shape[0]
    waves = load.shape[0]
    leaf = 4 * edge
    pair = 2 * edge
    iface = cols * pair
    load_here = load[:, 0, 0, :]
    inner = load_here.shape[1]

    def my_column():
        return lax.axis_index("box")

    def my_row():
        return lax.axis_index(row_axes)

    def bit(value, level):
        return (value >> level) & 1

    def edge_of(x, number):
        return x[:, number * edge : (number + 1) * edge]

    def exchange_shape(level):
        kept = x_levels - 1 - level
        lanes = (2 + 2 * kept) * edge
        return (pair, -(-lanes // LANES) * LANES)

    def pieces_of(x, first, count):
        return [edge_of(x, first + i) for i in range(count)]

    whole_solve = (x_levels, y_levels) == (3, 2) and iface * iface <= 1 << 18
    in_lanes = -(-x_levels * edge // LANES) * LANES
    width = iface if whole_solve else 4 * in_lanes
    runs = width // in_lanes
    in_rows = pair // runs
    solve_rows = edge if whole_solve else 0

    def held_shape(count, *parts):
        return (count, sum(parts), width)

    def passed_on(held, bit_no):
        return lax.ppermute(held, "box", [(i, i ^ (1 << bit_no)) for i in range(cols)])

    steps = [x_levels - 1] + list(range(x_levels - 1))
    joined_at = [0] + list(range(2, x_levels))

    def held_of(c, held_ref, moved_ref):
        place = sum(bit(c, b) << k for k, b in enumerate(steps[:-1]))
        same = bit(my_column(), steps[-1]) == bit(c, steps[-1])
        return jnp.where(same, held_ref[place], moved_ref[place])

    def join(step, held, moved, both_ref):
        high = bit(my_column(), steps[step]) == 1
        both_ref[: 1 << step] = jnp.where(high, moved, held)
        both_ref[1 << step :] = jnp.where(high, held, moved)

    def placing(body, shapes, *args, scratch=(), live=0):
        return pl.pallas_call(
            body,
            out_shape=[pltpu.VMEM(s, f32) for s in shapes],
            in_specs=[pl.BlockSpec(memory_space=pl.ANY)] * len(args),
            out_specs=[pl.BlockSpec(memory_space=pltpu.VMEM)] * len(shapes),
            scratch_shapes=[pltpu.VMEM(s, f32) for s in scratch]
            + [pltpu.SemaphoreType.DMA((len(args) + 1,))],
            compiler_params=pltpu.CompilerParams(
                vmem_limit_bytes=PLACING_VMEM - live - sum(4 * math.prod(s) for s in shapes)
            ),
        )(*args)

    def hold_body(solve_any, xi_any, *refs):
        *held_refs, solve, xi, sems = refs
        copies = [
            pltpu.make_async_copy(solve_any, solve, sems.at[0]),
            pltpu.make_async_copy(xi_any, xi, sems.at[1]),
        ]
        for copy in copies:
            copy.start()
        for copy in copies:
            copy.wait()
        odd_row = bit(my_row(), 0) == 1
        row_in = pad_lanes(
            jnp.concatenate(
                [
                    jnp.where(odd_row, edge_of(xi[k], 0), edge_of(xi[k], 2))
                    for k in range(x_levels)
                ],
                axis=1,
            ),
            in_lanes,
        )
        held_refs[-1][0, :in_rows] = jnp.concatenate(
            [row_in[i * in_rows : (i + 1) * in_rows] for i in range(runs)], axis=1
        )
        if whole_solve:
            for level, held_ref in enumerate(held_refs[:2]):
                low, high = (
                    jnp.concatenate(
                        [edge_of(solve[level], 2 * c + side) for c in range(cols)], axis=1
                    )
                    for side in range(2)
                )
                mine = jnp.where(odd_row == (level == 0), high, low)
                start = in_rows * level
                held_ref[0, start : start + edge] = jnp.concatenate(
                    [mine[:edge], mine[edge:]], axis=1
                )

    ys_here, xi_here = y_solve[:, 0, 0], x_in[:, 0, 0]
    held, *upper_held = placing(
        hold_body,
        [held_shape(1, solve_rows)] * whole_solve + [held_shape(1, in_rows, solve_rows)],
        ys_here,
        xi_here,
        scratch=[ys_here.shape, xi_here.shape],
    )

    columns_here = [x[:, 0, 0] for x in (jnp.swapaxes(x_out, 3, 4), x_in, x_solve)]
    rows_here = [x[:, 0, 0] for x in (y_out, y_in)] + [leaf_out_map[0, 0]]
    if not whole_solve:
        rows_here.append(ys_here)

    def start_body(load_any, map_any, xo_any, xi_any, xs_any, h_ref, out_ref, load_out, *refs):
        xo, xi, xs, load_v, map_v, sems = refs
        pairs = zip((load_any, map_any, xo_any, xi_any, xs_any), (load_v, map_v, xo, xi, xs))
        copies = [pltpu.make_async_copy(a, b, sems.at[i]) for i, (a, b) in enumerate(pairs)]
        for copy in copies:
            copy.start()
        copies[0].wait()
        copies[1].wait()
        loaded = load_v[...].reshape(waves, inner)
        load_out[...] = loaded
        h = dot_t(loaded, map_v[...])
        h_ref[...] = h
        copies[2].wait()
        copies[3].wait()
        is_right = bit(my_column(), 0) == 1
        travelling = [
            jnp.where(is_right, edge_of(x[k], 1), edge_of(x[k], 3))
            for x in (xi, xo)
            for k in range(x_levels - 1)
        ]
        out_ref[...] = pad_lanes(
            jnp.concatenate([edge_of(h, 3), edge_of(h, 1)] + travelling, axis=1), out_ref.shape[1]
        )
        copies[4].wait()

    h0, to_send, loaded, xo_all, xi_all, xs_all = placing(
        start_body,
        [(waves, leaf), exchange_shape(0), (waves, inner)] + [x.shape for x in columns_here],
        load,
        leaf_load_map[0, 0],
        *columns_here,
        scratch=[load.shape, (leaf, inner)],
    )

    def place_body(field_any, *refs):
        *refs, sems = refs
        count = len(rows_here)
        sources = [field_any.at[:, pl.ds(0, leaf)], field_any.at[:, pl.ds(leaf, inner)]]
        pairs = zip(sources + list(refs[:count]), refs[count:])
        copies = [pltpu.make_async_copy(a, b, sems.at[i]) for i, (a, b) in enumerate(pairs)]
        for copy in copies:
            copy.start()
        for copy in copies:
            copy.wait()

    field_edges, field_inner, yo_all, yi_all, out_map, *ys_all = placing(
        place_body,
        [(inner, leaf), (inner, inner)] + [x.shape for x in rows_here],
        leaf_field_map[0, 0],
        *rows_here,
        live=2 << 20,
    )

    side_rows = iface * edge // LANES

    def at_upper():
        return (my_row() == 1) | (my_row() == 2)

    def upper_edge(x):
        return jnp.where(my_row() == 1, x[2 * edge : 3 * edge], x[:edge])

    def aside_body(load_ref, map_ref, yi_ref, yo_ref, out_ref, *side_ref):
        out_ref[...] = dot_t(load_ref[...], map_ref[...])
        for ref in side_ref:
            ref[:side_rows] = packed(
                jnp.where(my_row() == 1, edge_of(yi_ref[0], 2), edge_of(yi_ref[0], 0)), edge
            )
            out_rows = upper_edge(yo_ref[0])
            ref[side_rows:] = jnp.concatenate(
                [out_rows[:, i * LANES : (i + 1) * LANES] for i in range(iface // LANES)], axis=0
            )

    from_load, *side = fused(
        aside_body,
        [(waves, inner)] + [(2 * side_rows, LANES)] * whole_solve,
        loaded,
        field_inner,
        yi_all,
        yo_all,
    )

    core = row_axes[-1]
    swapped = [(0, 1), (1, 0)]

    def group(level):
        return tuple(row_axes[y_levels - 1 - level :]) + ("box",)

    def span(level):
        return 2 << level

    def swap(x, level):
        return lax.all_to_all(x, group(level), 0, 0, tiled=True)

    def offer_shape(level):
        if whole_solve:
            return (rows**level * cols, (waves >> level) * edge // LANES, LANES)
        return (span(level) * cols, waves // span(level) * edge // LANES, LANES)

    def store_offer(level, h, out):
        size = span(level)
        share = waves // size
        facing = jnp.where(
            lax.rem(my_row(), size) == size // 2 - 1, edge_of(h, 2), edge_of(h, 0)
        )
        if whole_solve:
            out[...] = jnp.broadcast_to(packed(facing, edge), out.shape)
            return
        for target in range(size):
            piece = packed(facing[target * share : (target + 1) * share], edge)
            out[target * cols : (target + 1) * cols] = jnp.broadcast_to(piece, (cols,) + piece.shape)

    def x_body(level, tasks, h_ref, own_ref, got_ref, solve_ref, xo_ref, *refs):
        kept = x_levels - 1 - level
        count = sum(len(args) for _, args, _ in tasks)
        ins, (h_out, w_out, *rest) = refs[:count], refs[count:]
        rest, outs = rest[: 2 if kept else 0], rest[2 if kept else 0 :]
        offer_ref = outs[-1] if outs else None
        for task, args, shapes in tasks:
            task(*ins[: len(args)], *outs[: len(shapes)])
            ins, outs = ins[len(args) :], outs[len(shapes) :]
        is_right = bit(my_column(), level) == 1
        own, got = own_ref[...], got_ref[...]
        left_child = jnp.where(is_right, got, own)
        right_child = jnp.where(is_right, own, got)
        v = jnp.concatenate([edge_of(left_child, 1), edge_of(right_child, 0)], axis=1)
        w = dot_t(v, solve_ref[level])
        w_out[...] = w
        if kept:
            next_ref, ends_ref = rest
            outer = [edge_of(x, 2 + kept) for x in (left_child, right_child)]
            spread = dot(w, jnp.concatenate([xo_ref[level]] + outer, axis=1))
            h_out[...] = h_ref[...] + spread[:, :leaf]
            left = edge_of(left_child, 0) + edge_of(spread, 4)
            right = edge_of(right_child, 1) + edge_of(spread, 5)
            ends_ref[...] = jnp.concatenate(
                [edge_of(left_child, 2), edge_of(right_child, 2)], axis=1
            )
            mine = jnp.where(bit(my_column(), level + 1) == 1, right_child, left_child)
            travelling = pieces_of(mine, 3, kept - 1) + pieces_of(mine, 3 + kept, kept - 1)
            next_ref[...] = pad_lanes(
                jnp.concatenate([left, right] + travelling, axis=1), next_ref.shape[1]
            )
        else:
            h = h_ref[...] + dot(w, xo_ref[level])
            h_out[...] = h
            if whole_solve:
                store_offer(0, h, offer_ref)

    def nothing(*refs):
        pass

    def join_upper(held_ref, moved_ref, both_ref):
        kept = in_rows + solve_rows
        join(0, held_ref[...], moved_ref[...], both_ref.at[:, :kept])
        both_ref[:, kept:] = jnp.zeros((2, in_rows, width), f32)

    def join_plain(step, held_ref, moved_ref, both_ref):
        join(step, held_ref[...], moved_ref[...], both_ref)

    h = h0
    x_keep, ends = [], []
    moved = passed_on(held, steps[0])
    upper_moved = [passed_on(x, steps[0]) for x in upper_held]
    for level in range(x_levels):
        got = lax.ppermute(to_send, "box", [(i, i ^ (1 << level)) for i in range(cols)])
        outs = [(waves, leaf), (waves, pair)]
        if level < x_levels - 1:
            outs += [exchange_shape(level + 1), (pair, pair)]
        args = [h, to_send, got, xs_all, xo_all]
        tasks = []
        if level == 0:
            tasks.append((nothing, [from_load], []))
        if whole_solve and level == 0:
            shapes = [held_shape(2, solve_rows)]
            tasks.append((functools.partial(join_plain, 0), [held, moved], shapes))
        elif whole_solve and level == 1:
            tasks.append((nothing, side, [x.shape for x in side]))
            shapes = [held_shape(2, in_rows, solve_rows, in_rows)]
            tasks.append((join_upper, upper_held + upper_moved, shapes))
        elif whole_solve:
            tasks.append((nothing, other_side, []))
            shapes = [held_shape(4, solve_rows)]
            tasks.append((functools.partial(join_plain, 1), [held, moved], shapes))
            tasks.append((nothing, [], [offer_shape(0)]))
        elif level in joined_at:
            step = joined_at.index(level)
            shape = held_shape(2 << step, in_rows)
            tasks.append((functools.partial(join_plain, step), [held, moved], [shape]))
        aliases = {len(args): len(outs)} if level == 1 and whole_solve else None
        h, w, *rest = fused(
            functools.partial(x_body, level, tasks),
            outs + [shape for task in tasks for shape in task[2]],
            *args,
            *(x for task in tasks for x in task[1]),
            aliases=aliases,
        )
        x_keep.append(w)
        if level < x_levels - 1:
            to_send, end, *rest = rest
            ends.append(end)
        if whole_solve and level == 0:
            (held,) = rest
            moved = passed_on(held, steps[1])
        elif whole_solve and level == 1:
            side, upper_held = rest[:1], rest[1]
            upper_moved = passed_on(upper_held, steps[1])
            other_side = [lax.ppermute(x, core, swapped) for x in side]
        elif whole_solve:
            held, offer = rest
            moved = passed_on(held, steps[2])
        elif level in joined_at:
            (held,) = rest
            moved = passed_on(held, steps[step + 1])

    def offer_body(level, h_ref, out_ref):
        store_offer(level, h_ref[...], out_ref)

    def folded(x):
        return jnp.concatenate([x[i : i + 8] for i in range(0, x.shape[0], 8)], axis=1)

    def unfolded(x, rows):
        return jnp.concatenate([edge_of(x, i) for i in range(rows // 8)], axis=0)

    def gather_v(level, got_ref, v_ref):
        size = span(level)
        low = (size // 2 - 1) * cols
        run = got_ref.shape[1]
        for side in range(2):
            for c in range(cols):
                piece = got_ref[low + side * cols + c]
                for k in range(LANES // edge):
                    start = c * pair + side * edge
                    v_ref[k * run : (k + 1) * run, start : start + edge] = edge_of(piece, k)

    def solve_body(level, got_ref, solve_ref, out_ref, v_ref):
        gather_v(level, got_ref, v_ref)
        w = packed(dot_t(v_ref[...], solve_ref[level]), pair)
        out_ref[...] = jnp.broadcast_to(w, out_ref.shape)

    def own_columns(w_all):
        own = w_all[:, :pair]
        for c in range(1, cols):
            own = jnp.where(my_column() == c, w_all[:, c * pair : (c + 1) * pair], own)
        return own

    def gather_w(level, got_ref, w_ref):
        size = span(level)
        share = waves // size
        run = got_ref.shape[1]
        for target in range(size):
            for c in range(cols):
                piece = got_ref[target * cols + c]
                for k in range(LANES // pair):
                    start = target * share + k * run
                    w_ref[start : start + run, c * pair : (c + 1) * pair] = piece[
                        :, k * pair : (k + 1) * pair
                    ]
        return w_ref[...]

    def upper_face(h_ref):
        return jnp.where(my_row() == 1, edge_of(h_ref[...], 2), edge_of(h_ref[...], 0))

    def half_body(level, got_ref, held_ref, moved_ref, *refs):
        if level == 0:
            upper_held_ref, upper_moved_ref, h_ref, out_ref, face_ref, upper_ref, v_ref = refs
            face_ref[...] = packed(upper_face(h_ref), edge)
            kept = in_rows + solve_rows
            join(1, upper_held_ref[:, :kept], upper_moved_ref[:, :kept], upper_ref)
        else:
            out_ref, v_ref = refs
        odd_row = bit(my_row(), 0) == 1
        run = got_ref.shape[1]
        for c in range(cols):
            for part in range(1 + level):
                piece = got_ref[part * cols + c]
                if level == 1:
                    piece = jnp.where(odd_row, piece, got_ref[(2 + part) * cols + c])
                for k in range(LANES // edge):
                    start = (part * LANES // edge + k) * run
                    v_ref[start : start + run, c * edge : (c + 1) * edge] = edge_of(piece, k)
        solve = []
        for c in range(cols):
            start = in_rows * level
            block = held_of(c, held_ref, moved_ref)[start : start + edge]
            solve += [block[:, : iface // 2], block[:, iface // 2 :]]
        out_ref[...] = dot_t(v_ref[...], jnp.concatenate(solve, axis=0))

    def whole_body(h_ref, mine_ref, other_ref, yo_ref, face_ref, side_ref, h_out, w_out, next_ref):
        w_all = mine_ref[...] + other_ref[...]
        w_out[...] = own_columns(w_all)
        out_rows = side_ref[side_rows:]
        out_rows = jnp.concatenate(
            [out_rows[i * edge : (i + 1) * edge] for i in range(iface // LANES)], axis=1
        )
        out_rows = jnp.where(at_upper(), upper_edge(yo_ref[0]), out_rows)
        spread = dot_t(w_all, jnp.concatenate([yo_ref[0], out_rows], axis=0))
        h_out[...] = h_ref[...] + spread[:, :leaf]
        face = jnp.where(at_upper(), upper_face(h_ref), unpacked(face_ref[...], edge))
        face = face + spread[:, leaf:]
        half = jnp.where(bit(my_row(), 0) == 1, face[waves // 2 :], face[: waves // 2])
        next_ref[...] = jnp.broadcast_to(packed(half, edge), next_ref.shape)

    def spread_body(level, h_ref, got_ref, yo_ref, h_out, w_out, next_ref, w_ref):
        w_all = gather_w(level, got_ref, w_ref)
        w_out[...] = own_columns(w_all)
        h = h_ref[...] + dot_t(w_all, yo_ref[level])
        h_out[...] = h
        store_offer(level + 1, h, next_ref)

    def halves(level):
        return span(level) // 2

    def terms_shape(level):
        return (span(level) * cols, waves // halves(level) * edge // LANES, LANES)

    def store_terms(level, g, yi_ref, out):
        terms = dot_t(g, yi_ref[level])
        half = halves(level)
        share = waves // half
        for side in range(2):
            for c in range(cols):
                start = c * pair + side * edge
                piece = terms[:, start : start + edge]
                for part in range(half):
                    out[(side * half + part) * cols + c] = packed(
                        piece[part * share : (part + 1) * share], edge
                    )

    def turn_body(level, h_ref, got_ref, *refs):
        if whole_solve:
            other_ref, yo_ref, yi_ref, reflect_ref, w_out, g_out, out_ref = refs
            w_all = got_ref[...] + other_ref[...]
        else:
            yo_ref, yi_ref, reflect_ref, w_out, g_out, out_ref, w_ref = refs
            w_all = gather_w(level, got_ref, w_ref)
        w_out[...] = own_columns(w_all)
        h = h_ref[...] + dot_t(w_all, yo_ref[level])
        lane = lax.broadcasted_iota(jnp.int32, (1, leaf), 1)

        def side(number):
            return (lane >= number * edge) & (lane < (number + 1) * edge)

        outer = (
            side(0) & (my_row() == 0)
            | side(1) & (my_column() == cols - 1)
            | side(2) & (my_row() == rows - 1)
            | side(3) & (my_column() == 0)
        )
        g = jnp.where(outer, h * reflect_ref[...], 0.0)
        g_out[...] = g
        store_terms(level, g, yi_ref, out_ref)

    def sum_body(got_ref, out_ref):
        out_ref[...] = jnp.sum(got_ref[...], axis=0)

    def with_row_edge(level, g, w, q):
        size = span(level)
        place = lax.rem(my_row(), size)
        is_low = place == size // 2 - 1
        is_high = place == size // 2
        value = jnp.where(place < size // 2, w[:, :edge], w[:, edge:]) + q
        bottom = jnp.where(is_high, value, edge_of(g, 0))
        top = jnp.where(is_low, value, edge_of(g, 2))
        return jnp.concatenate([bottom, edge_of(g, 1), top, edge_of(g, 3)], axis=1)

    def row_down_body(level, g_ref, w_ref, sum_ref, yi_ref, g_out, out_ref):
        g = with_row_edge(level, g_ref[...], w_ref[...], unpacked_parts(level, sum_ref))
        g_out[...] = g
        store_terms(level - 1, g, yi_ref, out_ref)

    def unpacked_parts(level, sum_ref):
        run = waves // halves(level) * edge // LANES
        return jnp.concatenate(
            [unpacked(sum_ref[i * run : (i + 1) * run], edge) for i in range(halves(level))], axis=0
        )

    def collect(total, level):
        for axis_no in range(level):
            axis = row_axes[y_levels - 1 - axis_no]
            other = lax.ppermute(total, axis, [(0, 1), (1, 0)])
            first = lax.axis_index(axis) == 0
            total = jnp.concatenate(
                [jnp.where(first, total, other), jnp.where(first, other, total)], axis=0
            )
        return total

    x_lanes = -(-(x_levels + 1) * edge // LANES) * LANES

    def sides_of(terms):
        low, high = (
            jnp.concatenate([edge_of(terms, 2 * c + side) for c in range(cols)], axis=1)
            for side in range(2)
        )
        odd_row = bit(my_row(), 0) == 1
        return jnp.where(odd_row, high, low), jnp.where(odd_row, low, high)

    def split_body(g_ref, w_ref, sum_ref, yi_ref, g_out, own_out, other_out):
        g = with_row_edge(1, g_ref[...], w_ref[...], unpacked_parts(1, sum_ref))
        g_out[...] = g
        own_out[...], other_out[...] = sides_of(dot_t(g, yi_ref[0]))

    def upper_body(got_ref, g_ref, w_ref, yi_ref, side_ref, other_ref, own_out, other_out, half_out):
        q = unpacked(jnp.sum(got_ref[...], axis=0), edge)
        w = w_ref[...]
        w = jnp.where(my_row() < 2, w[:, :edge], w[:, edge:])
        odd_row = bit(my_row(), 0) == 1
        half = waves // 2
        value = jnp.where(odd_row, w[half:], w[:half]) + q
        half_out[...] = value
        columns = jnp.where(at_upper(), side_ref[:side_rows], other_ref[:side_rows])
        columns = unpacked(columns, edge)
        added = dot_t(value, columns)
        terms = dot_t(g_ref[...], yi_ref[0])
        terms = jnp.concatenate(
            [
                terms[:half] + jnp.where(odd_row, 0.0, added),
                terms[half:] + jnp.where(odd_row, added, 0.0),
            ],
            axis=0,
        )
        own_out[...], other_out[:waves] = sides_of(terms)
        other_out[waves:] = jnp.zeros((8, iface // 2), f32)
        other_out[waves:, : half // 8 * edge] = folded(value)

    node_starts = []
    for k in range(x_levels):
        node_starts.append(sum(cols >> (i + 1) for i in range(k)) * pair)
    node_lanes = (cols - 1) * pair

    inner_lanes = x_levels * edge

    def prepare_body(g_ref, w_ref, xi_ref, held_ref, moved_ref, lo_ref, *refs):
        keep_ref, ends_ref = refs[:x_levels], refs[x_levels : 2 * x_levels - 1]
        matrix_out, known_out, chain_out, keep_out = refs[2 * x_levels - 1 :]
        unit = lax.broadcasted_iota(jnp.int32, (edge, inner_lanes), 0)
        unit = lax.broadcasted_iota(jnp.int32, (edge, inner_lanes), 1) - unit
        gl = jnp.zeros((edge, inner_lanes), f32)
        gr = gl
        for level in reversed(range(x_levels)):
            is_right = bit(my_column(), level) == 1
            keep = keep_ref[level][...]
            keep_out[:, level * edge : (level + 1) * edge] = jnp.where(
                is_right, keep[:, edge:], keep[:, :edge]
            )
            value = jnp.where(unit == level * edge, 1.0, 0.0)
            if level < x_levels - 1:
                end = ends_ref[level][...]
                end = jnp.where(is_right, end[edge:], end[:edge])
                value = value + dot(end, jnp.concatenate([gl, gr], axis=0))
            gl = jnp.where(is_right, value, gl)
            gr = jnp.where(is_right, gr, value)
        none = jnp.zeros((edge, inner_lanes), f32)
        out_map = lo_ref[...]
        added = dot(out_map, jnp.concatenate([none, gr, none, gl], axis=0))
        none = jnp.zeros((pair, leaf), f32)
        chain_out[...] = jnp.concatenate(
            [
                jnp.concatenate([out_map, added], axis=1),
                jnp.concatenate([none, jnp.concatenate([gr, gl], axis=0)], axis=1),
            ],
            axis=0,
        )
        g = with_row_edge(0, g_ref[...], w_ref[...], 0.0)
        row = []
        for c in range(cols):
            held = held_of(c, held_ref, moved_ref)[:in_rows]
            row.append(
                jnp.concatenate(
                    [held[:, i * in_lanes : (i + 1) * in_lanes] for i in range(runs)], axis=0
                )
            )
        matrix_out[...] = jnp.zeros_like(matrix_out)
        for k in range(x_levels):
            known = dot_t(g, xi_ref[k])
            for node in range(cols >> (k + 1)):
                start = node_starts[k] + node * pair
                inside = my_column() >> (k + 1) == node
                known_out[:, start : start + pair] = jnp.where(inside, known, 0.0)
                for c in range(node << (k + 1), (node + 1) << (k + 1)):
                    matrix_out[start : start + pair, c * edge : (c + 1) * edge] = edge_of(row[c], k)

    def x_terms_body(own_ref, got_ref, matrix_ref, known_ref, *refs):
        out_ref = refs[-1]
        q = own_ref[...] + got_ref[:waves]
        terms = dot_t(q, matrix_ref[...]) + known_ref[...]
        if whole_solve:
            g_ref, half_ref, xi_ref, g_out, _ = refs
            odd_row = bit(my_row(), 0) == 1
            mine, other = half_ref[...], unfolded(got_ref[waves:], waves // 2)
            value = jnp.concatenate(
                [jnp.where(odd_row, other, mine), jnp.where(odd_row, mine, other)], axis=0
            )
            none = jnp.zeros_like(value)
            upper = jnp.concatenate(
                [
                    jnp.where(my_row() == 2, value, 0.0),
                    none,
                    jnp.where(my_row() == 1, value, 0.0),
                    none,
                ],
                axis=1,
            )
            g_out[...] = g_ref[...] + upper
            added = dot_t(upper, xi_ref[...].reshape(x_levels * pair, leaf))
        for c in range(cols):
            picked = []
            for k in range(x_levels):
                start = node_starts[k] + (c >> (k + 1)) * pair + bit(c, k) * edge
                piece = terms[:, start : start + edge]
                if whole_solve:
                    inside = my_column() >> (k + 1) == c >> (k + 1)
                    piece = piece + jnp.where(inside, edge_of(added, 2 * k + bit(c, k)), 0.0)
                picked.append(piece)
            out_ref[c] = pad_lanes(jnp.concatenate(picked + [edge_of(q, c)], axis=1), x_lanes)

    def finish_body(g_ref, w_ref, h0_ref, got_ref, chain_ref, keep_ref, g_out, t_out, *faces):
        q = jnp.sum(got_ref[...], axis=0)
        g = with_row_edge(0, g_ref[...], w_ref[...], edge_of(q, x_levels))
        terms = q[:, :inner_lanes] + keep_ref[...]
        result = dot_t(jnp.concatenate([g, terms], axis=1), chain_ref[...])
        gr, gl = edge_of(result, 4), edge_of(result, 5)
        g = jnp.concatenate(
            [edge_of(g, 0), edge_of(g, 1) + gr, edge_of(g, 2), edge_of(g, 3) + gl], axis=1
        )
        g_out[...] = g
        t = g - (result[:, :leaf] + h0_ref[...])
        t_out[...] = t
        odd_col = bit(my_column(), 0) == 1
        odd_row = bit(my_row(), 0) == 1
        bottom, right, top, left = (packed(edge_of(t, i), edge) for i in range(4))
        faces[0][...] = jnp.where(odd_col, left, right)
        faces[1][...] = jnp.where(odd_col, right, left)
        faces[2][...] = jnp.where(odd_row, bottom, top)
        faces[3][...] = jnp.where(odd_row, top, bottom)

    def trace_body(t_ref, a_ref, b_ref, c_ref, d_ref, out_ref):
        t = t_ref[...]
        odd_col = bit(my_column(), 0) == 1
        odd_row = bit(my_row(), 0) == 1
        near_x, far_x, near_y, far_y = (
            unpacked(ref[...], edge) for ref in (a_ref, b_ref, c_ref, d_ref)
        )
        east = jnp.where(odd_col, far_x, near_x)
        west = jnp.where(odd_col, near_x, far_x)
        north = jnp.where(odd_row, far_y, near_y)
        south = jnp.where(odd_row, near_y, far_y)

        def mean(shared, own, other):
            return jnp.where(shared, 0.5 * (own + other), own)

        trace = jnp.concatenate(
            [
                mean(my_row() > 0, edge_of(t, 0), south),
                mean(my_column() < cols - 1, edge_of(t, 1), east),
                mean(my_row() < rows - 1, edge_of(t, 2), north),
                mean(my_column() > 0, edge_of(t, 3), west),
            ],
            axis=1,
        )
        out_ref[...] = trace.reshape(out_ref.shape)

    face = (waves * edge // LANES, LANES)
    if not whole_solve:
        (offer,) = fused(functools.partial(offer_body, 0), [offer_shape(0)], h)
    y_keep = []
    for level in range(y_levels):
        if whole_solve:
            axes = "box" if level == 0 else group(1)
            got = lax.all_to_all(offer, axes, 0, 0, tiled=True)
            if level == 0:
                mine, upper, second = fused(
                    functools.partial(half_body, 0),
                    [(waves, iface), face, held_shape(4, in_rows, solve_rows)],
                    got,
                    held,
                    moved,
                    upper_held,
                    upper_moved,
                    h,
                    scratch=[(waves, cols * edge)],
                )
                upper = lax.ppermute(upper, core, swapped)
                second_moved = passed_on(second, steps[2])
            else:
                (mine,) = fused(
                    functools.partial(half_body, 1),
                    [(waves, iface)],
                    got,
                    second,
                    second_moved,
                    scratch=[(waves, cols * edge)],
                )
            other = lax.ppermute(mine, core, swapped)
            if level == 0:
                h, w, offer = fused(
                    whole_body,
                    [(waves, leaf), (waves, pair), offer_shape(1)],
                    h,
                    mine,
                    other,
                    yo_all,
                    upper,
                    *other_side,
                )
            else:
                w, g, terms = fused(
                    functools.partial(turn_body, level),
                    [(waves, pair), (waves, leaf), terms_shape(level)],
                    h,
                    mine,
                    other,
                    yo_all,
                    yi_all,
                    reflect[0],
                )
            y_keep.append(w)
            continue
        share = waves // span(level)
        (w_offer,) = fused(
            functools.partial(solve_body, level),
            [(span(level) * cols, share * pair // LANES, LANES)],
            swap(offer, level),
            *ys_all,
            scratch=[(share, iface)],
        )
        got = swap(w_offer, level)
        if level < y_levels - 1:
            h, w, offer = fused(
                functools.partial(spread_body, level),
                [(waves, leaf), (waves, pair), offer_shape(level + 1)],
                h,
                got,
                yo_all,
                scratch=[(waves, iface)],
            )
        else:
            w, g, terms = fused(
                functools.partial(turn_body, level),
                [(waves, pair), (waves, leaf), terms_shape(level)],
                h,
                got,
                yo_all,
                yi_all,
                reflect[0],
                scratch=[(waves, iface)],
            )
        y_keep.append(w)
    for level in reversed(range(1, 1 if whole_solve else y_levels)):
        (total,) = fused(sum_body, [terms_shape(level)[1:]], swap(terms, level))
        total = collect(total, level)
        if level > 1:
            g, terms = fused(
                functools.partial(row_down_body, level),
                [(waves, leaf), terms_shape(level - 1)],
                g,
                y_keep[level],
                total,
                yi_all,
            )
    share = (waves, iface // 2)
    if whole_solve:
        own, other, half = fused(
            upper_body,
            [share, (waves + 8, iface // 2), (waves // 2, edge)],
            swap(terms, 1),
            g,
            y_keep[1],
            yi_all,
            *side,
            *other_side,
        )
    else:
        g, own, other = fused(
            split_body, [(waves, leaf), share, share], g, y_keep[1], total, yi_all
        )
    got = lax.ppermute(other, core, swapped)
    matrix, known, chain, keep = fused(
        prepare_body,
        [
            (node_lanes, cols * edge),
            (waves, node_lanes),
            (leaf + pair, leaf + inner_lanes),
            (waves, inner_lanes),
        ],
        g,
        y_keep[0],
        xi_all,
        *((second, second_moved) if whole_solve else (held, moved)),
        out_map,
        *x_keep,
        *ends,
    )
    upper = []
    if whole_solve:
        upper = [g, half, xi_all]
    *g_now, terms = fused(
        x_terms_body,
        [(waves, leaf)] * whole_solve + [(cols, waves, x_lanes)],
        own,
        got,
        matrix,
        known,
        *upper,
    )
    g = g_now[0] if g_now else g
    got = lax.all_to_all(terms, "box", 0, 0, tiled=True)
    g, t, *faces = fused(
        finish_body,
        [(waves, leaf), (waves, leaf)] + [face] * 4,
        g,
        y_keep[0],
        h0,
        got,
        chain,
        keep,
    )

    def near(count):
        return [(i, i ^ 1) for i in range(count)]

    def far(count):
        one_way = [(i, i + 1) for i in range(1, count - 1, 2)]
        return one_way + [(j, i) for i, j in one_way]

    seen = [
        lax.ppermute(faces[0], "box", near(cols)),
        lax.ppermute(faces[1], "box", far(cols)),
        lax.ppermute(faces[2], row_axes, near(rows)),
        lax.ppermute(faces[3], row_axes, far(rows)),
    ]
    def field_body(g_ref, map_ref, from_load_ref, out_ref):
        field = from_load_ref[...] + dot_t(g_ref[...], map_ref[...])
        out_ref[...] = field.reshape(out_ref.shape)

    (field_vals,) = fused(
        field_body, [(waves, 1, 1, inner)], g, field_edges, from_load
    )
    (edge_trace,) = fused(trace_body, [(waves, 1, 1, leaf)], t, *seen)
    return field_vals, edge_trace


def solution(mesh):
    rows, cols = mesh.devices.shape
    bits = rows.bit_length() - 1
    row_axes = tuple(f"row{i}" for i in reversed(range(bits)))
    split = Mesh(mesh.devices.reshape((2,) * bits + (cols,)), row_axes + ("box",))
    late = P(None, row_axes, "box")
    early = P(row_axes, "box")
    return jax.shard_map(
        functools.partial(local, row_axes),
        mesh=split,
        in_specs=(late, early, early, early) + (late,) * 6 + (early,),
        out_specs=(late, late),
        check_vma=False,
    )
```

```python
import functools
import math

import jax
import jax.numpy as jnp
from jax import lax
from jax.experimental import pallas as pl
from jax.experimental.pallas import tpu as pltpu
from jax.sharding import Mesh, PartitionSpec as P

f32 = jnp.float32
LANES = 128
PLACING_VMEM = 60 << 20


def dot(a, b, over=0):
    dims = (((1,), (over,)), ((), ()))

    def parts(x):
        high = x.astype(jnp.bfloat16)
        return high, (x - high.astype(f32)).astype(jnp.bfloat16)

    def product(x, y):
        return lax.dot_general(x, y, dims, preferred_element_type=f32)

    a_high, a_low = parts(a)
    b_high, b_low = parts(b)
    both = product(jnp.concatenate([a_high, a_low], axis=0), b_high)
    return both[: a.shape[0]] + (product(a_high, b_low) + both[a.shape[0] :])


def dot_t(a, b):
    return dot(a, b, 1)


def fused(body, outs, *args, scratch=(), aliases=None):
    vmem = pl.BlockSpec(memory_space=pltpu.VMEM)
    return pl.pallas_call(
        body,
        out_shape=[pltpu.VMEM(s, f32) for s in outs],
        in_specs=[vmem] * len(args),
        out_specs=[vmem] * len(outs),
        scratch_shapes=[pltpu.VMEM(s, f32) for s in scratch],
        input_output_aliases=aliases or {},
        compiler_params=pltpu.CompilerParams(vmem_limit_bytes=12 << 20),
    )(*args)


def packed(x, width):
    runs = LANES // width
    rows = x.shape[0] // runs
    return jnp.concatenate([x[i * rows : (i + 1) * rows] for i in range(runs)], axis=1)


def unpacked(x, width):
    return jnp.concatenate(
        [x[:, i * width : (i + 1) * width] for i in range(x.shape[1] // width)], axis=0
    )


def pad_lanes(x, lanes):
    if x.shape[1] == lanes:
        return x
    return jnp.concatenate([x, jnp.zeros((x.shape[0], lanes - x.shape[1]), f32)], axis=1)


def local(
    row_axes,
    load,
    leaf_load_map,
    leaf_out_map,
    leaf_field_map,
    x_solve,
    x_out,
    x_in,
    y_solve,
    y_out,
    y_in,
    reflect,
):
    edge = leaf_out_map.shape[-1] // 4
    cols = lax.axis_size("box")
    rows = 1
    for axis in row_axes:
        rows *= lax.axis_size(axis)
    x_levels = x_solve.shape[0]
    y_levels = y_solve.shape[0]
    waves = load.shape[0]
    leaf = 4 * edge
    pair = 2 * edge
    iface = cols * pair
    load_here = load[:, 0, 0, :]
    inner = load_here.shape[1]

    def my_column():
        return lax.axis_index("box")

    def my_row():
        return lax.axis_index(row_axes)

    def bit(value, level):
        return (value >> level) & 1

    def edge_of(x, number):
        return x[:, number * edge : (number + 1) * edge]

    def exchange_shape(level):
        kept = x_levels - 1 - level
        lanes = (2 + 2 * kept) * edge
        return (pair, -(-lanes // LANES) * LANES)

    def pieces_of(x, first, count):
        return [edge_of(x, first + i) for i in range(count)]

    whole_solve = (x_levels, y_levels) == (3, 2) and iface * iface <= 1 << 18
    in_lanes = -(-x_levels * edge // LANES) * LANES
    width = iface if whole_solve else 4 * in_lanes
    runs = width // in_lanes
    in_rows = pair // runs
    solve_rows = edge if whole_solve else 0

    def held_shape(count, *parts):
        return (count, sum(parts), width)

    def passed_on(held, bit_no):
        return lax.ppermute(held, "box", [(i, i ^ (1 << bit_no)) for i in range(cols)])

    steps = [x_levels - 1] + list(range(x_levels - 1))
    joined_at = [0] + list(range(2, x_levels))

    def held_of(c, held_ref, moved_ref):
        place = sum(bit(c, b) << k for k, b in enumerate(steps[:-1]))
        same = bit(my_column(), steps[-1]) == bit(c, steps[-1])
        return jnp.where(same, held_ref[place], moved_ref[place])

    def join(step, held, moved, both_ref):
        high = bit(my_column(), steps[step]) == 1
        both_ref[: 1 << step] = jnp.where(high, moved, held)
        both_ref[1 << step :] = jnp.where(high, held, moved)

    def placing(body, shapes, *args, scratch=(), live=0):
        return pl.pallas_call(
            body,
            out_shape=[pltpu.VMEM(s, f32) for s in shapes],
            in_specs=[pl.BlockSpec(memory_space=pl.ANY)] * len(args),
            out_specs=[pl.BlockSpec(memory_space=pltpu.VMEM)] * len(shapes),
            scratch_shapes=[pltpu.VMEM(s, f32) for s in scratch]
            + [pltpu.SemaphoreType.DMA((len(args) + 1,))],
            compiler_params=pltpu.CompilerParams(
                vmem_limit_bytes=PLACING_VMEM - live - sum(4 * math.prod(s) for s in shapes)
            ),
        )(*args)

    def hold_body(solve_any, xi_any, *refs):
        *held_refs, solve, xi, sems = refs
        copies = [
            pltpu.make_async_copy(solve_any, solve, sems.at[0]),
            pltpu.make_async_copy(xi_any, xi, sems.at[1]),
        ]
        for copy in copies:
            copy.start()
        for copy in copies:
            copy.wait()
        odd_row = bit(my_row(), 0) == 1
        row_in = pad_lanes(
            jnp.concatenate(
                [
                    jnp.where(odd_row, edge_of(xi[k], 0), edge_of(xi[k], 2))
                    for k in range(x_levels)
                ],
                axis=1,
            ),
            in_lanes,
        )
        held_refs[-1][0, :in_rows] = jnp.concatenate(
            [row_in[i * in_rows : (i + 1) * in_rows] for i in range(runs)], axis=1
        )
        if whole_solve:
            for level, held_ref in enumerate(held_refs[:2]):
                low, high = (
                    jnp.concatenate(
                        [edge_of(solve[level], 2 * c + side) for c in range(cols)], axis=1
                    )
                    for side in range(2)
                )
                mine = jnp.where(odd_row == (level == 0), high, low)
                start = in_rows * level
                held_ref[0, start : start + edge] = jnp.concatenate(
                    [mine[:edge], mine[edge:]], axis=1
                )

    ys_here, xi_here = y_solve[:, 0, 0], x_in[:, 0, 0]
    held, *upper_held = placing(
        hold_body,
        [held_shape(1, solve_rows)] * whole_solve + [held_shape(1, in_rows, solve_rows)],
        ys_here,
        xi_here,
        scratch=[ys_here.shape, xi_here.shape],
    )

    columns_here = [x[:, 0, 0] for x in (jnp.swapaxes(x_out, 3, 4), x_in, x_solve)]
    rows_here = [x[:, 0, 0] for x in (y_out, y_in)] + [leaf_out_map[0, 0], reflect[0]]
    if not whole_solve:
        rows_here.append(ys_here)

    def start_body(load_any, map_any, xo_any, xi_any, xs_any, h_ref, out_ref, load_out, *refs):
        xo, xi, xs, load_v, map_v, sems = refs
        pairs = zip((load_any, map_any, xo_any, xi_any, xs_any), (load_v, map_v, xo, xi, xs))
        copies = [pltpu.make_async_copy(a, b, sems.at[i]) for i, (a, b) in enumerate(pairs)]
        for copy in copies:
            copy.start()
        copies[0].wait()
        copies[1].wait()
        loaded = load_v[...].reshape(waves, inner)
        load_out[...] = loaded
        h = dot_t(loaded, map_v[...])
        h_ref[...] = h
        copies[2].wait()
        copies[3].wait()
        is_right = bit(my_column(), 0) == 1
        travelling = [
            jnp.where(is_right, edge_of(x[k], 1), edge_of(x[k], 3))
            for x in (xi, xo)
            for k in range(x_levels - 1)
        ]
        out_ref[...] = pad_lanes(
            jnp.concatenate([edge_of(h, 3), edge_of(h, 1)] + travelling, axis=1), out_ref.shape[1]
        )
        copies[4].wait()

    h0, to_send, loaded, xo_all, xi_all, xs_all = placing(
        start_body,
        [(waves, leaf), exchange_shape(0), (waves, inner)] + [x.shape for x in columns_here],
        load,
        leaf_load_map[0, 0],
        *columns_here,
        scratch=[load.shape, (leaf, inner)],
    )

    def place_body(field_any, *refs):
        *refs, sems = refs
        count = len(rows_here)
        sources = [field_any.at[:, pl.ds(0, leaf)], field_any.at[:, pl.ds(leaf, inner)]]
        pairs = zip(sources + list(refs[:count]), refs[count:])
        copies = [pltpu.make_async_copy(a, b, sems.at[i]) for i, (a, b) in enumerate(pairs)]
        for copy in copies:
            copy.start()
        for copy in copies:
            copy.wait()

    field_edges, field_inner, yo_all, yi_all, out_map, mirror, *ys_all = placing(
        place_body,
        [(inner, leaf), (inner, inner)] + [x.shape for x in rows_here],
        leaf_field_map[0, 0],
        *rows_here,
        live=2 << 20,
    )

    side_rows = iface * edge // LANES

    def at_upper():
        return (my_row() == 1) | (my_row() == 2)

    def upper_edge(x):
        return jnp.where(my_row() == 1, x[2 * edge : 3 * edge], x[:edge])

    def aside_body(load_ref, map_ref, yi_ref, yo_ref, out_ref, *side_ref):
        out_ref[...] = dot_t(load_ref[...], map_ref[...])
        for ref in side_ref:
            ref[:side_rows] = packed(
                jnp.where(my_row() == 1, edge_of(yi_ref[0], 2), edge_of(yi_ref[0], 0)), edge
            )
            out_rows = upper_edge(yo_ref[0])
            ref[side_rows:] = jnp.concatenate(
                [out_rows[:, i * LANES : (i + 1) * LANES] for i in range(iface // LANES)], axis=0
            )

    from_load, *side = fused(
        aside_body,
        [(waves, inner)] + [(2 * side_rows, LANES)] * whole_solve,
        loaded,
        field_inner,
        yi_all,
        yo_all,
    )

    core = row_axes[-1]
    swapped = [(0, 1), (1, 0)]

    def group(level):
        return tuple(row_axes[y_levels - 1 - level :]) + ("box",)

    def span(level):
        return 2 << level

    def swap(x, level):
        return lax.all_to_all(x, group(level), 0, 0, tiled=True)

    def offer_shape(level):
        if whole_solve:
            return (rows**level * cols, (waves >> level) * edge // LANES, LANES)
        return (span(level) * cols, waves // span(level) * edge // LANES, LANES)

    def store_offer(level, h, out):
        size = span(level)
        share = waves // size
        facing = jnp.where(
            lax.rem(my_row(), size) == size // 2 - 1, edge_of(h, 2), edge_of(h, 0)
        )
        if whole_solve:
            out[...] = jnp.broadcast_to(packed(facing, edge), out.shape)
            return
        for target in range(size):
            piece = packed(facing[target * share : (target + 1) * share], edge)
            out[target * cols : (target + 1) * cols] = jnp.broadcast_to(piece, (cols,) + piece.shape)

    def x_body(level, tasks, h_ref, own_ref, got_ref, solve_ref, xo_ref, *refs):
        kept = x_levels - 1 - level
        count = sum(len(args) for _, args, _ in tasks)
        ins, (h_out, w_out, *rest) = refs[:count], refs[count:]
        rest, outs = rest[: 2 if kept else 0], rest[2 if kept else 0 :]
        offer_ref = outs[-1] if outs else None
        for task, args, shapes in tasks:
            task(*ins[: len(args)], *outs[: len(shapes)])
            ins, outs = ins[len(args) :], outs[len(shapes) :]
        is_right = bit(my_column(), level) == 1
        own, got = own_ref[...], got_ref[...]
        left_child = jnp.where(is_right, got, own)
        right_child = jnp.where(is_right, own, got)
        v = jnp.concatenate([edge_of(left_child, 1), edge_of(right_child, 0)], axis=1)
        w = dot_t(v, solve_ref[level])
        w_out[...] = w
        if kept:
            next_ref, ends_ref = rest
            outer = [edge_of(x, 2 + kept) for x in (left_child, right_child)]
            spread = dot(w, jnp.concatenate([xo_ref[level]] + outer, axis=1))
            h_out[...] = h_ref[...] + spread[:, :leaf]
            left = edge_of(left_child, 0) + edge_of(spread, 4)
            right = edge_of(right_child, 1) + edge_of(spread, 5)
            ends_ref[...] = jnp.concatenate(
                [edge_of(left_child, 2), edge_of(right_child, 2)], axis=1
            )
            mine = jnp.where(bit(my_column(), level + 1) == 1, right_child, left_child)
            travelling = pieces_of(mine, 3, kept - 1) + pieces_of(mine, 3 + kept, kept - 1)
            next_ref[...] = pad_lanes(
                jnp.concatenate([left, right] + travelling, axis=1), next_ref.shape[1]
            )
        else:
            h = h_ref[...] + dot(w, xo_ref[level])
            h_out[...] = h
            if whole_solve:
                store_offer(0, h, offer_ref)

    def nothing(*refs):
        pass

    def join_upper(held_ref, moved_ref, both_ref):
        kept = in_rows + solve_rows
        join(0, held_ref[...], moved_ref[...], both_ref.at[:, :kept])
        both_ref[:, kept:] = jnp.zeros((2, in_rows, width), f32)

    def join_plain(step, held_ref, moved_ref, both_ref):
        join(step, held_ref[...], moved_ref[...], both_ref)

    h = h0
    x_keep, ends = [], []
    moved = passed_on(held, steps[0])
    upper_moved = [passed_on(x, steps[0]) for x in upper_held]
    for level in range(x_levels):
        got = lax.ppermute(to_send, "box", [(i, i ^ (1 << level)) for i in range(cols)])
        outs = [(waves, leaf), (waves, pair)]
        if level < x_levels - 1:
            outs += [exchange_shape(level + 1), (pair, pair)]
        args = [h, to_send, got, xs_all, xo_all]
        tasks = []
        if level == 0:
            tasks.append((nothing, [from_load], []))
        if whole_solve and level == 0:
            shapes = [held_shape(2, solve_rows)]
            tasks.append((functools.partial(join_plain, 0), [held, moved], shapes))
        elif whole_solve and level == 1:
            tasks.append((nothing, side, [x.shape for x in side]))
            shapes = [held_shape(2, in_rows, solve_rows, in_rows)]
            tasks.append((join_upper, upper_held + upper_moved, shapes))
        elif whole_solve:
            tasks.append((nothing, other_side, []))
            shapes = [held_shape(4, solve_rows)]
            tasks.append((functools.partial(join_plain, 1), [held, moved], shapes))
            tasks.append((nothing, [], [offer_shape(0)]))
        elif level in joined_at:
            step = joined_at.index(level)
            shape = held_shape(2 << step, in_rows)
            tasks.append((functools.partial(join_plain, step), [held, moved], [shape]))
        aliases = {len(args): len(outs)} if level == 1 and whole_solve else None
        h, w, *rest = fused(
            functools.partial(x_body, level, tasks),
            outs + [shape for task in tasks for shape in task[2]],
            *args,
            *(x for task in tasks for x in task[1]),
            aliases=aliases,
        )
        x_keep.append(w)
        if level < x_levels - 1:
            to_send, end, *rest = rest
            ends.append(end)
        if whole_solve and level == 0:
            (held,) = rest
            moved = passed_on(held, steps[1])
        elif whole_solve and level == 1:
            side, upper_held = rest[:1], rest[1]
            upper_moved = passed_on(upper_held, steps[1])
            other_side = [lax.ppermute(x, core, swapped) for x in side]
        elif whole_solve:
            held, offer = rest
            moved = passed_on(held, steps[2])
        elif level in joined_at:
            (held,) = rest
            moved = passed_on(held, steps[step + 1])

    def offer_body(level, h_ref, out_ref):
        store_offer(level, h_ref[...], out_ref)

    def folded(x):
        return jnp.concatenate([x[i : i + 8] for i in range(0, x.shape[0], 8)], axis=1)

    def unfolded(x, rows):
        return jnp.concatenate([edge_of(x, i) for i in range(rows // 8)], axis=0)

    def gather_v(level, got_ref, v_ref):
        size = span(level)
        low = (size // 2 - 1) * cols
        run = got_ref.shape[1]
        for side in range(2):
            for c in range(cols):
                piece = got_ref[low + side * cols + c]
                for k in range(LANES // edge):
                    start = c * pair + side * edge
                    v_ref[k * run : (k + 1) * run, start : start + edge] = edge_of(piece, k)

    def solve_body(level, got_ref, solve_ref, out_ref, v_ref):
        gather_v(level, got_ref, v_ref)
        w = packed(dot_t(v_ref[...], solve_ref[level]), pair)
        out_ref[...] = jnp.broadcast_to(w, out_ref.shape)

    def own_columns(w_all):
        own = w_all[:, :pair]
        for c in range(1, cols):
            own = jnp.where(my_column() == c, w_all[:, c * pair : (c + 1) * pair], own)
        return own

    def gather_w(level, got_ref, w_ref):
        size = span(level)
        share = waves // size
        run = got_ref.shape[1]
        for target in range(size):
            for c in range(cols):
                piece = got_ref[target * cols + c]
                for k in range(LANES // pair):
                    start = target * share + k * run
                    w_ref[start : start + run, c * pair : (c + 1) * pair] = piece[
                        :, k * pair : (k + 1) * pair
                    ]
        return w_ref[...]

    def upper_face(h_ref):
        return jnp.where(my_row() == 1, edge_of(h_ref[...], 2), edge_of(h_ref[...], 0))

    def half_body(level, got_ref, held_ref, moved_ref, *refs):
        if level == 0:
            upper_held_ref, upper_moved_ref, h_ref, out_ref, face_ref, upper_ref, v_ref = refs
            face_ref[...] = packed(upper_face(h_ref), edge)
            kept = in_rows + solve_rows
            join(1, upper_held_ref[:, :kept], upper_moved_ref[:, :kept], upper_ref)
        else:
            out_ref, v_ref = refs
        odd_row = bit(my_row(), 0) == 1
        run = got_ref.shape[1]
        for c in range(cols):
            for part in range(1 + level):
                piece = got_ref[part * cols + c]
                if level == 1:
                    piece = jnp.where(odd_row, piece, got_ref[(2 + part) * cols + c])
                for k in range(LANES // edge):
                    start = (part * LANES // edge + k) * run
                    v_ref[start : start + run, c * edge : (c + 1) * edge] = edge_of(piece, k)
        solve = []
        for c in range(cols):
            start = in_rows * level
            block = held_of(c, held_ref, moved_ref)[start : start + edge]
            solve += [block[:, : iface // 2], block[:, iface // 2 :]]
        out_ref[...] = dot_t(v_ref[...], jnp.concatenate(solve, axis=0))

    def whole_body(h_ref, mine_ref, other_ref, yo_ref, face_ref, side_ref, h_out, w_out, next_ref):
        w_all = mine_ref[...] + other_ref[...]
        w_out[...] = own_columns(w_all)
        out_rows = side_ref[side_rows:]
        out_rows = jnp.concatenate(
            [out_rows[i * edge : (i + 1) * edge] for i in range(iface // LANES)], axis=1
        )
        out_rows = jnp.where(at_upper(), upper_edge(yo_ref[0]), out_rows)
        spread = dot_t(w_all, jnp.concatenate([yo_ref[0], out_rows], axis=0))
        h_out[...] = h_ref[...] + spread[:, :leaf]
        face = jnp.where(at_upper(), upper_face(h_ref), unpacked(face_ref[...], edge))
        face = face + spread[:, leaf:]
        half = jnp.where(bit(my_row(), 0) == 1, face[waves // 2 :], face[: waves // 2])
        next_ref[...] = jnp.broadcast_to(packed(half, edge), next_ref.shape)

    def spread_body(level, h_ref, got_ref, yo_ref, h_out, w_out, next_ref, w_ref):
        w_all = gather_w(level, got_ref, w_ref)
        w_out[...] = own_columns(w_all)
        h = h_ref[...] + dot_t(w_all, yo_ref[level])
        h_out[...] = h
        store_offer(level + 1, h, next_ref)

    def halves(level):
        return span(level) // 2

    def terms_shape(level):
        return (span(level) * cols, waves // halves(level) * edge // LANES, LANES)

    def store_terms(level, g, yi_ref, out):
        terms = dot_t(g, yi_ref[level])
        half = halves(level)
        share = waves // half
        for side in range(2):
            for c in range(cols):
                start = c * pair + side * edge
                piece = terms[:, start : start + edge]
                for part in range(half):
                    out[(side * half + part) * cols + c] = packed(
                        piece[part * share : (part + 1) * share], edge
                    )

    def turn_body(level, h_ref, got_ref, *refs):
        if whole_solve:
            other_ref, yo_ref, yi_ref, reflect_ref, w_out, g_out, out_ref = refs
            w_all = got_ref[...] + other_ref[...]
        else:
            yo_ref, yi_ref, reflect_ref, w_out, g_out, out_ref, w_ref = refs
            w_all = gather_w(level, got_ref, w_ref)
        w_out[...] = own_columns(w_all)
        h = h_ref[...] + dot_t(w_all, yo_ref[level])
        lane = lax.broadcasted_iota(jnp.int32, (1, leaf), 1)

        def side(number):
            return (lane >= number * edge) & (lane < (number + 1) * edge)

        outer = (
            side(0) & (my_row() == 0)
            | side(1) & (my_column() == cols - 1)
            | side(2) & (my_row() == rows - 1)
            | side(3) & (my_column() == 0)
        )
        g = jnp.where(outer, h * reflect_ref[...], 0.0)
        g_out[...] = g
        store_terms(level, g, yi_ref, out_ref)

    def sum_body(got_ref, out_ref):
        out_ref[...] = jnp.sum(got_ref[...], axis=0)

    def with_row_edge(level, g, w, q):
        size = span(level)
        place = lax.rem(my_row(), size)
        is_low = place == size // 2 - 1
        is_high = place == size // 2
        value = jnp.where(place < size // 2, w[:, :edge], w[:, edge:]) + q
        bottom = jnp.where(is_high, value, edge_of(g, 0))
        top = jnp.where(is_low, value, edge_of(g, 2))
        return jnp.concatenate([bottom, edge_of(g, 1), top, edge_of(g, 3)], axis=1)

    def row_down_body(level, g_ref, w_ref, sum_ref, yi_ref, g_out, out_ref):
        g = with_row_edge(level, g_ref[...], w_ref[...], unpacked_parts(level, sum_ref))
        g_out[...] = g
        store_terms(level - 1, g, yi_ref, out_ref)

    def unpacked_parts(level, sum_ref):
        run = waves // halves(level) * edge // LANES
        return jnp.concatenate(
            [unpacked(sum_ref[i * run : (i + 1) * run], edge) for i in range(halves(level))], axis=0
        )

    def collect(total, level):
        for axis_no in range(level):
            axis = row_axes[y_levels - 1 - axis_no]
            other = lax.ppermute(total, axis, [(0, 1), (1, 0)])
            first = lax.axis_index(axis) == 0
            total = jnp.concatenate(
                [jnp.where(first, total, other), jnp.where(first, other, total)], axis=0
            )
        return total

    x_lanes = -(-(x_levels + 1) * edge // LANES) * LANES

    def sides_of(terms):
        low, high = (
            jnp.concatenate([edge_of(terms, 2 * c + side) for c in range(cols)], axis=1)
            for side in range(2)
        )
        odd_row = bit(my_row(), 0) == 1
        return jnp.where(odd_row, high, low), jnp.where(odd_row, low, high)

    def split_body(g_ref, w_ref, sum_ref, yi_ref, g_out, own_out, other_out):
        g = with_row_edge(1, g_ref[...], w_ref[...], unpacked_parts(1, sum_ref))
        g_out[...] = g
        own_out[...], other_out[...] = sides_of(dot_t(g, yi_ref[0]))

    def upper_body(got_ref, g_ref, w_ref, yi_ref, side_ref, other_ref, own_out, other_out, half_out):
        q = unpacked(jnp.sum(got_ref[...], axis=0), edge)
        w = w_ref[...]
        w = jnp.where(my_row() < 2, w[:, :edge], w[:, edge:])
        odd_row = bit(my_row(), 0) == 1
        half = waves // 2
        value = jnp.where(odd_row, w[half:], w[:half]) + q
        half_out[...] = value
        columns = jnp.where(at_upper(), side_ref[:side_rows], other_ref[:side_rows])
        columns = unpacked(columns, edge)
        added = dot_t(value, columns)
        terms = dot_t(g_ref[...], yi_ref[0])
        terms = jnp.concatenate(
            [
                terms[:half] + jnp.where(odd_row, 0.0, added),
                terms[half:] + jnp.where(odd_row, added, 0.0),
            ],
            axis=0,
        )
        own_out[...], other_out[:waves] = sides_of(terms)
        other_out[waves:] = jnp.zeros((8, iface // 2), f32)
        other_out[waves:, : half // 8 * edge] = folded(value)

    node_starts = []
    for k in range(x_levels):
        node_starts.append(sum(cols >> (i + 1) for i in range(k)) * pair)
    node_lanes = (cols - 1) * pair

    inner_lanes = x_levels * edge

    def prepare_body(g_ref, w_ref, xi_ref, held_ref, moved_ref, lo_ref, *refs):
        keep_ref, ends_ref = refs[:x_levels], refs[x_levels : 2 * x_levels - 1]
        matrix_out, known_out, chain_out, keep_out = refs[2 * x_levels - 1 :]
        unit = lax.broadcasted_iota(jnp.int32, (edge, inner_lanes), 0)
        unit = lax.broadcasted_iota(jnp.int32, (edge, inner_lanes), 1) - unit
        gl = jnp.zeros((edge, inner_lanes), f32)
        gr = gl
        for level in reversed(range(x_levels)):
            is_right = bit(my_column(), level) == 1
            keep = keep_ref[level][...]
            keep_out[:, level * edge : (level + 1) * edge] = jnp.where(
                is_right, keep[:, edge:], keep[:, :edge]
            )
            value = jnp.where(unit == level * edge, 1.0, 0.0)
            if level < x_levels - 1:
                end = ends_ref[level][...]
                end = jnp.where(is_right, end[edge:], end[:edge])
                value = value + dot(end, jnp.concatenate([gl, gr], axis=0))
            gl = jnp.where(is_right, value, gl)
            gr = jnp.where(is_right, gr, value)
        none = jnp.zeros((edge, inner_lanes), f32)
        out_map = lo_ref[...]
        added = dot(out_map, jnp.concatenate([none, gr, none, gl], axis=0))
        none = jnp.zeros((pair, leaf), f32)
        chain_out[...] = jnp.concatenate(
            [
                jnp.concatenate([out_map, added], axis=1),
                jnp.concatenate([none, jnp.concatenate([gr, gl], axis=0)], axis=1),
            ],
            axis=0,
        )
        g = with_row_edge(0, g_ref[...], w_ref[...], 0.0)
        row = []
        for c in range(cols):
            held = held_of(c, held_ref, moved_ref)[:in_rows]
            row.append(
                jnp.concatenate(
                    [held[:, i * in_lanes : (i + 1) * in_lanes] for i in range(runs)], axis=0
                )
            )
        matrix_out[...] = jnp.zeros_like(matrix_out)
        for k in range(x_levels):
            known = dot_t(g, xi_ref[k])
            for node in range(cols >> (k + 1)):
                start = node_starts[k] + node * pair
                inside = my_column() >> (k + 1) == node
                known_out[:, start : start + pair] = jnp.where(inside, known, 0.0)
                for c in range(node << (k + 1), (node + 1) << (k + 1)):
                    matrix_out[start : start + pair, c * edge : (c + 1) * edge] = edge_of(row[c], k)

    def x_terms_body(own_ref, got_ref, matrix_ref, known_ref, *refs):
        out_ref = refs[-1]
        q = own_ref[...] + got_ref[:waves]
        terms = dot_t(q, matrix_ref[...]) + known_ref[...]
        if whole_solve:
            g_ref, half_ref, xi_ref, g_out, _ = refs
            odd_row = bit(my_row(), 0) == 1
            mine, other = half_ref[...], unfolded(got_ref[waves:], waves // 2)
            value = jnp.concatenate(
                [jnp.where(odd_row, other, mine), jnp.where(odd_row, mine, other)], axis=0
            )
            none = jnp.zeros_like(value)
            upper = jnp.concatenate(
                [
                    jnp.where(my_row() == 2, value, 0.0),
                    none,
                    jnp.where(my_row() == 1, value, 0.0),
                    none,
                ],
                axis=1,
            )
            g_out[...] = g_ref[...] + upper
            added = dot_t(upper, xi_ref[...].reshape(x_levels * pair, leaf))
        for c in range(cols):
            picked = []
            for k in range(x_levels):
                start = node_starts[k] + (c >> (k + 1)) * pair + bit(c, k) * edge
                piece = terms[:, start : start + edge]
                if whole_solve:
                    inside = my_column() >> (k + 1) == c >> (k + 1)
                    piece = piece + jnp.where(inside, edge_of(added, 2 * k + bit(c, k)), 0.0)
                picked.append(piece)
            out_ref[c] = pad_lanes(jnp.concatenate(picked + [edge_of(q, c)], axis=1), x_lanes)

    def finish_body(g_ref, w_ref, h0_ref, got_ref, chain_ref, keep_ref, g_out, t_out, *faces):
        q = jnp.sum(got_ref[...], axis=0)
        g = with_row_edge(0, g_ref[...], w_ref[...], edge_of(q, x_levels))
        terms = q[:, :inner_lanes] + keep_ref[...]
        result = dot_t(jnp.concatenate([g, terms], axis=1), chain_ref[...])
        gr, gl = edge_of(result, 4), edge_of(result, 5)
        g = jnp.concatenate(
            [edge_of(g, 0), edge_of(g, 1) + gr, edge_of(g, 2), edge_of(g, 3) + gl], axis=1
        )
        g_out[...] = g
        t = g - (result[:, :leaf] + h0_ref[...])
        t_out[...] = t
        odd_col = bit(my_column(), 0) == 1
        odd_row = bit(my_row(), 0) == 1
        bottom, right, top, left = (packed(edge_of(t, i), edge) for i in range(4))
        faces[0][...] = jnp.where(odd_col, left, right)
        faces[1][...] = jnp.where(odd_col, right, left)
        faces[2][...] = jnp.where(odd_row, bottom, top)
        faces[3][...] = jnp.where(odd_row, top, bottom)

    def trace_body(t_ref, a_ref, b_ref, c_ref, d_ref, out_ref):
        t = t_ref[...]
        odd_col = bit(my_column(), 0) == 1
        odd_row = bit(my_row(), 0) == 1
        near_x, far_x, near_y, far_y = (
            unpacked(ref[...], edge) for ref in (a_ref, b_ref, c_ref, d_ref)
        )
        east = jnp.where(odd_col, far_x, near_x)
        west = jnp.where(odd_col, near_x, far_x)
        north = jnp.where(odd_row, far_y, near_y)
        south = jnp.where(odd_row, near_y, far_y)

        def mean(shared, own, other):
            return jnp.where(shared, 0.5 * (own + other), own)

        trace = jnp.concatenate(
            [
                mean(my_row() > 0, edge_of(t, 0), south),
                mean(my_column() < cols - 1, edge_of(t, 1), east),
                mean(my_row() < rows - 1, edge_of(t, 2), north),
                mean(my_column() > 0, edge_of(t, 3), west),
            ],
            axis=1,
        )
        out_ref[...] = trace.reshape(out_ref.shape)

    face = (waves * edge // LANES, LANES)
    if not whole_solve:
        (offer,) = fused(functools.partial(offer_body, 0), [offer_shape(0)], h)
    y_keep = []
    for level in range(y_levels):
        if whole_solve:
            axes = "box" if level == 0 else group(1)
            got = lax.all_to_all(offer, axes, 0, 0, tiled=True)
            if level == 0:
                mine, upper, second = fused(
                    functools.partial(half_body, 0),
                    [(waves, iface), face, held_shape(4, in_rows, solve_rows)],
                    got,
                    held,
                    moved,
                    upper_held,
                    upper_moved,
                    h,
                    scratch=[(waves, cols * edge)],
                )
                upper = lax.ppermute(upper, core, swapped)
                second_moved = passed_on(second, steps[2])
            else:
                (mine,) = fused(
                    functools.partial(half_body, 1),
                    [(waves, iface)],
                    got,
                    second,
                    second_moved,
                    scratch=[(waves, cols * edge)],
                )
            other = lax.ppermute(mine, core, swapped)
            if level == 0:
                h, w, offer = fused(
                    whole_body,
                    [(waves, leaf), (waves, pair), offer_shape(1)],
                    h,
                    mine,
                    other,
                    yo_all,
                    upper,
                    *other_side,
                )
            else:
                w, g, terms = fused(
                    functools.partial(turn_body, level),
                    [(waves, pair), (waves, leaf), terms_shape(level)],
                    h,
                    mine,
                    other,
                    yo_all,
                    yi_all,
                    mirror,
                )
            y_keep.append(w)
            continue
        share = waves // span(level)
        (w_offer,) = fused(
            functools.partial(solve_body, level),
            [(span(level) * cols, share * pair // LANES, LANES)],
            swap(offer, level),
            *ys_all,
            scratch=[(share, iface)],
        )
        got = swap(w_offer, level)
        if level < y_levels - 1:
            h, w, offer = fused(
                functools.partial(spread_body, level),
                [(waves, leaf), (waves, pair), offer_shape(level + 1)],
                h,
                got,
                yo_all,
                scratch=[(waves, iface)],
            )
        else:
            w, g, terms = fused(
                functools.partial(turn_body, level),
                [(waves, pair), (waves, leaf), terms_shape(level)],
                h,
                got,
                yo_all,
                yi_all,
                mirror,
                scratch=[(waves, iface)],
            )
        y_keep.append(w)
    for level in reversed(range(1, 1 if whole_solve else y_levels)):
        (total,) = fused(sum_body, [terms_shape(level)[1:]], swap(terms, level))
        total = collect(total, level)
        if level > 1:
            g, terms = fused(
                functools.partial(row_down_body, level),
                [(waves, leaf), terms_shape(level - 1)],
                g,
                y_keep[level],
                total,
                yi_all,
            )
    share = (waves, iface // 2)
    if whole_solve:
        own, other, half = fused(
            upper_body,
            [share, (waves + 8, iface // 2), (waves // 2, edge)],
            swap(terms, 1),
            g,
            y_keep[1],
            yi_all,
            *side,
            *other_side,
        )
    else:
        g, own, other = fused(
            split_body, [(waves, leaf), share, share], g, y_keep[1], total, yi_all
        )
    got = lax.ppermute(other, core, swapped)
    matrix, known, chain, keep = fused(
        prepare_body,
        [
            (node_lanes, cols * edge),
            (waves, node_lanes),
            (leaf + pair, leaf + inner_lanes),
            (waves, inner_lanes),
        ],
        g,
        y_keep[0],
        xi_all,
        *((second, second_moved) if whole_solve else (held, moved)),
        out_map,
        *x_keep,
        *ends,
    )
    upper = []
    if whole_solve:
        upper = [g, half, xi_all]
    *g_now, terms = fused(
        x_terms_body,
        [(waves, leaf)] * whole_solve + [(cols, waves, x_lanes)],
        own,
        got,
        matrix,
        known,
        *upper,
    )
    g = g_now[0] if g_now else g
    got = lax.all_to_all(terms, "box", 0, 0, tiled=True)
    g, t, *faces = fused(
        finish_body,
        [(waves, leaf), (waves, leaf)] + [face] * 4,
        g,
        y_keep[0],
        h0,
        got,
        chain,
        keep,
    )

    def near(count):
        return [(i, i ^ 1) for i in range(count)]

    def far(count):
        one_way = [(i, i + 1) for i in range(1, count - 1, 2)]
        return one_way + [(j, i) for i, j in one_way]

    seen = [
        lax.ppermute(faces[0], "box", near(cols)),
        lax.ppermute(faces[1], "box", far(cols)),
        lax.ppermute(faces[2], row_axes, near(rows)),
        lax.ppermute(faces[3], row_axes, far(rows)),
    ]
    def field_body(g_ref, map_ref, from_load_ref, out_ref):
        field = from_load_ref[...] + dot_t(g_ref[...], map_ref[...])
        out_ref[...] = field.reshape(out_ref.shape)

    (field_vals,) = fused(
        field_body, [(waves, 1, 1, inner)], g, field_edges, from_load
    )
    (edge_trace,) = fused(trace_body, [(waves, 1, 1, leaf)], t, *seen)
    return field_vals, edge_trace


def solution(mesh):
    rows, cols = mesh.devices.shape
    bits = rows.bit_length() - 1
    row_axes = tuple(f"row{i}" for i in reversed(range(bits)))
    split = Mesh(mesh.devices.reshape((2,) * bits + (cols,)), row_axes + ("box",))
    late = P(None, row_axes, "box")
    early = P(row_axes, "box")
    return jax.shard_map(
        functools.partial(local, row_axes),
        mesh=split,
        in_specs=(late, early, early, early) + (late,) * 6 + (early,),
        out_specs=(late, late),
        check_vma=False,
    )
```

```python
import functools
import math

import jax
import jax.numpy as jnp
from jax import lax
from jax.experimental import pallas as pl
from jax.experimental.pallas import tpu as pltpu
from jax.sharding import Mesh, PartitionSpec as P

f32 = jnp.float32
LANES = 128
PLACING_VMEM = 60 << 20


def dot(a, b, over=0):
    dims = (((1,), (over,)), ((), ()))

    def parts(x):
        high = x.astype(jnp.bfloat16)
        return high, (x - high.astype(f32)).astype(jnp.bfloat16)

    def product(x, y):
        return lax.dot_general(x, y, dims, preferred_element_type=f32)

    a_high, a_low = parts(a)
    b_high, b_low = parts(b)
    both = product(jnp.concatenate([a_high, a_low], axis=0), b_high)
    return both[: a.shape[0]] + (product(a_high, b_low) + both[a.shape[0] :])


def dot_t(a, b):
    return dot(a, b, 1)


def fused(body, outs, *args, scratch=(), aliases=None):
    vmem = pl.BlockSpec(memory_space=pltpu.VMEM)
    return pl.pallas_call(
        body,
        out_shape=[pltpu.VMEM(s, f32) for s in outs],
        in_specs=[vmem] * len(args),
        out_specs=[vmem] * len(outs),
        scratch_shapes=[pltpu.VMEM(s, f32) for s in scratch],
        input_output_aliases=aliases or {},
        compiler_params=pltpu.CompilerParams(vmem_limit_bytes=12 << 20),
    )(*args)


def packed(x, width):
    runs = LANES // width
    rows = x.shape[0] // runs
    return jnp.concatenate([x[i * rows : (i + 1) * rows] for i in range(runs)], axis=1)


def unpacked(x, width):
    return jnp.concatenate(
        [x[:, i * width : (i + 1) * width] for i in range(x.shape[1] // width)], axis=0
    )


def pad_lanes(x, lanes):
    if x.shape[1] == lanes:
        return x
    return jnp.concatenate([x, jnp.zeros((x.shape[0], lanes - x.shape[1]), f32)], axis=1)


def local(
    row_axes,
    load,
    leaf_load_map,
    leaf_out_map,
    leaf_field_map,
    x_solve,
    x_out,
    x_in,
    y_solve,
    y_out,
    y_in,
    reflect,
):
    edge = leaf_out_map.shape[-1] // 4
    cols = lax.axis_size("box")
    rows = 1
    for axis in row_axes:
        rows *= lax.axis_size(axis)
    x_levels = x_solve.shape[0]
    y_levels = y_solve.shape[0]
    waves = load.shape[0]
    leaf = 4 * edge
    pair = 2 * edge
    iface = cols * pair
    load_here = load[:, 0, 0, :]
    inner = load_here.shape[1]

    def my_column():
        return lax.axis_index("box")

    def my_row():
        return lax.axis_index(row_axes)

    def bit(value, level):
        return (value >> level) & 1

    def edge_of(x, number):
        return x[:, number * edge : (number + 1) * edge]

    def exchange_shape(level):
        kept = x_levels - 1 - level
        lanes = (2 + 2 * kept) * edge
        return (pair, -(-lanes // LANES) * LANES)

    def pieces_of(x, first, count):
        return [edge_of(x, first + i) for i in range(count)]

    whole_solve = (x_levels, y_levels) == (3, 2) and iface * iface <= 1 << 18
    in_lanes = -(-x_levels * edge // LANES) * LANES
    width = iface if whole_solve else 4 * in_lanes
    runs = width // in_lanes
    in_rows = pair // runs
    solve_rows = edge if whole_solve else 0

    def held_shape(count, *parts):
        return (count, sum(parts), width)

    def passed_on(held, bit_no):
        return lax.ppermute(held, "box", [(i, i ^ (1 << bit_no)) for i in range(cols)])

    steps = [x_levels - 1] + list(range(x_levels - 1))
    joined_at = [0] + list(range(2, x_levels))

    def held_of(c, held_ref, moved_ref):
        place = sum(bit(c, b) << k for k, b in enumerate(steps[:-1]))
        same = bit(my_column(), steps[-1]) == bit(c, steps[-1])
        return jnp.where(same, held_ref[place], moved_ref[place])

    def join(step, held, moved, both_ref):
        high = bit(my_column(), steps[step]) == 1
        both_ref[: 1 << step] = jnp.where(high, moved, held)
        both_ref[1 << step :] = jnp.where(high, held, moved)

    def placing(body, shapes, *args, scratch=(), live=0):
        return pl.pallas_call(
            body,
            out_shape=[pltpu.VMEM(s, f32) for s in shapes],
            in_specs=[pl.BlockSpec(memory_space=pl.ANY)] * len(args),
            out_specs=[pl.BlockSpec(memory_space=pltpu.VMEM)] * len(shapes),
            scratch_shapes=[pltpu.VMEM(s, f32) for s in scratch]
            + [pltpu.SemaphoreType.DMA((len(args) + 1,))],
            compiler_params=pltpu.CompilerParams(
                vmem_limit_bytes=PLACING_VMEM - live - sum(4 * math.prod(s) for s in shapes)
            ),
        )(*args)

    def hold_body(solve_any, xi_any, *refs):
        *held_refs, solve, xi, sems = refs
        copies = [
            pltpu.make_async_copy(solve_any, solve, sems.at[0]),
            pltpu.make_async_copy(xi_any, xi, sems.at[1]),
        ]
        for copy in copies:
            copy.start()
        for copy in copies:
            copy.wait()
        odd_row = bit(my_row(), 0) == 1
        row_in = pad_lanes(
            jnp.concatenate(
                [
                    jnp.where(odd_row, edge_of(xi[k], 0), edge_of(xi[k], 2))
                    for k in range(x_levels)
                ],
                axis=1,
            ),
            in_lanes,
        )
        held_refs[-1][0, :in_rows] = jnp.concatenate(
            [row_in[i * in_rows : (i + 1) * in_rows] for i in range(runs)], axis=1
        )
        if whole_solve:
            for level, held_ref in enumerate(held_refs[:2]):
                low, high = (
                    jnp.concatenate(
                        [edge_of(solve[level], 2 * c + side) for c in range(cols)], axis=1
                    )
                    for side in range(2)
                )
                mine = jnp.where(odd_row == (level == 0), high, low)
                start = in_rows * level
                held_ref[0, start : start + edge] = jnp.concatenate(
                    [mine[:edge], mine[edge:]], axis=1
                )

    ys_here, xi_here = y_solve[:, 0, 0], x_in[:, 0, 0]
    held, *upper_held = placing(
        hold_body,
        [held_shape(1, solve_rows)] * whole_solve + [held_shape(1, in_rows, solve_rows)],
        ys_here,
        xi_here,
        scratch=[ys_here.shape, xi_here.shape],
    )

    columns_here = [x[:, 0, 0] for x in (jnp.swapaxes(x_out, 3, 4), x_in, x_solve)]
    rows_here = [x[:, 0, 0] for x in (y_out, y_in)] + [leaf_out_map[0, 0], reflect[0]]
    if not whole_solve:
        rows_here.append(ys_here)

    def start_body(load_any, map_any, xo_any, xi_any, xs_any, h_ref, out_ref, load_out, *refs):
        xo, xi, xs, load_v, map_v, sems = refs
        pairs = zip((load_any, map_any, xo_any, xi_any, xs_any), (load_v, map_v, xo, xi, xs))
        copies = [pltpu.make_async_copy(a, b, sems.at[i]) for i, (a, b) in enumerate(pairs)]
        for copy in copies:
            copy.start()
        copies[0].wait()
        copies[1].wait()
        loaded = load_v[...].reshape(waves, inner)
        load_out[...] = loaded
        h = dot_t(loaded, map_v[...])
        h_ref[...] = h
        copies[2].wait()
        copies[3].wait()
        is_right = bit(my_column(), 0) == 1
        travelling = [
            jnp.where(is_right, edge_of(x[k], 1), edge_of(x[k], 3))
            for x in (xi, xo)
            for k in range(x_levels - 1)
        ]
        out_ref[...] = pad_lanes(
            jnp.concatenate([edge_of(h, 3), edge_of(h, 1)] + travelling, axis=1), out_ref.shape[1]
        )
        copies[4].wait()

    h0, to_send, loaded, xo_all, xi_all, xs_all = placing(
        start_body,
        [(waves, leaf), exchange_shape(0), (waves, inner)] + [x.shape for x in columns_here],
        load,
        leaf_load_map[0, 0],
        *columns_here,
        scratch=[load.shape, (leaf, inner)],
    )

    def place_body(field_any, *refs):
        *refs, sems = refs
        count = len(rows_here)
        sources = [field_any.at[:, pl.ds(0, leaf)], field_any.at[:, pl.ds(leaf, inner)]]
        pairs = zip(sources + list(refs[:count]), refs[count:])
        copies = [pltpu.make_async_copy(a, b, sems.at[i]) for i, (a, b) in enumerate(pairs)]
        for copy in copies:
            copy.start()
        for copy in copies:
            copy.wait()

    field_edges, field_inner, yo_all, yi_all, out_map, mirror, *ys_all = placing(
        place_body,
        [(inner, leaf), (inner, inner)] + [x.shape for x in rows_here],
        leaf_field_map[0, 0],
        *rows_here,
        live=2 << 20,
    )

    side_rows = iface * edge // LANES

    def at_upper():
        return (my_row() == 1) | (my_row() == 2)

    def upper_edge(x):
        return jnp.where(my_row() == 1, x[2 * edge : 3 * edge], x[:edge])

    def aside_body(load_ref, map_ref, yi_ref, yo_ref, out_ref, *side_ref):
        out_ref[...] = dot_t(load_ref[...], map_ref[...])
        for ref in side_ref:
            ref[:side_rows] = packed(
                jnp.where(my_row() == 1, edge_of(yi_ref[0], 2), edge_of(yi_ref[0], 0)), edge
            )
            out_rows = upper_edge(yo_ref[0])
            ref[side_rows:] = jnp.concatenate(
                [out_rows[:, i * LANES : (i + 1) * LANES] for i in range(iface // LANES)], axis=0
            )

    from_load, *side = fused(
        aside_body,
        [(waves, inner)] + [(2 * side_rows, LANES)] * whole_solve,
        loaded,
        field_inner,
        yi_all,
        yo_all,
    )

    core = row_axes[-1]
    swapped = [(0, 1), (1, 0)]

    def group(level):
        return tuple(row_axes[y_levels - 1 - level :]) + ("box",)

    def span(level):
        return 2 << level

    def swap(x, level):
        return lax.all_to_all(x, group(level), 0, 0, tiled=True)

    def offer_shape(level):
        if whole_solve:
            return (rows**level * cols, (waves >> level) * edge // LANES, LANES)
        return (span(level) * cols, waves // span(level) * edge // LANES, LANES)

    def store_offer(level, h, out):
        size = span(level)
        share = waves // size
        facing = jnp.where(
            lax.rem(my_row(), size) == size // 2 - 1, edge_of(h, 2), edge_of(h, 0)
        )
        if whole_solve:
            out[...] = jnp.broadcast_to(packed(facing, edge), out.shape)
            return
        for target in range(size):
            piece = packed(facing[target * share : (target + 1) * share], edge)
            out[target * cols : (target + 1) * cols] = jnp.broadcast_to(piece, (cols,) + piece.shape)

    def x_body(level, tasks, h_ref, own_ref, got_ref, solve_ref, xo_ref, *refs):
        kept = x_levels - 1 - level
        count = sum(len(args) for _, args, _ in tasks)
        ins, (h_out, w_out, *rest) = refs[:count], refs[count:]
        rest, outs = rest[: 2 if kept else 0], rest[2 if kept else 0 :]
        offer_ref = outs[-1] if outs else None
        for task, args, shapes in tasks:
            task(*ins[: len(args)], *outs[: len(shapes)])
            ins, outs = ins[len(args) :], outs[len(shapes) :]
        is_right = bit(my_column(), level) == 1
        own, got = own_ref[...], got_ref[...]
        left_child = jnp.where(is_right, got, own)
        right_child = jnp.where(is_right, own, got)
        v = jnp.concatenate([edge_of(left_child, 1), edge_of(right_child, 0)], axis=1)
        w = dot_t(v, solve_ref[level])
        w_out[...] = w
        if kept:
            next_ref, ends_ref = rest
            outer = [edge_of(x, 2 + kept) for x in (left_child, right_child)]
            spread = dot(w, jnp.concatenate([xo_ref[level]] + outer, axis=1))
            h_out[...] = h_ref[...] + spread[:, :leaf]
            left = edge_of(left_child, 0) + edge_of(spread, 4)
            right = edge_of(right_child, 1) + edge_of(spread, 5)
            ends_ref[...] = jnp.concatenate(
                [edge_of(left_child, 2), edge_of(right_child, 2)], axis=1
            )
            mine = jnp.where(bit(my_column(), level + 1) == 1, right_child, left_child)
            travelling = pieces_of(mine, 3, kept - 1) + pieces_of(mine, 3 + kept, kept - 1)
            next_ref[...] = pad_lanes(
                jnp.concatenate([left, right] + travelling, axis=1), next_ref.shape[1]
            )
        else:
            h = h_ref[...] + dot(w, xo_ref[level])
            h_out[...] = h
            if whole_solve:
                store_offer(0, h, offer_ref)

    def nothing(*refs):
        pass

    def join_upper(held_ref, moved_ref, both_ref):
        kept = in_rows + solve_rows
        join(0, held_ref[...], moved_ref[...], both_ref.at[:, :kept])
        both_ref[:, kept:] = jnp.zeros((2, in_rows, width), f32)

    def join_plain(step, held_ref, moved_ref, both_ref):
        join(step, held_ref[...], moved_ref[...], both_ref)

    h = h0
    x_keep, ends = [], []
    moved = passed_on(held, steps[0])
    upper_moved = [passed_on(x, steps[0]) for x in upper_held]
    for level in range(x_levels):
        got = lax.ppermute(to_send, "box", [(i, i ^ (1 << level)) for i in range(cols)])
        outs = [(waves, leaf), (waves, pair)]
        if level < x_levels - 1:
            outs += [exchange_shape(level + 1), (pair, pair)]
        args = [h, to_send, got, xs_all, xo_all]
        tasks = []
        if level == 0:
            tasks.append((nothing, [from_load], []))
        if whole_solve and level == 0:
            shapes = [held_shape(2, solve_rows)]
            tasks.append((functools.partial(join_plain, 0), [held, moved], shapes))
        elif whole_solve and level == 1:
            tasks.append((nothing, side, [x.shape for x in side]))
            shapes = [held_shape(2, in_rows, solve_rows, in_rows)]
            tasks.append((join_upper, upper_held + upper_moved, shapes))
        elif whole_solve:
            tasks.append((nothing, other_side, []))
            shapes = [held_shape(4, solve_rows)]
            tasks.append((functools.partial(join_plain, 1), [held, moved], shapes))
            tasks.append((nothing, [], [offer_shape(0)]))
        elif level in joined_at:
            step = joined_at.index(level)
            shape = held_shape(2 << step, in_rows)
            tasks.append((functools.partial(join_plain, step), [held, moved], [shape]))
        aliases = {len(args): len(outs)} if level == 1 and whole_solve else None
        h, w, *rest = fused(
            functools.partial(x_body, level, tasks),
            outs + [shape for task in tasks for shape in task[2]],
            *args,
            *(x for task in tasks for x in task[1]),
            aliases=aliases,
        )
        x_keep.append(w)
        if level < x_levels - 1:
            to_send, end, *rest = rest
            ends.append(end)
        if whole_solve and level == 0:
            (held,) = rest
            moved = passed_on(held, steps[1])
        elif whole_solve and level == 1:
            side, upper_held = rest[:1], rest[1]
            upper_moved = passed_on(upper_held, steps[1])
            other_side = [lax.ppermute(x, core, swapped) for x in side]
        elif whole_solve:
            held, offer = rest
            moved = passed_on(held, steps[2])
        elif level in joined_at:
            (held,) = rest
            moved = passed_on(held, steps[step + 1])

    def offer_body(level, h_ref, out_ref):
        store_offer(level, h_ref[...], out_ref)

    def folded(x):
        return jnp.concatenate([x[i : i + 8] for i in range(0, x.shape[0], 8)], axis=1)

    def unfolded(x, rows):
        return jnp.concatenate([edge_of(x, i) for i in range(rows // 8)], axis=0)

    def gather_v(level, got_ref, v_ref):
        size = span(level)
        low = (size // 2 - 1) * cols
        run = got_ref.shape[1]
        for side in range(2):
            for c in range(cols):
                piece = got_ref[low + side * cols + c]
                for k in range(LANES // edge):
                    start = c * pair + side * edge
                    v_ref[k * run : (k + 1) * run, start : start + edge] = edge_of(piece, k)

    def solve_body(level, got_ref, solve_ref, out_ref, v_ref):
        gather_v(level, got_ref, v_ref)
        w = packed(dot_t(v_ref[...], solve_ref[level]), pair)
        out_ref[...] = jnp.broadcast_to(w, out_ref.shape)

    def own_columns(w_all):
        own = w_all[:, :pair]
        for c in range(1, cols):
            own = jnp.where(my_column() == c, w_all[:, c * pair : (c + 1) * pair], own)
        return own

    def gather_w(level, got_ref, w_ref):
        size = span(level)
        share = waves // size
        run = got_ref.shape[1]
        for target in range(size):
            for c in range(cols):
                piece = got_ref[target * cols + c]
                for k in range(LANES // pair):
                    start = target * share + k * run
                    w_ref[start : start + run, c * pair : (c + 1) * pair] = piece[
                        :, k * pair : (k + 1) * pair
                    ]
        return w_ref[...]

    def upper_face(h_ref):
        return jnp.where(my_row() == 1, edge_of(h_ref[...], 2), edge_of(h_ref[...], 0))

    def half_body(level, got_ref, held_ref, moved_ref, *refs):
        if level == 0:
            upper_held_ref, upper_moved_ref, h_ref, out_ref, face_ref, upper_ref, v_ref = refs
            face_ref[...] = packed(upper_face(h_ref), edge)
            kept = in_rows + solve_rows
            join(1, upper_held_ref[:, :kept], upper_moved_ref[:, :kept], upper_ref)
        else:
            out_ref, v_ref = refs
        odd_row = bit(my_row(), 0) == 1
        run = got_ref.shape[1]
        for c in range(cols):
            for part in range(1 + level):
                piece = got_ref[part * cols + c]
                if level == 1:
                    piece = jnp.where(odd_row, piece, got_ref[(2 + part) * cols + c])
                for k in range(LANES // edge):
                    start = (part * LANES // edge + k) * run
                    v_ref[start : start + run, c * edge : (c + 1) * edge] = edge_of(piece, k)
        solve = []
        for c in range(cols):
            start = in_rows * level
            block = held_of(c, held_ref, moved_ref)[start : start + edge]
            solve += [block[:, : iface // 2], block[:, iface // 2 :]]
        out_ref[...] = dot_t(v_ref[...], jnp.concatenate(solve, axis=0))

    def whole_body(h_ref, mine_ref, other_ref, yo_ref, face_ref, side_ref, h_out, w_out, next_ref):
        w_all = mine_ref[...] + other_ref[...]
        w_out[...] = own_columns(w_all)
        out_rows = side_ref[side_rows:]
        out_rows = jnp.concatenate(
            [out_rows[i * edge : (i + 1) * edge] for i in range(iface // LANES)], axis=1
        )
        out_rows = jnp.where(at_upper(), upper_edge(yo_ref[0]), out_rows)
        spread = dot_t(w_all, jnp.concatenate([yo_ref[0], out_rows], axis=0))
        h_out[...] = h_ref[...] + spread[:, :leaf]
        face = jnp.where(at_upper(), upper_face(h_ref), unpacked(face_ref[...], edge))
        face = face + spread[:, leaf:]
        half = jnp.where(bit(my_row(), 0) == 1, face[waves // 2 :], face[: waves // 2])
        next_ref[...] = jnp.broadcast_to(packed(half, edge), next_ref.shape)

    def spread_body(level, h_ref, got_ref, yo_ref, h_out, w_out, next_ref, w_ref):
        w_all = gather_w(level, got_ref, w_ref)
        w_out[...] = own_columns(w_all)
        h = h_ref[...] + dot_t(w_all, yo_ref[level])
        h_out[...] = h
        store_offer(level + 1, h, next_ref)

    def halves(level):
        return span(level) // 2

    def terms_shape(level):
        return (span(level) * cols, waves // halves(level) * edge // LANES, LANES)

    def store_terms(level, g, yi_ref, out):
        terms = dot_t(g, yi_ref[level])
        half = halves(level)
        share = waves // half
        for side in range(2):
            for c in range(cols):
                start = c * pair + side * edge
                piece = terms[:, start : start + edge]
                for part in range(half):
                    out[(side * half + part) * cols + c] = packed(
                        piece[part * share : (part + 1) * share], edge
                    )

    def turn_body(level, h_ref, got_ref, *refs):
        if whole_solve:
            other_ref, yo_ref, yi_ref, reflect_ref, w_out, g_out, out_ref = refs
            w_all = got_ref[...] + other_ref[...]
        else:
            yo_ref, yi_ref, reflect_ref, w_out, g_out, out_ref, w_ref = refs
            w_all = gather_w(level, got_ref, w_ref)
        w_out[...] = own_columns(w_all)
        h = h_ref[...] + dot_t(w_all, yo_ref[level])
        lane = lax.broadcasted_iota(jnp.int32, (1, leaf), 1)

        def side(number):
            return (lane >= number * edge) & (lane < (number + 1) * edge)

        outer = (
            side(0) & (my_row() == 0)
            | side(1) & (my_column() == cols - 1)
            | side(2) & (my_row() == rows - 1)
            | side(3) & (my_column() == 0)
        )
        g = jnp.where(outer, h * reflect_ref[...], 0.0)
        g_out[...] = g
        store_terms(level, g, yi_ref, out_ref)

    def sum_body(got_ref, out_ref):
        out_ref[...] = jnp.sum(got_ref[...], axis=0)

    def with_row_edge(level, g, w, q):
        size = span(level)
        place = lax.rem(my_row(), size)
        is_low = place == size // 2 - 1
        is_high = place == size // 2
        value = jnp.where(place < size // 2, w[:, :edge], w[:, edge:]) + q
        bottom = jnp.where(is_high, value, edge_of(g, 0))
        top = jnp.where(is_low, value, edge_of(g, 2))
        return jnp.concatenate([bottom, edge_of(g, 1), top, edge_of(g, 3)], axis=1)

    def row_down_body(level, g_ref, w_ref, sum_ref, yi_ref, g_out, out_ref):
        g = with_row_edge(level, g_ref[...], w_ref[...], unpacked_parts(level, sum_ref))
        g_out[...] = g
        store_terms(level - 1, g, yi_ref, out_ref)

    def unpacked_parts(level, sum_ref):
        run = waves // halves(level) * edge // LANES
        return jnp.concatenate(
            [unpacked(sum_ref[i * run : (i + 1) * run], edge) for i in range(halves(level))], axis=0
        )

    def collect(total, level):
        for axis_no in range(level):
            axis = row_axes[y_levels - 1 - axis_no]
            other = lax.ppermute(total, axis, [(0, 1), (1, 0)])
            first = lax.axis_index(axis) == 0
            total = jnp.concatenate(
                [jnp.where(first, total, other), jnp.where(first, other, total)], axis=0
            )
        return total

    x_lanes = -(-(x_levels + 1) * edge // LANES) * LANES

    def sides_of(terms):
        low, high = (
            jnp.concatenate([edge_of(terms, 2 * c + side) for c in range(cols)], axis=1)
            for side in range(2)
        )
        odd_row = bit(my_row(), 0) == 1
        return jnp.where(odd_row, high, low), jnp.where(odd_row, low, high)

    def split_body(g_ref, w_ref, sum_ref, yi_ref, g_out, own_out, other_out):
        g = with_row_edge(1, g_ref[...], w_ref[...], unpacked_parts(1, sum_ref))
        g_out[...] = g
        own_out[...], other_out[...] = sides_of(dot_t(g, yi_ref[0]))

    def upper_body(got_ref, g_ref, w_ref, yi_ref, side_ref, other_ref, own_out, other_out, half_out):
        q = unpacked(jnp.sum(got_ref[...], axis=0), edge)
        w = w_ref[...]
        w = jnp.where(my_row() < 2, w[:, :edge], w[:, edge:])
        odd_row = bit(my_row(), 0) == 1
        half = waves // 2
        value = jnp.where(odd_row, w[half:], w[:half]) + q
        half_out[...] = value
        columns = jnp.where(at_upper(), side_ref[:side_rows], other_ref[:side_rows])
        columns = unpacked(columns, edge)
        added = dot_t(value, columns)
        terms = dot_t(g_ref[...], yi_ref[0])
        terms = jnp.concatenate(
            [
                terms[:half] + jnp.where(odd_row, 0.0, added),
                terms[half:] + jnp.where(odd_row, added, 0.0),
            ],
            axis=0,
        )
        own_out[...], other_out[:waves] = sides_of(terms)
        other_out[waves:] = jnp.zeros((8, iface // 2), f32)
        other_out[waves:, : half // 8 * edge] = folded(value)

    node_starts = []
    for k in range(x_levels):
        node_starts.append(sum(cols >> (i + 1) for i in range(k)) * pair)
    node_lanes = (cols - 1) * pair

    inner_lanes = x_levels * edge

    def prepare_body(g_ref, w_ref, xi_ref, held_ref, moved_ref, lo_ref, *refs):
        keep_ref, ends_ref = refs[:x_levels], refs[x_levels : 2 * x_levels - 1]
        matrix_out, known_out, chain_out, keep_out = refs[2 * x_levels - 1 :]
        unit = lax.broadcasted_iota(jnp.int32, (edge, inner_lanes), 0)
        unit = lax.broadcasted_iota(jnp.int32, (edge, inner_lanes), 1) - unit
        gl = jnp.zeros((edge, inner_lanes), f32)
        gr = gl
        for level in reversed(range(x_levels)):
            is_right = bit(my_column(), level) == 1
            keep = keep_ref[level][...]
            keep_out[:, level * edge : (level + 1) * edge] = jnp.where(
                is_right, keep[:, edge:], keep[:, :edge]
            )
            value = jnp.where(unit == level * edge, 1.0, 0.0)
            if level < x_levels - 1:
                end = ends_ref[level][...]
                end = jnp.where(is_right, end[edge:], end[:edge])
                value = value + dot(end, jnp.concatenate([gl, gr], axis=0))
            gl = jnp.where(is_right, value, gl)
            gr = jnp.where(is_right, gr, value)
        none = jnp.zeros((edge, inner_lanes), f32)
        out_map = lo_ref[...]
        added = dot(out_map, jnp.concatenate([none, gr, none, gl], axis=0))
        none = jnp.zeros((pair, leaf), f32)
        chain_out[...] = jnp.concatenate(
            [
                jnp.concatenate([out_map, added], axis=1),
                jnp.concatenate([none, jnp.concatenate([gr, gl], axis=0)], axis=1),
            ],
            axis=0,
        )
        g = with_row_edge(0, g_ref[...], w_ref[...], 0.0)
        row = []
        for c in range(cols):
            held = held_of(c, held_ref, moved_ref)[:in_rows]
            row.append(
                jnp.concatenate(
                    [held[:, i * in_lanes : (i + 1) * in_lanes] for i in range(runs)], axis=0
                )
            )
        matrix_out[...] = jnp.zeros_like(matrix_out)
        for k in range(x_levels):
            known = dot_t(g, xi_ref[k])
            for node in range(cols >> (k + 1)):
                start = node_starts[k] + node * pair
                inside = my_column() >> (k + 1) == node
                known_out[:, start : start + pair] = jnp.where(inside, known, 0.0)
                for c in range(node << (k + 1), (node + 1) << (k + 1)):
                    matrix_out[start : start + pair, c * edge : (c + 1) * edge] = edge_of(row[c], k)

    def x_terms_body(own_ref, got_ref, matrix_ref, known_ref, *refs):
        out_ref = refs[-1]
        q = own_ref[...] + got_ref[:waves]
        if whole_solve:
            g_ref, half_ref, xi_ref, g_out, _ = refs
            odd_row = bit(my_row(), 0) == 1
            mine, other = half_ref[...], unfolded(got_ref[waves:], waves // 2)
            value = jnp.concatenate(
                [jnp.where(odd_row, other, mine), jnp.where(odd_row, mine, other)], axis=0
            )
            none = jnp.zeros_like(value)
            upper = jnp.concatenate(
                [
                    jnp.where(my_row() == 2, value, 0.0),
                    none,
                    jnp.where(my_row() == 1, value, 0.0),
                    none,
                ],
                axis=1,
            )
            g_out[...] = g_ref[...] + upper
            matrix = []
            for k in range(x_levels):
                for node in range(cols >> (k + 1)):
                    inside = my_column() >> (k + 1) == node
                    matrix.append(jnp.where(inside, xi_ref[k], 0.0))
            matrix = jnp.concatenate([matrix_ref[...], jnp.concatenate(matrix, axis=0)], axis=1)
            terms = dot_t(jnp.concatenate([q, upper], axis=1), matrix) + known_ref[...]
        else:
            terms = dot_t(q, matrix_ref[...]) + known_ref[...]
        for c in range(cols):
            picked = []
            for k in range(x_levels):
                start = node_starts[k] + (c >> (k + 1)) * pair + bit(c, k) * edge
                picked.append(terms[:, start : start + edge])
            out_ref[c] = pad_lanes(jnp.concatenate(picked + [edge_of(q, c)], axis=1), x_lanes)

    def finish_body(g_ref, w_ref, h0_ref, got_ref, chain_ref, keep_ref, g_out, t_out, *faces):
        q = jnp.sum(got_ref[...], axis=0)
        g = with_row_edge(0, g_ref[...], w_ref[...], edge_of(q, x_levels))
        terms = q[:, :inner_lanes] + keep_ref[...]
        result = dot_t(jnp.concatenate([g, terms], axis=1), chain_ref[...])
        gr, gl = edge_of(result, 4), edge_of(result, 5)
        g = jnp.concatenate(
            [edge_of(g, 0), edge_of(g, 1) + gr, edge_of(g, 2), edge_of(g, 3) + gl], axis=1
        )
        g_out[...] = g
        t = g - (result[:, :leaf] + h0_ref[...])
        t_out[...] = t
        odd_col = bit(my_column(), 0) == 1
        odd_row = bit(my_row(), 0) == 1
        bottom, right, top, left = (packed(edge_of(t, i), edge) for i in range(4))
        faces[0][...] = jnp.where(odd_col, left, right)
        faces[1][...] = jnp.where(odd_col, right, left)
        faces[2][...] = jnp.where(odd_row, bottom, top)
        faces[3][...] = jnp.where(odd_row, top, bottom)

    def trace_body(t_ref, a_ref, b_ref, c_ref, d_ref, out_ref):
        t = t_ref[...]
        odd_col = bit(my_column(), 0) == 1
        odd_row = bit(my_row(), 0) == 1
        near_x, far_x, near_y, far_y = (
            unpacked(ref[...], edge) for ref in (a_ref, b_ref, c_ref, d_ref)
        )
        east = jnp.where(odd_col, far_x, near_x)
        west = jnp.where(odd_col, near_x, far_x)
        north = jnp.where(odd_row, far_y, near_y)
        south = jnp.where(odd_row, near_y, far_y)

        def mean(shared, own, other):
            return jnp.where(shared, 0.5 * (own + other), own)

        trace = jnp.concatenate(
            [
                mean(my_row() > 0, edge_of(t, 0), south),
                mean(my_column() < cols - 1, edge_of(t, 1), east),
                mean(my_row() < rows - 1, edge_of(t, 2), north),
                mean(my_column() > 0, edge_of(t, 3), west),
            ],
            axis=1,
        )
        out_ref[...] = trace.reshape(out_ref.shape)

    face = (waves * edge // LANES, LANES)
    if not whole_solve:
        (offer,) = fused(functools.partial(offer_body, 0), [offer_shape(0)], h)
    y_keep = []
    for level in range(y_levels):
        if whole_solve:
            axes = "box" if level == 0 else group(1)
            got = lax.all_to_all(offer, axes, 0, 0, tiled=True)
            if level == 0:
                mine, upper, second = fused(
                    functools.partial(half_body, 0),
                    [(waves, iface), face, held_shape(4, in_rows, solve_rows)],
                    got,
                    held,
                    moved,
                    upper_held,
                    upper_moved,
                    h,
                    scratch=[(waves, cols * edge)],
                )
                upper = lax.ppermute(upper, core, swapped)
                second_moved = passed_on(second, steps[2])
            else:
                (mine,) = fused(
                    functools.partial(half_body, 1),
                    [(waves, iface)],
                    got,
                    second,
                    second_moved,
                    scratch=[(waves, cols * edge)],
                )
            other = lax.ppermute(mine, core, swapped)
            if level == 0:
                h, w, offer = fused(
                    whole_body,
                    [(waves, leaf), (waves, pair), offer_shape(1)],
                    h,
                    mine,
                    other,
                    yo_all,
                    upper,
                    *other_side,
                )
            else:
                w, g, terms = fused(
                    functools.partial(turn_body, level),
                    [(waves, pair), (waves, leaf), terms_shape(level)],
                    h,
                    mine,
                    other,
                    yo_all,
                    yi_all,
                    mirror,
                )
            y_keep.append(w)
            continue
        share = waves // span(level)
        (w_offer,) = fused(
            functools.partial(solve_body, level),
            [(span(level) * cols, share * pair // LANES, LANES)],
            swap(offer, level),
            *ys_all,
            scratch=[(share, iface)],
        )
        got = swap(w_offer, level)
        if level < y_levels - 1:
            h, w, offer = fused(
                functools.partial(spread_body, level),
                [(waves, leaf), (waves, pair), offer_shape(level + 1)],
                h,
                got,
                yo_all,
                scratch=[(waves, iface)],
            )
        else:
            w, g, terms = fused(
                functools.partial(turn_body, level),
                [(waves, pair), (waves, leaf), terms_shape(level)],
                h,
                got,
                yo_all,
                yi_all,
                mirror,
                scratch=[(waves, iface)],
            )
        y_keep.append(w)
    for level in reversed(range(1, 1 if whole_solve else y_levels)):
        (total,) = fused(sum_body, [terms_shape(level)[1:]], swap(terms, level))
        total = collect(total, level)
        if level > 1:
            g, terms = fused(
                functools.partial(row_down_body, level),
                [(waves, leaf), terms_shape(level - 1)],
                g,
                y_keep[level],
                total,
                yi_all,
            )
    share = (waves, iface // 2)
    if whole_solve:
        own, other, half = fused(
            upper_body,
            [share, (waves + 8, iface // 2), (waves // 2, edge)],
            swap(terms, 1),
            g,
            y_keep[1],
            yi_all,
            *side,
            *other_side,
        )
    else:
        g, own, other = fused(
            split_body, [(waves, leaf), share, share], g, y_keep[1], total, yi_all
        )
    got = lax.ppermute(other, core, swapped)
    matrix, known, chain, keep = fused(
        prepare_body,
        [
            (node_lanes, cols * edge),
            (waves, node_lanes),
            (leaf + pair, leaf + inner_lanes),
            (waves, inner_lanes),
        ],
        g,
        y_keep[0],
        xi_all,
        *((second, second_moved) if whole_solve else (held, moved)),
        out_map,
        *x_keep,
        *ends,
    )
    upper = []
    if whole_solve:
        upper = [g, half, xi_all]
    *g_now, terms = fused(
        x_terms_body,
        [(waves, leaf)] * whole_solve + [(cols, waves, x_lanes)],
        own,
        got,
        matrix,
        known,
        *upper,
    )
    g = g_now[0] if g_now else g
    got = lax.all_to_all(terms, "box", 0, 0, tiled=True)
    g, t, *faces = fused(
        finish_body,
        [(waves, leaf), (waves, leaf)] + [face] * 4,
        g,
        y_keep[0],
        h0,
        got,
        chain,
        keep,
    )

    def near(count):
        return [(i, i ^ 1) for i in range(count)]

    def far(count):
        one_way = [(i, i + 1) for i in range(1, count - 1, 2)]
        return one_way + [(j, i) for i, j in one_way]

    seen = [
        lax.ppermute(faces[0], "box", near(cols)),
        lax.ppermute(faces[1], "box", far(cols)),
        lax.ppermute(faces[2], row_axes, near(rows)),
        lax.ppermute(faces[3], row_axes, far(rows)),
    ]
    def field_body(g_ref, map_ref, from_load_ref, out_ref):
        field = from_load_ref[...] + dot_t(g_ref[...], map_ref[...])
        out_ref[...] = field.reshape(out_ref.shape)

    (field_vals,) = fused(
        field_body, [(waves, 1, 1, inner)], g, field_edges, from_load
    )
    (edge_trace,) = fused(trace_body, [(waves, 1, 1, leaf)], t, *seen)
    return field_vals, edge_trace


def solution(mesh):
    rows, cols = mesh.devices.shape
    bits = rows.bit_length() - 1
    row_axes = tuple(f"row{i}" for i in reversed(range(bits)))
    split = Mesh(mesh.devices.reshape((2,) * bits + (cols,)), row_axes + ("box",))
    late = P(None, row_axes, "box")
    early = P(row_axes, "box")
    return jax.shard_map(
        functools.partial(local, row_axes),
        mesh=split,
        in_specs=(late, early, early, early) + (late,) * 6 + (early,),
        out_specs=(late, late),
        check_vma=False,
    )
```
